256 devices in a mesh: gz: 8 (over z_lo, core), gy: 4 (over y), gx: 8 (over z_hi, x).
Axes of the slice: x: 4, y: 4, z: 8 (z_hi: 2, z_lo: 4; z = z_hi * 4 + z_lo), core: 2. Of those that a mesh axis runs over, the one named last changes fastest.
Arguments:
- embedding: bfloat16 [32, 32, 256, 1024], P(None, 'gz', 'gy', 'gx'), may hold values from -18 to 18
- face_slot: int32 [32, 256, 1024], P('gz', 'gy', 'gx'), may hold values from 0 to 511
- face_edge: int32 [32768], P(('gz', 'gy', 'gx')), may hold values from 0 to 16383, as said below
- conv1_w: bfloat16 [3, 3, 3, 64, 32], replicated, may hold values from -0.21875 to 0.21875
- conv1_b: float32 [64], replicated, may hold values from -3 to 3
- conv2_w: bfloat16 [3, 3, 3, 64, 64], replicated, may hold values from -0.15625 to 0.15625
- conv2_b: float32 [64], replicated, may hold values from -3 to 3
Outputs:
- context: bfloat16 [64, 16, 64, 256], P(None, 'gz', 'gy', 'gx')
- edge_emb: float32 [32, 16384], P(None, ('gz', 'gy', 'gx'))
- edge_ctx: float32 [64, 16384], P(None, ('gz', 'gy', 'gx'))
The draws below stay inside these ranges and needn't reach their ends.
Inputs may be any that keep to these rules, and one draw needn't show every extreme that they name: A voxel whose face_slot is 128 or more lies on no contact face. `face_edge`: edge e belongs to tile e // 64 (tiles in order gz, gy, gx). The faces of a tile name only edges of the tiles in its own gz, gy row, exactly 16 faces for each tile of that row.
All inputs are finite; a program needn't handle non-finite values.
Results may differ from the reference program's by a relative error of at most 0.0046.
Values may be sent and summed in bfloat16 or wider, within the bound.
No kernel may reach another device: no remote copies, remote signals or barrier semaphores. Data moves between devices by JAX's collectives and lax.ppermute only.
A program may use at most 128 MiB of HBM per device.

```python
import jax
import jax.numpy as jnp
from jax import lax

C_EMB = 32
C_CTX = 64
FACES = 128
TZ = 4
TY = 64
TX = 128
EDGE_DEV = 64
NZ = 32
NY = 256
NX = 1024
EDGES = 16384
SLOTS = 512
CAP = 16
N_GZ = 8
N_GY = 4
N_GX = 8
DEVICES = 256


def draw_face_edge(key, part):
    key = jax.random.fold_in(key, 7)
    keys = jax.random.split(key, DEVICES)
    base = jnp.repeat(jnp.arange(N_GX, dtype=jnp.int32), CAP)
    owners = jax.vmap(lambda single: jax.random.permutation(single, base))(keys)
    local = jax.random.randint(jax.random.fold_in(key, 1), (DEVICES, FACES), 0, EDGE_DEV, dtype=jnp.int32)
    device = jnp.arange(DEVICES, dtype=jnp.int32)[:, None]
    edge = (device - device % N_GX + owners) * EDGE_DEV + local
    return edge.reshape(DEVICES * FACES).astype(jnp.int32)


def place_ends(result, stream_key, smallest, largest):
    shape = result.shape
    spot = [jax.random.randint(jax.random.fold_in(stream_key, axis), (), 0, shape[axis]) for axis in range(len(shape))]
    result = result.at[tuple(spot)].set(smallest)
    longest = shape.index(max(shape))
    spot[longest] = (spot[longest] + 1) % shape[longest]
    return result.at[tuple(spot)].set(largest)


def levels(key, extent, shards, least, largest):
    loudness, own = 1.0, jax.random.fold_in(key, 6)
    for axis_at, blocks in shards:
        draws = jnp.exp(jax.random.uniform(jax.random.fold_in(own, axis_at), (blocks,), jnp.float32, least / len(shards), largest / len(shards)))
        loudness = loudness * jnp.repeat(draws, extent[axis_at] // blocks).reshape([-1 if axis == axis_at else 1 for axis in range(len(extent))])
    return loudness


def scatter_about(own_key, dims, spread, most, pieces=(), kind=jnp.bfloat16):
    factor_of = levels(own_key, dims, pieces, -0.22, 0.18) if pieces else 1.0
    values = jax.random.normal(own_key, dims, jnp.float32) * spread * factor_of
    return jnp.minimum(jnp.maximum(values, -most), most).astype(kind)


def setup_inputs(seed: int = 0) -> dict:
    streams_of = jax.random.split(jax.random.key(seed), 8)
    return {
        "embedding": scatter_about(streams_of[0], (C_EMB, NZ, NY, NX), 3.0, 18.0, ((1, 8), (2, 4), (3, 8))),
        "face_slot": place_ends(jax.random.randint(streams_of[1], (NZ, NY, NX), 0, SLOTS), jax.random.fold_in(streams_of[1], 1), 0, SLOTS - 1).astype(jnp.int32),
        "face_edge": draw_face_edge(jax.random.fold_in(streams_of[7], 71), 0),
        "conv1_w": scatter_about(streams_of[3], (3, 3, 3, C_CTX, C_EMB), (27 * C_EMB) ** -0.5, 0.21875),
        "conv1_b": scatter_about(streams_of[4], (C_CTX,), 0.5, 3.0, (), jnp.float32),
        "conv2_w": scatter_about(streams_of[5], (3, 3, 3, C_CTX, C_CTX), (27 * C_CTX) ** -0.5, 0.15625),
        "conv2_b": scatter_about(streams_of[6], (C_CTX,), 0.5, 3.0, (), jnp.float32),
    }


def pool_field(field):
    chans, depth, rows, cols = field.shape
    shaped = field.reshape(chans, depth // 2, 2, rows // 4, 4, cols // 4, 4)
    return jnp.mean(shaped, axis=(2, 4, 6), dtype=jnp.float32).astype(jnp.bfloat16)


def convolve(source, weight, bias):
    chans, depth, rows, cols = source.shape
    padded = jnp.pad(source, ((0, 0), (1, 1), (1, 1), (1, 1))).astype(jnp.float32)
    total = jnp.zeros((weight.shape[3], depth, rows, cols), jnp.float32)
    for dz in range(3):
        for dy in range(3):
            for dx in range(3):
                window = padded[:, dz:dz + depth, dy:dy + rows, dx:dx + cols]
                total = total + jnp.einsum("oc,czyx->ozyx", weight[dz, dy, dx].astype(jnp.float32), window)
    return total + bias[:, None, None, None]


def upsample(coarse):
    return jnp.repeat(jnp.repeat(jnp.repeat(coarse, 2, axis=1), 4, axis=2), 4, axis=3)


def reference(embedding, face_slot, face_edge, conv1_w, conv1_b, conv2_w, conv2_b):
    pooled = pool_field(embedding)
    hidden1 = jax.nn.relu(convolve(pooled, conv1_w, conv1_b)).astype(jnp.bfloat16)
    context = convolve(hidden1, conv2_w, conv2_b).astype(jnp.bfloat16)
    cells = TZ * TY * TX

    def tile_faces(tile):
        iz = tile // (N_GY * N_GX)
        iy = (tile // N_GX) % N_GY
        ix = tile % N_GX
        zero = jnp.int32(0)
        emb_tile = lax.dynamic_slice(embedding, (zero, iz * TZ, iy * TY, ix * TX), (C_EMB, TZ, TY, TX))
        ctx_tile = lax.dynamic_slice(context, (zero, iz * (TZ // 2), iy * (TY // 4), ix * (TX // 4)), (C_CTX, TZ // 2, TY // 4, TX // 4))
        slot_tile = lax.dynamic_slice(face_slot, (iz * TZ, iy * TY, ix * TX), (TZ, TY, TX)).reshape(cells)
        values = jnp.concatenate([emb_tile.reshape(C_EMB, cells).astype(jnp.float32), upsample(ctx_tile).reshape(C_CTX, cells).astype(jnp.float32), jnp.ones((1, cells), jnp.float32)], axis=0)
        labels = jnp.minimum(slot_tile, FACES).astype(jnp.int32)
        return jax.ops.segment_sum(values.T, labels, FACES + 1)[:FACES]

    faces = lax.map(tile_faces, jnp.arange(N_GZ * N_GY * N_GX, dtype=jnp.int32))
    faces = faces.reshape(N_GZ * N_GY * N_GX * FACES, C_EMB + C_CTX + 1)
    edges = jax.ops.segment_sum(faces, face_edge.astype(jnp.int32), EDGES)
    means = edges[:, :C_EMB + C_CTX] / jnp.maximum(edges[:, C_EMB + C_CTX:], 1.0)
    return context, means[:, :C_EMB].T, means[:, C_EMB:].T
```

```python
import jax
import jax.numpy as jnp
from jax import lax
from jax.experimental import pallas as pl
from jax.experimental.pallas import tpu as pltpu
from jax.sharding import PartitionSpec as P

BF = jnp.bfloat16
F32 = jnp.float32
NT = (((1,), (1,)), ((), ()))
NN = (((1,), (0,)), ((), ()))


def dot(a, b, dims=NN):
    return lax.dot_general(a, b, dims, preferred_element_type=F32)


def iota(shape, dim):
    return lax.broadcasted_iota(jnp.int32, shape, dim)


def split3(x):
    hi = x.astype(BF)
    rest = x - hi.astype(F32)
    mid = rest.astype(BF)
    low = (rest - mid.astype(F32)).astype(BF)
    return hi, mid, low


def pool_x_matrix():
    row, col = iota((32, 128), 0), iota((32, 128), 1)
    cell = 4 * (row & 7) + (row >> 3)
    return jnp.where((col >> 2) == cell, 1.0, 0.0).astype(BF)


def pool_kernel(emb_ref, out_ref, sums):
    step = pl.program_id(0)
    row, col = iota((32, 256), 0), iota((32, 256), 1)
    cell = ((col >> 7) << 4) + ((col & 63) >> 2)
    pool_zy = jnp.where(cell == row, 1.0, 0.0).astype(BF)
    per = emb_ref.shape[0]
    for i in range(per):
        sums[step * per + i] = dot(pool_zy, emb_ref[i])

    @pl.when(step == pl.num_programs(0) - 1)
    def _():
        pool_x = pool_x_matrix()
        lane = iota((8, 128), 1)
        for block in range(8):
            rows = jnp.concatenate([sums[:, 4 * block + i, :] for i in range(4)], axis=0)
            cells = sum(dot(pool_x, part, NT) for part in split3(rows)) * (1.0 / 32.0)
            v = [cells[8 * i : 8 * i + 8] for i in range(4)]
            far = lane < 64
            a = [jnp.where(far, v[i], pltpu.roll(v[i + 2], 64, 1)) for i in range(2)]
            b = [jnp.where(far, pltpu.roll(v[i], 64, 1), v[i + 2]) for i in range(2)]
            near = (lane & 32) == 0
            done = []
            for lo, hi in (a, b):
                done.append(jnp.where(near, lo, pltpu.roll(hi, 32, 1)))
                done.append(jnp.where(near, pltpu.roll(lo, 96, 1), hi))
            out_ref[pl.ds(32 * block, 32), :] = jnp.concatenate(done, axis=0).astype(BF)


def pool(emb):
    steps = 4
    return pl.pallas_call(
        pool_kernel,
        grid=(steps,),
        in_specs=[pl.BlockSpec((32 // steps, 256, 128), lambda i: (i, 0, 0))],
        out_specs=pl.BlockSpec((256, 128), lambda i: (0, 0)),
        out_shape=jax.ShapeDtypeStruct((256, 128), BF),
        scratch_shapes=[pltpu.VMEM((32, 32, 128), F32)],
        compiler_params=pltpu.CompilerParams(vmem_limit_bytes=16 << 20),
        cost_estimate=pl.CostEstimate(flops=80_000_000, bytes_accessed=2_200_000, transcendentals=0),
        name="pool",
    )(emb)


def banded(tap, taps):
    zero = jnp.zeros_like(taps(tap, 0))
    w = [taps(tap, k) if 0 <= k < 3 else zero for k in range(-1, 4)]
    return [jnp.concatenate([w[k + 1], w[k]], axis=1) for k in range(4)]


def face_kernel(emb_ref, slot_ref, edge_ref, w1_ref, w2_ref, cnt_ref, face_ref, w1a_ref, w1b_ref, w2a_ref,
                wide, order, cells, total):
    step = pl.program_id(0)
    last = pl.num_programs(0) - 1
    i0, i1 = iota((128, 128), 0), iota((128, 128), 1)

    @pl.when(step == 0)
    def _():
        label = jnp.broadcast_to(edge_ref[...], (128, 128))
        owner = ((label >> 6) & 7).astype(F32)
        local = (label & 63).astype(F32)
        ahead = jnp.where((owner == owner.T) & (i0 < i1), 1.0, 0.0)
        place = owner[0:1, :] * 16.0 + jnp.sum(ahead, axis=0, keepdims=True)
        chosen = place == i0.astype(F32)
        face = jnp.sum(jnp.where(chosen, i1.astype(F32), 0.0), axis=1, keepdims=True)
        edge = jnp.sum(jnp.where(chosen, local, 0.0), axis=1, keepdims=True)
        order[0] = jnp.broadcast_to(face, (128, 128))
        order[1] = jnp.broadcast_to(edge, (128, 128))
        total[...] = jnp.zeros_like(total)

    wide[...] = emb_ref[...].astype(F32)
    faces = order[0].astype(BF)
    pool_x = pool_x_matrix()
    pool_x8 = jnp.concatenate([pool_x] * 8, axis=1)
    sums = jnp.zeros((32, 128), F32)
    count = jnp.zeros((8, 128), F32)
    for yc in range(16):
        voxels, member = [], []
        for q in (64 * zi + 4 * yc + yy for zi in range(2) for yy in range(4)):
            voxels.append(wide[:, q, :].astype(BF))
            row = jnp.broadcast_to(slot_ref[q : q + 1, :].astype(F32), (16, 128)).astype(BF)
            row = jnp.concatenate([row] * 8, axis=0)
            member.append(jnp.where(row == faces, jnp.ones((), BF), jnp.zeros((), BF)))
        left = jnp.concatenate([jnp.concatenate(voxels, axis=1), pool_x8], axis=0)
        out = dot(left, jnp.concatenate(member, axis=1), NT)
        sums = sums + out[:32]
        for x4 in range(4):
            part = out[32 + 8 * x4 : 40 + 8 * x4]
            cells[x4, 8 * yc : 8 * yc + 8, :] = part
            count = count + part
    total[0:32] += sums
    total[32:40] += count
    for x4 in range(4):
        cnt_ref[x4 // 2, 128 * (x4 % 2) : 128 * (x4 % 2) + 128, :] = cells[x4].T.astype(BF)

    @pl.when(step == last)
    def _():
        number = jnp.sum(total[32:40], axis=0, keepdims=True)
        stacked = jnp.concatenate(
            [jnp.zeros((64, 128), F32), total[0:32], jnp.broadcast_to(number, (32, 128))], axis=0
        )
        face_ref[...] = jnp.where(i1 == 97, order[1], stacked.T)
        for tap in range(9):
            bands = banded(tap, lambda t, k: w1_ref[3 * t + k])
            w1a_ref[pl.ds(128 * tap, 128), :] = jnp.concatenate(bands, axis=0)
            w1b_ref[pl.ds(128 * tap, 128), :] = jnp.concatenate(bands[2:] + bands[:2], axis=0)
            bands = banded(tap, lambda t, k: w2_ref[3 * t + k].astype(F32).T.astype(BF))
            w2a_ref[pl.ds(256 * tap, 256), :] = jnp.concatenate(bands, axis=0)


def faces(emb, slot, edge, w1, w2):
    whole = lambda *shape: pl.BlockSpec(shape, lambda i: (0,) * len(shape))
    return pl.pallas_call(
        face_kernel,
        grid=(2,),
        in_specs=[
            pl.BlockSpec((32, 128, 128), lambda i: (0, i, 0)),
            pl.BlockSpec((128, 128), lambda i: (i, 0)),
            whole(1, 128),
            whole(27, 32, 64),
            whole(27, 64, 64),
        ],
        out_specs=[
            pl.BlockSpec((2, 256, 128), lambda i: (i, 0, 0)),
            whole(128, 128),
            whole(1152, 128),
            whole(1152, 128),
            whole(2304, 128),
        ],
        out_shape=[
            jax.ShapeDtypeStruct((4, 256, 128), BF),
            jax.ShapeDtypeStruct((128, 128), F32),
            jax.ShapeDtypeStruct((1152, 128), BF),
            jax.ShapeDtypeStruct((1152, 128), BF),
            jax.ShapeDtypeStruct((2304, 128), BF),
        ],
        scratch_shapes=[
            pltpu.VMEM((32, 128, 128), F32),
            pltpu.VMEM((2, 128, 128), F32),
            pltpu.VMEM((4, 128, 128), F32),
            pltpu.VMEM((40, 128), F32),
        ],
        compiler_params=pltpu.CompilerParams(vmem_limit_bytes=32 << 20),
        cost_estimate=pl.CostEstimate(flops=600_000_000, bytes_accessed=4_000_000, transcendentals=0),
        name="faces",
    )(emb, slot, edge, w1, w2)


HEAD = 16
ROWS1 = 6 * 20 * 16
ROWS2 = 4 * 18 * 16


def conv_kernel(spot_ref, own_ref, za_ref, zb_ref, ya_ref, yb_ref, xl_ref, xr_ref, w1a_ref, w1b_ref, b1_ref, w2_ref,
                b2_ref, cnt_ref, face_ref, ctx_ref, send_ref, field, this, mixed, h0f, h0b, h0n, h1b, fine):
    gz, gy, gx = spot_ref[0], spot_ref[1], spot_ref[2]
    z_even, y_even = (gz & 1) == 0, (gy & 1) == 0
    widen = lambda ref, *at: ref[at].astype(F32) if at else ref[...].astype(F32)

    za, zb, own = widen(za_ref), widen(zb_ref), widen(own_ref)
    zs = (jnp.where(z_even, zb, za), own, jnp.where(z_even, za, zb))
    ya, yb = widen(ya_ref), widen(yb_ref)
    y_low, y_high = jnp.where(y_even, yb, ya), jnp.where(y_even, ya, yb)

    def by_z(parts):
        a, mid, b = parts
        return (jnp.where(z_even, b, a), mid, jnp.where(z_even, a, b))

    y_low = by_z([y_low[32 * i : 32 * i + 32] for i in range(3)])
    y_high = by_z([y_high[32 * i : 32 * i + 32] for i in range(3)])
    sides = []
    for ref in (xl_ref, xr_ref):
        whole = widen(ref)
        parts = by_z([whole[2 * i : 2 * i + 2] for i in range(3)])
        sides.append(parts)
    for part in range(3):
        for i in range(2):
            base = HEAD + (2 * part + i) * 320
            for y in range(16):
                field[pl.ds(base + 32 + 16 * y, 8), :] = zs[part][128 * i + 8 * y : 128 * i + 8 * y + 8]
            for y in range(2):
                field[pl.ds(base + 16 * y, 8), :] = y_low[part][16 * i + 8 * y : 16 * i + 8 * y + 8]
                field[pl.ds(base + 288 + 16 * y, 8), :] = y_high[part][16 * i + 8 * y : 16 * i + 8 * y + 8]
            for side, at in ((sides[0], -1), (sides[1], 8)):
                rows = side[part][i]
                a, b = rows[16:18], rows[18:20]
                low, high = jnp.where(y_even, b, a), jnp.where(y_even, a, b)
                column = jnp.concatenate([low, rows[0:16], high], axis=0)
                for y in range(20):
                    field[pl.ds(base + 16 * y + at, 1), :] = column[y : y + 1]

    lane = iota((320, 128), 1)
    for z in range(6):
        now = field[pl.ds(HEAD + 320 * z, 320), :]
        before = field[pl.ds(HEAD + 320 * z - 1, 320), :]
        this[pl.ds(320 * z, 320), :] = now.astype(BF)
        mixed[pl.ds(320 * z, 320), :] = jnp.where(lane < 64, now, before).astype(BF)

    row, lane = iota((288, 128), 0), iota((288, 128), 1)
    slot = row & 15
    keep = jnp.where((row < 16) & (gy == 0), 0.0, 1.0)
    keep = jnp.where((row >= 272) & (gy == 3), 0.0, keep)
    keep0 = jnp.where((slot == 0) & (lane < 64) & (gx == 0), 0.0, keep)
    keep0 = jnp.where((slot == 8) & (lane >= 64) & (gx == 7), 0.0, keep0)
    b1, b2 = b1_ref[...], b2_ref[...]

    def conv1(source, weights, z):
        total = None
        for t in range(0, 9, 2):
            group = range(t, min(t + 2, 9))
            at = [((z + tap // 3) * 20 + tap % 3) * 16 for tap in group]
            left = jnp.concatenate([source[pl.ds(r, 288), :] for r in at], axis=1)
            term = dot(left, weights[pl.ds(128 * t, 128 * len(at)), :])
            total = term if total is None else total + term
        return jnp.maximum(total + b1, 0.0)

    for z in range(4):
        inside = 1.0
        if z == 0:
            inside = jnp.where(gz == 0, 0.0, 1.0)
        if z == 3:
            inside = jnp.where(gz == 7, 0.0, 1.0)
        h0f[pl.ds(288 * z, 288), :] = conv1(mixed, w1b_ref, z) * (keep0 * inside)
        h1b[pl.ds(288 * z, 288), :] = (conv1(this, w1a_ref, z) * (keep * inside)).astype(BF)
    for z in range(4):
        h0b[pl.ds(288 * z, 288), :] = h0f[pl.ds(288 * z, 288), :].astype(BF)
        h0n[pl.ds(288 * z, 288), :] = h0f[pl.ds(288 * z + 1, 288), :].astype(BF)

    def conv2(first, second, z):
        total = None
        for tap in range(9):
            r = ((z + tap // 3) * 18 + tap % 3) * 16
            left = jnp.concatenate([first[pl.ds(r, 256), :], second[pl.ds(r, 256), :]], axis=1)
            term = dot(left, w2_ref[pl.ds(256 * tap, 256), :])
            total = term if total is None else total + term
        total = total.reshape(16, 16, 128)[:, :8, :].reshape(128, 128)
        return (total + b2).astype(BF)

    sums = None
    for z in range(2):
        for p, (first, second) in enumerate(((h0b, h1b), (h1b, h0n))):
            ctx = conv2(first, second, z)
            wide = ctx.astype(F32)
            fine[pl.ds(512 * z + 2 * p, 128, stride=4), :] = wide
            fine[pl.ds(512 * z + 2 * p + 1, 128, stride=4), :] = pltpu.roll(wide, 64, 1)
            term = dot(cnt_ref[2 * z + p], ctx)
            sums = term if sums is None else sums + term
    ctx_ref[...] = fine[...][:, :64].astype(BF)
    both = sums[:128] + pltpu.roll(sums[128:], 64, 1)
    send_ref[...] = jnp.where(iota((128, 128), 1) < 64, both, face_ref[...])


def convolve(spot, *arrays):
    return pl.pallas_call(
        conv_kernel,
        in_specs=[pl.BlockSpec(memory_space=pltpu.SMEM)] + [pl.BlockSpec(memory_space=pltpu.VMEM)] * len(arrays),
        out_specs=[pl.BlockSpec(memory_space=pltpu.VMEM)] * 2,
        out_shape=[jax.ShapeDtypeStruct((1024, 64), BF), jax.ShapeDtypeStruct((128, 128), F32)],
        scratch_shapes=[
            pltpu.VMEM((HEAD + ROWS1, 128), F32),
            pltpu.VMEM((ROWS1, 128), BF),
            pltpu.VMEM((ROWS1, 128), BF),
            pltpu.VMEM((ROWS2 + 16, 128), F32),
            pltpu.VMEM((ROWS2, 128), BF),
            pltpu.VMEM((ROWS2, 128), BF),
            pltpu.VMEM((ROWS2, 128), BF),
            pltpu.VMEM((1024, 128), F32),
        ],
        compiler_params=pltpu.CompilerParams(vmem_limit_bytes=32 << 20),
        cost_estimate=pl.CostEstimate(flops=1_000_000_000, bytes_accessed=3_000_000, transcendentals=0),
        name="convolve",
    )(spot, *arrays)


def edge_kernel(rows_ref, emb_ref, ctx_ref):
    rows = rows_ref[...]
    hits = jnp.where(rows[:, 97:98] == iota((128, 64), 1).astype(F32), 1.0, 0.0).astype(BF)
    sums = sum(dot(part, hits) for part in split3(rows.T))
    scale = jnp.maximum(sums[96:97], 1.0)
    ctx_ref[...] = sums[:64] / scale
    emb_ref[...] = sums[64:96] / scale


def edges(rows):
    return pl.pallas_call(
        edge_kernel,
        out_shape=[jax.ShapeDtypeStruct((32, 64), F32), jax.ShapeDtypeStruct((64, 64), F32)],
        name="edges",
    )(rows)


def pairs(first, count):
    return [pair for i in range(first, count - 1, 2) for pair in ((i, i + 1), (i + 1, i))]


def per_device(embedding, face_slot, face_edge, conv1_w, conv1_b, conv2_w, conv2_b):
    emb = embedding.reshape(32, 256, 128)
    gz, gy, gx = (lax.axis_index(a) for a in ("gz", "gy", "gx"))
    own = pool(emb)
    za = lax.ppermute(own, "gz", pairs(0, 8))
    zb = lax.ppermute(own, "gz", pairs(1, 8))
    cnt, face, w1a, w1b, w2a = faces(
        emb,
        face_slot.reshape(256, 128),
        face_edge.reshape(1, 128),
        jnp.swapaxes(conv1_w, 3, 4).reshape(27, 32, 64),
        conv2_w.reshape(27, 64, 64),
    )
    planes = [a.reshape(2, 16, 8, 128) for a in (za, own, zb)]
    y_even = (gy & 1) == 0

    def y_edge(high):
        first = jnp.where(high, 14, 0)
        return jnp.concatenate([lax.dynamic_slice_in_dim(a, first, 2, axis=1) for a in planes], axis=0)

    ya = lax.ppermute(y_edge(y_even), "gy", pairs(0, 4))
    yb = lax.ppermute(y_edge(jnp.logical_not(y_even)), "gy", pairs(1, 4))

    def x_edge(g):
        mid = jnp.concatenate([a[:, :, g] for a in planes], axis=0)
        return jnp.concatenate([mid, ya[:, :, g], yb[:, :, g]], axis=1)

    right = [(i, i + 1) for i in range(7)]
    xl = lax.ppermute(x_edge(7), "gx", right)
    xr = lax.ppermute(x_edge(0), "gx", [(b, a) for a, b in right])
    spot = jnp.stack([gz, gy, gx]).astype(jnp.int32)
    twice = lambda b: jnp.concatenate([b, b]).reshape(1, 128)
    context, send = convolve(
        spot, own, za, zb, ya.reshape(96, 128), yb.reshape(96, 128), xl, xr, w1a, w1b, twice(conv1_b), w2a,
        twice(conv2_b), cnt, face,
    )
    rows = lax.all_to_all(send, "gx", 0, 0, tiled=True)
    edge_emb, edge_ctx = edges(rows)
    context = jnp.transpose(context.reshape(2, 16, 32, 64), (3, 0, 1, 2))
    return (context, edge_emb, edge_ctx)


def solution(mesh):
    in_specs = (P(None, "gz", "gy", "gx"), P("gz", "gy", "gx"), P(("gz", "gy", "gx")), P(), P(), P(), P())
    out_specs = (P(None, "gz", "gy", "gx"), P(None, ("gz", "gy", "gx")), P(None, ("gz", "gy", "gx")))
    return jax.shard_map(per_device, mesh=mesh, in_specs=in_specs, out_specs=out_specs, check_vma=False)
```

```python
import jax
import jax.numpy as jnp
from jax import lax
from jax.experimental import pallas as pl
from jax.experimental.pallas import tpu as pltpu
from jax.sharding import PartitionSpec as P

BF = jnp.bfloat16
F32 = jnp.float32
NT = (((1,), (1,)), ((), ()))
NN = (((1,), (0,)), ((), ()))


def dot(a, b, dims=NN):
    return lax.dot_general(a, b, dims, preferred_element_type=F32)


def iota(shape, dim):
    return lax.broadcasted_iota(jnp.int32, shape, dim)


def split3(x):
    hi = x.astype(BF)
    rest = x - hi.astype(F32)
    mid = rest.astype(BF)
    low = (rest - mid.astype(F32)).astype(BF)
    return hi, mid, low


def pool_x_matrix():
    row, col = iota((32, 128), 0), iota((32, 128), 1)
    cell = 4 * (row & 7) + (row >> 3)
    return jnp.where((col >> 2) == cell, 1.0, 0.0).astype(BF)


def pool_kernel(emb_ref, out_ref, block, sums, arrived):
    chunks = arrived.shape[0]
    per = 32 // chunks
    copies = [
        pltpu.make_async_copy(emb_ref.at[pl.ds(per * i, per)], block.at[pl.ds(per * i, per)], arrived.at[i])
        for i in range(chunks)
    ]
    for copy in copies:
        copy.start()
    row, col = iota((32, 256), 0), iota((32, 256), 1)
    cell = ((col >> 7) << 4) + ((col & 63) >> 2)
    pool_zy = jnp.where(cell == row, 1.0, 0.0).astype(BF)
    pool_x = pool_x_matrix()
    lane = iota((8, 128), 1)
    far, near = lane < 64, (lane & 32) == 0
    for i in range(chunks):
        copies[i].wait()
        for c in range(per * i, per * i + per):
            sums[c] = dot(pool_zy, block[c])
    for part in range(8):
        rows = jnp.concatenate([sums[:, 4 * part + i, :] for i in range(4)], axis=0)
        cells = sum(dot(pool_x, term, NT) for term in split3(rows)) * (1.0 / 32.0)
        v = [cells[8 * i : 8 * i + 8] for i in range(4)]
        a = [jnp.where(far, v[i], pltpu.roll(v[i + 2], 64, 1)) for i in range(2)]
        b = [jnp.where(far, pltpu.roll(v[i], 64, 1), v[i + 2]) for i in range(2)]
        done = []
        for lo, hi in (a, b):
            done.append(jnp.where(near, lo, pltpu.roll(hi, 32, 1)))
            done.append(jnp.where(near, pltpu.roll(lo, 96, 1), hi))
        out_ref[pl.ds(32 * part, 32), :] = jnp.concatenate(done, axis=0).astype(BF)


def pool(emb):
    chunks = 2
    return pl.pallas_call(
        pool_kernel,
        in_specs=[pl.BlockSpec(memory_space=pl.ANY)],
        out_specs=pl.BlockSpec(memory_space=pltpu.VMEM),
        out_shape=pltpu.VMEM((256, 128), BF),
        scratch_shapes=[
            pltpu.VMEM((32, 256, 128), BF),
            pltpu.VMEM((32, 32, 128), F32),
            pltpu.SemaphoreType.DMA((chunks,)),
        ],
        compiler_params=pltpu.CompilerParams(vmem_limit_bytes=32 << 20),
        cost_estimate=pl.CostEstimate(flops=80_000_000, bytes_accessed=2_200_000, transcendentals=0),
        name="pool",
    )(pltpu.with_memory_space_constraint(emb, pltpu.HBM))


def banded(tap, taps):
    zero = jnp.zeros_like(taps(tap, 0))
    w = [taps(tap, k) if 0 <= k < 3 else zero for k in range(-1, 4)]
    return [jnp.concatenate([w[k + 1], w[k]], axis=1) for k in range(4)]


def face_kernel(emb_ref, slot_ref, edge_ref, w1_ref, w2_ref, cnt_ref, face_ref, w1a_ref, w1b_ref, w2a_ref,
                block, wide, order, cells, total, arrived):
    step = pl.program_id(0)
    last = pl.num_programs(0) - 1
    copies = [
        pltpu.make_async_copy(emb_ref.at[:, pl.ds(128 * i, 128), :], block.at[i], arrived.at[i]) for i in range(2)
    ]
    i0, i1 = iota((128, 128), 0), iota((128, 128), 1)

    @pl.when(step == 0)
    def _():
        for copy in copies:
            copy.start()
        label = jnp.broadcast_to(edge_ref[...], (128, 128))
        owner = ((label >> 6) & 7).astype(F32)
        local = (label & 63).astype(F32)
        ahead = jnp.where((owner == owner.T) & (i0 < i1), 1.0, 0.0)
        place = owner[0:1, :] * 16.0 + jnp.sum(ahead, axis=0, keepdims=True)
        chosen = place == i0.astype(F32)
        face = jnp.sum(jnp.where(chosen, i1.astype(F32), 0.0), axis=1, keepdims=True)
        edge = jnp.sum(jnp.where(chosen, local, 0.0), axis=1, keepdims=True)
        order[0] = jnp.broadcast_to(face, (128, 128))
        order[1] = jnp.broadcast_to(edge, (128, 128))
        total[...] = jnp.zeros_like(total)
        for tap in range(9):
            bands = banded(tap, lambda t, k: w1_ref[3 * t + k])
            w1a_ref[pl.ds(128 * tap, 128), :] = jnp.concatenate(bands, axis=0)
            w1b_ref[pl.ds(128 * tap, 128), :] = jnp.concatenate(bands[2:] + bands[:2], axis=0)
            bands = banded(tap, lambda t, k: w2_ref[3 * t + k].astype(F32).T.astype(BF))
            w2a_ref[pl.ds(256 * tap, 256), :] = jnp.concatenate(bands, axis=0)

    for i in range(2):

        @pl.when(step == i)
        def _():
            copies[i].wait()

    wide[...] = block[step].astype(F32).reshape(4096, 128)
    faces = order[0].astype(jnp.int32)
    pool_x = pool_x_matrix()
    pool_x8 = jnp.concatenate([pool_x] * 8, axis=1)
    sums = jnp.zeros((32, 128), F32)
    count = jnp.zeros((8, 128), F32)
    for yc in range(16):
        voxels, member = [], []
        for q in (64 * zi + 4 * yc + yy for zi in range(2) for yy in range(4)):
            voxels.append(wide[pl.ds(q, 32, stride=128), :].astype(BF))
            row = jnp.broadcast_to(slot_ref[q : q + 1, :], (128, 128))
            member.append(jnp.where(row == faces, 1.0, 0.0).astype(BF))
        left = jnp.concatenate([jnp.concatenate(voxels, axis=1), pool_x8], axis=0)
        out = dot(left, jnp.concatenate(member, axis=1), NT)
        sums = sums + out[:32]
        for x4 in range(4):
            part = out[32 + 8 * x4 : 40 + 8 * x4]
            cells[x4, 8 * yc : 8 * yc + 8, :] = part
            count = count + part
    total[0:32] += sums
    total[32:40] += count
    for x4 in range(4):
        cnt_ref[x4 // 2, 128 * (x4 % 2) : 128 * (x4 % 2) + 128, :] = cells[x4].T.astype(BF)

    @pl.when(step == last)
    def _():
        number = jnp.sum(total[32:40], axis=0, keepdims=True)
        stacked = jnp.concatenate(
            [jnp.zeros((64, 128), F32), total[0:32], jnp.broadcast_to(number, (32, 128))], axis=0
        )
        face_ref[...] = jnp.where(i1 == 97, order[1], stacked.T)


def faces(emb, slot, edge, w1, w2):
    whole = lambda *shape: pl.BlockSpec(shape, lambda i: (0,) * len(shape))
    return pl.pallas_call(
        face_kernel,
        grid=(2,),
        in_specs=[
            pl.BlockSpec(memory_space=pl.ANY),
            pl.BlockSpec((128, 128), lambda i: (i, 0)),
            whole(1, 128),
            whole(27, 32, 64),
            whole(27, 64, 64),
        ],
        out_specs=[
            pl.BlockSpec((2, 256, 128), lambda i: (i, 0, 0)),
            whole(128, 128),
            whole(1152, 128),
            whole(1152, 128),
            whole(2304, 128),
        ],
        out_shape=[
            jax.ShapeDtypeStruct((4, 256, 128), BF),
            jax.ShapeDtypeStruct((128, 128), F32),
            jax.ShapeDtypeStruct((1152, 128), BF),
            jax.ShapeDtypeStruct((1152, 128), BF),
            jax.ShapeDtypeStruct((2304, 128), BF),
        ],
        scratch_shapes=[
            pltpu.VMEM((2, 32, 128, 128), BF),
            pltpu.VMEM((4096, 128), F32),
            pltpu.VMEM((2, 128, 128), F32),
            pltpu.VMEM((4, 128, 128), F32),
            pltpu.VMEM((40, 128), F32),
            pltpu.SemaphoreType.DMA((2,)),
        ],
        compiler_params=pltpu.CompilerParams(vmem_limit_bytes=32 << 20),
        cost_estimate=pl.CostEstimate(flops=600_000_000, bytes_accessed=4_000_000, transcendentals=0),
        name="faces",
    )(pltpu.with_memory_space_constraint(emb, pltpu.HBM), slot, edge, w1, w2)


HEAD = 16
ROWS1 = 6 * 20 * 16
ROWS2 = 4 * 18 * 16


def conv_kernel(spot_ref, own_ref, za_ref, zb_ref, ya_ref, yb_ref, xl_ref, xr_ref, far_ref, w1a_ref, w1b_ref, b1_ref,
                w2_ref, b2_ref, cnt_ref, face_ref, ctx_ref, send_ref, field, this, mixed, h0f, h0b, h0n, h1b, fine):
    gz, gy, gx = spot_ref[0], spot_ref[1], spot_ref[2]
    z_even, y_even = (gz & 1) == 0, (gy & 1) == 0
    widen = lambda ref, *at: ref[at].astype(F32) if at else ref[...].astype(F32)

    za, zb, own = widen(za_ref), widen(zb_ref), widen(own_ref)
    zs = (jnp.where(z_even, zb, za), own, jnp.where(z_even, za, zb))
    ya, yb = widen(ya_ref), widen(yb_ref)
    y_low, y_high = jnp.where(y_even, yb, ya), jnp.where(y_even, ya, yb)

    def by_z(parts):
        a, mid, b = parts
        return (jnp.where(z_even, b, a), mid, jnp.where(z_even, a, b))

    y_low = by_z([y_low[32 * i : 32 * i + 32] for i in range(3)])
    y_high = by_z([y_high[32 * i : 32 * i + 32] for i in range(3)])
    sides = []
    far = widen(far_ref)
    for ref, end in ((xl_ref, 4), (xr_ref, 3)):
        whole = jnp.where(gx == end, far, widen(ref))
        parts = by_z([whole[2 * i : 2 * i + 2] for i in range(3)])
        sides.append(parts)
    for part in range(3):
        for i in range(2):
            base = HEAD + (2 * part + i) * 320
            for y in range(16):
                field[pl.ds(base + 32 + 16 * y, 8), :] = zs[part][128 * i + 8 * y : 128 * i + 8 * y + 8]
            for y in range(2):
                field[pl.ds(base + 16 * y, 8), :] = y_low[part][16 * i + 8 * y : 16 * i + 8 * y + 8]
                field[pl.ds(base + 288 + 16 * y, 8), :] = y_high[part][16 * i + 8 * y : 16 * i + 8 * y + 8]
            for side, at in ((sides[0], -1), (sides[1], 8)):
                rows = side[part][i]
                a, b = rows[16:18], rows[18:20]
                low, high = jnp.where(y_even, b, a), jnp.where(y_even, a, b)
                column = jnp.concatenate([low, rows[0:16], high], axis=0)
                for y in range(20):
                    field[pl.ds(base + 16 * y + at, 1), :] = column[y : y + 1]

    lane = iota((320, 128), 1)
    for z in range(6):
        now = field[pl.ds(HEAD + 320 * z, 320), :]
        before = field[pl.ds(HEAD + 320 * z - 1, 320), :]
        this[pl.ds(320 * z, 320), :] = now.astype(BF)
        mixed[pl.ds(320 * z, 320), :] = jnp.where(lane < 64, now, before).astype(BF)

    row, lane = iota((288, 128), 0), iota((288, 128), 1)
    slot = row & 15
    keep = jnp.where((row < 16) & (gy == 0), 0.0, 1.0)
    keep = jnp.where((row >= 272) & (gy == 3), 0.0, keep)
    keep0 = jnp.where((slot == 0) & (lane < 64) & (gx == 0), 0.0, keep)
    keep0 = jnp.where((slot == 8) & (lane >= 64) & (gx == 7), 0.0, keep0)
    b1, b2 = b1_ref[...], b2_ref[...]

    def conv1(source, weights, z):
        total = None
        for t in range(0, 9, 2):
            group = range(t, min(t + 2, 9))
            at = [((z + tap // 3) * 20 + tap % 3) * 16 for tap in group]
            left = jnp.concatenate([source[pl.ds(r, 288), :] for r in at], axis=1)
            term = dot(left, weights[pl.ds(128 * t, 128 * len(at)), :])
            total = term if total is None else total + term
        return jnp.maximum(total + b1, 0.0)

    for z in range(4):
        inside = 1.0
        if z == 0:
            inside = jnp.where(gz == 0, 0.0, 1.0)
        if z == 3:
            inside = jnp.where(gz == 7, 0.0, 1.0)
        h0f[pl.ds(288 * z, 288), :] = conv1(mixed, w1b_ref, z) * (keep0 * inside)
        h1b[pl.ds(288 * z, 288), :] = (conv1(this, w1a_ref, z) * (keep * inside)).astype(BF)
    for z in range(4):
        h0b[pl.ds(288 * z, 288), :] = h0f[pl.ds(288 * z, 288), :].astype(BF)
        h0n[pl.ds(288 * z, 288), :] = h0f[pl.ds(288 * z + 1, 288), :].astype(BF)

    def conv2(first, second, z):
        total = None
        for tap in range(9):
            r = ((z + tap // 3) * 18 + tap % 3) * 16
            left = jnp.concatenate([first[pl.ds(r, 256), :], second[pl.ds(r, 256), :]], axis=1)
            term = dot(left, w2_ref[pl.ds(256 * tap, 256), :])
            total = term if total is None else total + term
        total = total.reshape(16, 16, 128)[:, :8, :].reshape(128, 128)
        return (total + b2).astype(BF)

    sums = None
    for z in range(2):
        for p, (first, second) in enumerate(((h0b, h1b), (h1b, h0n))):
            ctx = conv2(first, second, z)
            wide = ctx.astype(F32)
            fine[pl.ds(512 * z + 2 * p, 128, stride=4), :] = wide
            fine[pl.ds(512 * z + 2 * p + 1, 128, stride=4), :] = pltpu.roll(wide, 64, 1)
            term = dot(cnt_ref[2 * z + p], ctx)
            sums = term if sums is None else sums + term
    ctx_ref[...] = fine[...][:, :64].astype(BF)
    both = sums[:128] + pltpu.roll(sums[128:], 64, 1)
    send_ref[...] = jnp.where(iota((128, 128), 1) < 64, both, face_ref[...])


def convolve(spot, *arrays):
    return pl.pallas_call(
        conv_kernel,
        in_specs=[pl.BlockSpec(memory_space=pltpu.SMEM)] + [pl.BlockSpec(memory_space=pltpu.VMEM)] * len(arrays),
        out_specs=[pl.BlockSpec(memory_space=pltpu.VMEM)] * 2,
        out_shape=[jax.ShapeDtypeStruct((1024, 64), BF), jax.ShapeDtypeStruct((128, 128), F32)],
        scratch_shapes=[
            pltpu.VMEM((HEAD + ROWS1, 128), F32),
            pltpu.VMEM((ROWS1, 128), BF),
            pltpu.VMEM((ROWS1, 128), BF),
            pltpu.VMEM((ROWS2 + 16, 128), F32),
            pltpu.VMEM((ROWS2, 128), BF),
            pltpu.VMEM((ROWS2, 128), BF),
            pltpu.VMEM((ROWS2, 128), BF),
            pltpu.VMEM((1024, 128), F32),
        ],
        compiler_params=pltpu.CompilerParams(vmem_limit_bytes=32 << 20),
        cost_estimate=pl.CostEstimate(flops=1_000_000_000, bytes_accessed=3_000_000, transcendentals=0),
        name="convolve",
    )(spot, *arrays)


def edge_kernel(rows_ref, emb_ref, ctx_ref):
    rows = rows_ref[...]
    hits = jnp.where(rows[:, 97:98] == iota((128, 64), 1).astype(F32), 1.0, 0.0).astype(BF)
    sums = sum(dot(part, hits) for part in split3(rows.T))
    scale = jnp.maximum(sums[96:97], 1.0)
    ctx_ref[...] = sums[:64] / scale
    emb_ref[...] = sums[64:96] / scale


def edges(rows):
    return pl.pallas_call(
        edge_kernel,
        out_shape=[jax.ShapeDtypeStruct((32, 64), F32), jax.ShapeDtypeStruct((64, 64), F32)],
        name="edges",
    )(rows)


def pairs(first, count):
    return [pair for i in range(first, count - 1, 2) for pair in ((i, i + 1), (i + 1, i))]


def per_device(embedding, face_slot, face_edge, conv1_w, conv1_b, conv2_w, conv2_b):
    emb = embedding.reshape(32, 256, 128)
    gz, gy, gx = (lax.axis_index(a) for a in ("gz", "gy", "gx"))
    own = pool(emb)
    za = lax.ppermute(own, "gz", pairs(0, 8))
    zb = lax.ppermute(own, "gz", pairs(1, 8))
    cnt, face, w1a, w1b, w2a = faces(
        emb,
        face_slot.reshape(256, 128),
        face_edge.reshape(1, 128),
        jnp.swapaxes(conv1_w, 3, 4).reshape(27, 32, 64),
        conv2_w.reshape(27, 64, 64),
    )
    planes = [a.reshape(2, 16, 8, 128) for a in (za, own, zb)]
    y_even = (gy & 1) == 0

    def y_edge(high):
        first = jnp.where(high, 14, 0)
        return jnp.concatenate([lax.dynamic_slice_in_dim(a, first, 2, axis=1) for a in planes], axis=0)

    ya = lax.ppermute(y_edge(y_even), "gy", pairs(0, 4))
    yb = lax.ppermute(y_edge(jnp.logical_not(y_even)), "gy", pairs(1, 4))

    def x_edge(g):
        mid = jnp.concatenate([a[:, :, g] for a in planes], axis=0)
        return jnp.concatenate([mid, ya[:, :, g], yb[:, :, g]], axis=1)

    low, high = x_edge(0), x_edge(7)
    far = lax.ppermute(jnp.where(gx == 3, high, low), "gx", [(3, 4), (4, 3)])
    right = [(i, i + 1) for i in range(7) if i != 3]
    xl = lax.ppermute(high, "gx", right)
    xr = lax.ppermute(low, "gx", [(b, a) for a, b in right])
    spot = jnp.stack([gz, gy, gx]).astype(jnp.int32)
    twice = lambda b: jnp.concatenate([b, b]).reshape(1, 128)
    context, send = convolve(
        spot, own, za, zb, ya.reshape(96, 128), yb.reshape(96, 128), xl, xr, far, w1a, w1b, twice(conv1_b), w2a,
        twice(conv2_b), cnt, face,
    )
    rows = lax.all_to_all(send, "gx", 0, 0, tiled=True)
    edge_emb, edge_ctx = edges(rows)
    context = jnp.transpose(context.reshape(2, 16, 32, 64), (3, 0, 1, 2))
    return (context, edge_emb, edge_ctx)


def solution(mesh):
    in_specs = (P(None, "gz", "gy", "gx"), P("gz", "gy", "gx"), P(("gz", "gy", "gx")), P(), P(), P(), P())
    out_specs = (P(None, "gz", "gy", "gx"), P(None, ("gz", "gy", "gx")), P(None, ("gz", "gy", "gx")))
    return jax.shard_map(per_device, mesh=mesh, in_specs=in_specs, out_specs=out_specs, check_vma=False)
```

```python
import functools

import jax
import jax.numpy as jnp
from jax import lax
from jax.experimental import pallas as pl
from jax.experimental.pallas import tpu as pltpu
from jax.sharding import PartitionSpec as P

BF = jnp.bfloat16
F32 = jnp.float32
NT = (((1,), (1,)), ((), ()))
NN = (((1,), (0,)), ((), ()))


def dot(a, b, dims=NN):
    return lax.dot_general(a, b, dims, preferred_element_type=F32)


def keep(array):
    return pltpu.with_memory_space_constraint(array, pltpu.VMEM)


def iota(shape, dim):
    return lax.broadcasted_iota(jnp.int32, shape, dim)


def split3(x):
    hi = x.astype(BF)
    rest = x - hi.astype(F32)
    mid = rest.astype(BF)
    low = (rest - mid.astype(F32)).astype(BF)
    return hi, mid, low


def pool_x_matrix():
    row, col = iota((32, 128), 0), iota((32, 128), 1)
    cell = 4 * (row & 7) + (row >> 3)
    return jnp.where((col >> 2) == cell, 1.0, 0.0).astype(BF)


def pool_kernel(emb_ref, out_ref, block, sums, arrived):
    chunks = arrived.shape[0]
    per = 32 // chunks
    copies = [
        pltpu.make_async_copy(emb_ref.at[pl.ds(per * i, per)], block.at[pl.ds(per * i, per)], arrived.at[i])
        for i in range(chunks)
    ]
    for copy in copies:
        copy.start()
    row, col = iota((32, 256), 0), iota((32, 256), 1)
    cell = ((col >> 7) << 4) + ((col & 63) >> 2)
    pool_zy = jnp.where(cell == row, 1.0, 0.0).astype(BF)
    pool_x = pool_x_matrix()
    lane = iota((8, 128), 1)
    far, near = lane < 64, (lane & 32) == 0
    for i in range(chunks):
        copies[i].wait()
        for c in range(per * i, per * i + per):
            sums[c] = dot(pool_zy, block[c])
    for part in range(8):
        rows = jnp.concatenate([sums[:, 4 * part + i, :] for i in range(4)], axis=0)
        cells = sum(dot(pool_x, term, NT) for term in split3(rows)) * (1.0 / 32.0)
        v = [cells[8 * i : 8 * i + 8] for i in range(4)]
        a = [jnp.where(far, v[i], pltpu.roll(v[i + 2], 64, 1)) for i in range(2)]
        b = [jnp.where(far, pltpu.roll(v[i], 64, 1), v[i + 2]) for i in range(2)]
        done = []
        for lo, hi in (a, b):
            done.append(jnp.where(near, lo, pltpu.roll(hi, 32, 1)))
            done.append(jnp.where(near, pltpu.roll(lo, 96, 1), hi))
        out_ref[pl.ds(32 * part, 32), :] = jnp.concatenate(done, axis=0).astype(BF)


def pool(emb):
    chunks = 2
    return pl.pallas_call(
        pool_kernel,
        in_specs=[pl.BlockSpec(memory_space=pl.ANY)],
        out_specs=[pl.BlockSpec(memory_space=pltpu.VMEM)] * 2,
        out_shape=[pltpu.VMEM((256, 128), BF), pltpu.VMEM((32, 256, 128), BF)],
        scratch_shapes=[
            pltpu.VMEM((32, 32, 128), F32),
            pltpu.SemaphoreType.DMA((chunks,)),
        ],
        compiler_params=pltpu.CompilerParams(vmem_limit_bytes=32 << 20),
        cost_estimate=pl.CostEstimate(flops=80_000_000, bytes_accessed=2_200_000, transcendentals=0),
        name="pool",
    )(pltpu.with_memory_space_constraint(emb, pltpu.HBM))


def banded(tap, taps):
    zero = jnp.zeros_like(taps(tap, 0))
    w = [taps(tap, k) if 0 <= k < 3 else zero for k in range(-1, 4)]
    return [jnp.concatenate([w[k + 1], w[k]], axis=1) for k in range(4)]


def prepare_kernel(edge_ref, w1_ref, w2_ref, order_ref, w1a_ref, w1b_ref, w2a_ref):
    i0, i1 = iota((128, 128), 0), iota((128, 128), 1)
    label = jnp.broadcast_to(edge_ref[...], (128, 128))
    owner = ((label >> 6) & 7).astype(F32)
    local = (label & 63).astype(F32)
    ahead = jnp.where((owner == owner.T) & (i0 < i1), 1.0, 0.0)
    place = owner[0:1, :] * 16.0 + jnp.sum(ahead, axis=0, keepdims=True)
    chosen = place == i0.astype(F32)
    face = jnp.sum(jnp.where(chosen, i1.astype(F32), 0.0), axis=1, keepdims=True)
    edge = jnp.sum(jnp.where(chosen, local, 0.0), axis=1, keepdims=True)
    order_ref[0] = jnp.broadcast_to(face, (128, 128))
    order_ref[1] = jnp.broadcast_to(edge, (128, 128))
    for tap in range(9):
        bands = banded(tap, lambda t, k: w1_ref[3 * t + k])
        w1a_ref[pl.ds(128 * tap, 128), :] = jnp.concatenate(bands, axis=0)
        w1b_ref[pl.ds(128 * tap, 128), :] = jnp.concatenate(bands[2:] + bands[:2], axis=0)
        bands = banded(tap, lambda t, k: w2_ref[3 * t + k].astype(F32).T.astype(BF))
        w2a_ref[pl.ds(256 * tap, 256), :] = jnp.concatenate(bands, axis=0)


def prepare(edge, w1, w2):
    return pl.pallas_call(
        prepare_kernel,
        in_specs=[pl.BlockSpec(memory_space=pltpu.VMEM)] * 3,
        out_specs=[pl.BlockSpec(memory_space=pltpu.VMEM)] * 4,
        out_shape=[
            pltpu.VMEM((2, 128, 128), F32),
            pltpu.VMEM((1152, 128), BF),
            pltpu.VMEM((1152, 128), BF),
            pltpu.VMEM((2304, 128), BF),
        ],
        compiler_params=pltpu.CompilerParams(vmem_limit_bytes=16 << 20),
        cost_estimate=pl.CostEstimate(flops=1_000_000_000, bytes_accessed=2_000_000, transcendentals=0),
        name="prepare",
    )(edge, w1, w2)


def face_kernel(half, emb_ref, slot_ref, order_ref, before_ref, cnt_ref, after_ref, wide, cells):
    wide[...] = emb_ref[:, pl.ds(128 * half, 128), :].astype(F32).reshape(4096, 128)
    faces = order_ref[0].astype(jnp.int32)
    pool_x8 = jnp.concatenate([pool_x_matrix()] * 8, axis=1)
    sums = jnp.zeros((32, 128), F32)
    count = jnp.zeros((8, 128), F32)
    for yc in range(16):
        voxels, member = [], []
        for q in (64 * zi + 4 * yc + yy for zi in range(2) for yy in range(4)):
            voxels.append(wide[pl.ds(q, 32, stride=128), :].astype(BF))
            row = jnp.broadcast_to(slot_ref[128 * half + q : 128 * half + q + 1, :], (128, 128))
            member.append(jnp.where(row == faces, 1.0, 0.0).astype(BF))
        left = jnp.concatenate([jnp.concatenate(voxels, axis=1), pool_x8], axis=0)
        out = dot(left, jnp.concatenate(member, axis=1), NT)
        sums = sums + out[:32]
        for x4 in range(4):
            part = out[32 + 8 * x4 : 40 + 8 * x4]
            cells[x4, 8 * yc : 8 * yc + 8, :] = part
            count = count + part
    for x4 in range(4):
        cnt_ref[x4 // 2, 128 * (x4 % 2) : 128 * (x4 % 2) + 128, :] = cells[x4].T.astype(BF)
    if half == 0:
        after_ref[0:32] = sums
        after_ref[32:40] = count
    else:
        sums = sums + before_ref[0:32]
        number = jnp.sum(count + before_ref[32:40], axis=0, keepdims=True)
        stacked = jnp.concatenate([jnp.zeros((64, 128), F32), sums, jnp.broadcast_to(number, (32, 128))], axis=0)
        after_ref[...] = jnp.where(iota((128, 128), 1) == 97, order_ref[1], stacked.T)


def faces(half, emb, slot, order, before):
    return pl.pallas_call(
        functools.partial(face_kernel, half),
        in_specs=[pl.BlockSpec(memory_space=pltpu.VMEM)] * 4,
        out_specs=[pl.BlockSpec(memory_space=pltpu.VMEM)] * 2,
        out_shape=[pltpu.VMEM((2, 256, 128), BF), pltpu.VMEM((128 if half else 40, 128), F32)],
        scratch_shapes=[pltpu.VMEM((4096, 128), F32), pltpu.VMEM((4, 128, 128), F32)],
        compiler_params=pltpu.CompilerParams(vmem_limit_bytes=16 << 20),
        cost_estimate=pl.CostEstimate(flops=2_000_000_000, bytes_accessed=4_000_000, transcendentals=0),
        name="faces",
    )(keep(emb), slot, keep(order), keep(before))


HEAD = 16
ROWS1 = 6 * 20 * 16
ROWS2 = 4 * 18 * 16


def conv_kernel(spot_ref, own_ref, za_ref, zb_ref, ya_ref, yb_ref, xa_ref, xb_ref, w1a_ref, w1b_ref, b1_ref, w2_ref,
                b2_ref, cnt0_ref, cnt1_ref, face_ref, ctx_ref, send_ref, field, this, mixed, h0f, h0b, h0n, h1b, fine):
    gz, gy, gx = spot_ref[0], spot_ref[1], spot_ref[2]
    z_even, y_even, x_even = (gz & 1) == 0, (gy & 1) == 0, (gx & 1) == 0
    widen = lambda ref, *at: ref[at].astype(F32) if at else ref[...].astype(F32)

    za, zb, own = widen(za_ref), widen(zb_ref), widen(own_ref)
    zs = (jnp.where(z_even, zb, za), own, jnp.where(z_even, za, zb))
    ya, yb = widen(ya_ref), widen(yb_ref)
    y_low, y_high = jnp.where(y_even, yb, ya), jnp.where(y_even, ya, yb)

    def by_z(parts):
        a, mid, b = parts
        return (jnp.where(z_even, b, a), mid, jnp.where(z_even, a, b))

    y_low = by_z([y_low[32 * i : 32 * i + 32] for i in range(3)])
    y_high = by_z([y_high[32 * i : 32 * i + 32] for i in range(3)])
    sides = []
    xa, xb = widen(xa_ref), widen(xb_ref)
    for whole in (jnp.where(x_even, xb, xa), jnp.where(x_even, xa, xb)):
        parts = by_z([whole[2 * i : 2 * i + 2] for i in range(3)])
        sides.append(parts)
    for part in range(3):
        for i in range(2):
            base = HEAD + (2 * part + i) * 320
            for y in range(16):
                field[pl.ds(base + 32 + 16 * y, 8), :] = zs[part][128 * i + 8 * y : 128 * i + 8 * y + 8]
            for y in range(2):
                field[pl.ds(base + 16 * y, 8), :] = y_low[part][16 * i + 8 * y : 16 * i + 8 * y + 8]
                field[pl.ds(base + 288 + 16 * y, 8), :] = y_high[part][16 * i + 8 * y : 16 * i + 8 * y + 8]
            for side, at in ((sides[0], -1), (sides[1], 8)):
                rows = side[part][i]
                a, b = rows[16:18], rows[18:20]
                low, high = jnp.where(y_even, b, a), jnp.where(y_even, a, b)
                column = jnp.concatenate([low, rows[0:16], high], axis=0)
                for y in range(20):
                    field[pl.ds(base + 16 * y + at, 1), :] = column[y : y + 1]

    lane = iota((320, 128), 1)
    for z in range(6):
        now = field[pl.ds(HEAD + 320 * z, 320), :]
        before = field[pl.ds(HEAD + 320 * z - 1, 320), :]
        this[pl.ds(320 * z, 320), :] = now.astype(BF)
        mixed[pl.ds(320 * z, 320), :] = jnp.where(lane < 64, now, before).astype(BF)

    row, lane = iota((288, 128), 0), iota((288, 128), 1)
    slot = row & 15
    stay = jnp.where((row < 16) & (gy == 0), 0.0, 1.0)
    stay = jnp.where((row >= 272) & (gy == 3), 0.0, stay)
    stay0 = jnp.where((slot == 0) & (lane < 64) & (gx == 0), 0.0, stay)
    stay0 = jnp.where((slot == 8) & (lane >= 64) & (gx == 7), 0.0, stay0)
    b1, b2 = b1_ref[...], b2_ref[...]

    def conv1(source, weights, z):
        total = None
        for t in range(0, 9, 2):
            group = range(t, min(t + 2, 9))
            at = [((z + tap // 3) * 20 + tap % 3) * 16 for tap in group]
            left = jnp.concatenate([source[pl.ds(r, 288), :] for r in at], axis=1)
            term = dot(left, weights[pl.ds(128 * t, 128 * len(at)), :])
            total = term if total is None else total + term
        return jnp.maximum(total + b1, 0.0)

    for z in range(4):
        inside = 1.0
        if z == 0:
            inside = jnp.where(gz == 0, 0.0, 1.0)
        if z == 3:
            inside = jnp.where(gz == 7, 0.0, 1.0)
        h0f[pl.ds(288 * z, 288), :] = conv1(mixed, w1b_ref, z) * (stay0 * inside)
        h1b[pl.ds(288 * z, 288), :] = (conv1(this, w1a_ref, z) * (stay * inside)).astype(BF)
    for z in range(4):
        h0b[pl.ds(288 * z, 288), :] = h0f[pl.ds(288 * z, 288), :].astype(BF)
        h0n[pl.ds(288 * z, 288), :] = h0f[pl.ds(288 * z + 1, 288), :].astype(BF)

    def conv2(first, second, z):
        total = None
        for tap in range(9):
            r = ((z + tap // 3) * 18 + tap % 3) * 16
            left = jnp.concatenate([first[pl.ds(r, 256), :], second[pl.ds(r, 256), :]], axis=1)
            term = dot(left, w2_ref[pl.ds(256 * tap, 256), :])
            total = term if total is None else total + term
        total = total.reshape(16, 16, 128)[:, :8, :].reshape(128, 128)
        return (total + b2).astype(BF)

    sums = None
    for z in range(2):
        for p, (first, second) in enumerate(((h0b, h1b), (h1b, h0n))):
            ctx = conv2(first, second, z)
            wide = ctx.astype(F32)
            fine[pl.ds(512 * z + 2 * p, 128, stride=4), :] = wide
            fine[pl.ds(512 * z + 2 * p + 1, 128, stride=4), :] = pltpu.roll(wide, 64, 1)
            term = dot((cnt0_ref, cnt1_ref)[z][p], ctx)
            sums = term if sums is None else sums + term
    ctx_ref[...] = fine[...][:, :64].astype(BF)
    both = sums[:128] + pltpu.roll(sums[128:], 64, 1)
    send_ref[...] = jnp.where(iota((128, 128), 1) < 64, both, face_ref[...])


def convolve(spot, *arrays):
    return pl.pallas_call(
        conv_kernel,
        in_specs=[pl.BlockSpec(memory_space=pltpu.SMEM)] + [pl.BlockSpec(memory_space=pltpu.VMEM)] * len(arrays),
        out_specs=[pl.BlockSpec(memory_space=pltpu.VMEM)] * 2,
        out_shape=[jax.ShapeDtypeStruct((1024, 64), BF), pltpu.VMEM((128, 128), F32)],
        scratch_shapes=[
            pltpu.VMEM((HEAD + ROWS1, 128), F32),
            pltpu.VMEM((ROWS1, 128), BF),
            pltpu.VMEM((ROWS1, 128), BF),
            pltpu.VMEM((ROWS2 + 16, 128), F32),
            pltpu.VMEM((ROWS2, 128), BF),
            pltpu.VMEM((ROWS2, 128), BF),
            pltpu.VMEM((ROWS2, 128), BF),
            pltpu.VMEM((1024, 128), F32),
        ],
        compiler_params=pltpu.CompilerParams(vmem_limit_bytes=32 << 20),
        cost_estimate=pl.CostEstimate(flops=1_000_000_000, bytes_accessed=3_000_000, transcendentals=0),
        name="convolve",
    )(spot, *arrays)


def edge_kernel(rows_ref, emb_ref, ctx_ref):
    rows = rows_ref[...]
    hits = jnp.where(rows[:, 97:98] == iota((128, 64), 1).astype(F32), 1.0, 0.0).astype(BF)
    sums = sum(dot(part, hits) for part in split3(rows.T))
    scale = jnp.maximum(sums[96:97], 1.0)
    ctx_ref[...] = sums[:64] / scale
    emb_ref[...] = sums[64:96] / scale


def edges(rows):
    return pl.pallas_call(
        edge_kernel,
        out_shape=[jax.ShapeDtypeStruct((32, 64), F32), jax.ShapeDtypeStruct((64, 64), F32)],
        name="edges",
    )(rows)


def pairs(first, count):
    return [pair for i in range(first, count - 1, 2) for pair in ((i, i + 1), (i + 1, i))]


def per_device(embedding, face_slot, face_edge, conv1_w, conv1_b, conv2_w, conv2_b):
    emb = embedding.reshape(32, 256, 128)
    gz, gy, gx = (lax.axis_index(a) for a in ("gz", "gy", "gx"))
    slot = face_slot.reshape(256, 128)
    own, voxels = pool(emb)
    zb = lax.ppermute(own, "gz", pairs(1, 8))
    za = lax.ppermute(own, "gz", pairs(0, 8))
    order, w1a, w1b, w2a = prepare(
        face_edge.reshape(1, 128),
        jnp.swapaxes(conv1_w, 3, 4).reshape(27, 32, 64),
        conv2_w.reshape(27, 64, 64),
    )
    za, zb, order = lax.optimization_barrier((za, zb, order))
    planes = [a.reshape(2, 16, 8, 128) for a in (za, own, zb)]
    y_even, x_even = (gy & 1) == 0, (gx & 1) == 0

    def y_edge(high):
        first = jnp.where(high, 14, 0)
        return jnp.concatenate([lax.dynamic_slice_in_dim(a, first, 2, axis=1) for a in planes], axis=0)

    yb = lax.ppermute(y_edge(jnp.logical_not(y_even)), "gy", pairs(1, 4))
    ya = lax.ppermute(y_edge(y_even), "gy", pairs(0, 4))
    cnt0, half = faces(0, voxels, slot, order, order[0, :40])
    ya, yb, half = lax.optimization_barrier((ya, yb, half))

    def x_edge(g):
        mid = jnp.concatenate([a[:, :, g] for a in planes], axis=0)
        return jnp.concatenate([mid, ya[:, :, g], yb[:, :, g]], axis=1)

    low, high = x_edge(0), x_edge(7)
    xb = lax.ppermute(jnp.where(x_even, low, high), "gx", pairs(1, 8))
    xa = lax.ppermute(jnp.where(x_even, high, low), "gx", pairs(0, 8))
    cnt1, face = faces(1, voxels, slot, order, half)
    spot = jnp.stack([gz, gy, gx]).astype(jnp.int32)
    twice = lambda b: jnp.concatenate([b, b]).reshape(1, 128)
    context, send = convolve(
        spot, own, za, zb, ya.reshape(96, 128), yb.reshape(96, 128), xa, xb, keep(w1a), keep(w1b), twice(conv1_b),
        keep(w2a), twice(conv2_b), keep(cnt0), keep(cnt1), keep(face),
    )
    rows = lax.all_to_all(send, "gx", 0, 0, tiled=True)
    edge_emb, edge_ctx = edges(rows)
    context = jnp.transpose(context.reshape(2, 16, 32, 64), (3, 0, 1, 2))
    return (context, edge_emb, edge_ctx)


def solution(mesh):
    in_specs = (P(None, "gz", "gy", "gx"), P("gz", "gy", "gx"), P(("gz", "gy", "gx")), P(), P(), P(), P())
    out_specs = (P(None, "gz", "gy", "gx"), P(None, ("gz", "gy", "gx")), P(None, ("gz", "gy", "gx")))
    return jax.shard_map(per_device, mesh=mesh, in_specs=in_specs, out_specs=out_specs, check_vma=False)
```

```python
import functools

import jax
import jax.numpy as jnp
from jax import lax
from jax.experimental import pallas as pl
from jax.experimental.pallas import tpu as pltpu
from jax.sharding import PartitionSpec as P

BF = jnp.bfloat16
F32 = jnp.float32
NT = (((1,), (1,)), ((), ()))
NN = (((1,), (0,)), ((), ()))


def dot(a, b, dims=NN):
    return lax.dot_general(a, b, dims, preferred_element_type=F32)


def keep(array):
    return pltpu.with_memory_space_constraint(array, pltpu.VMEM)


def iota(shape, dim):
    return lax.broadcasted_iota(jnp.int32, shape, dim)


def split3(x):
    hi = x.astype(BF)
    rest = x - hi.astype(F32)
    mid = rest.astype(BF)
    low = (rest - mid.astype(F32)).astype(BF)
    return hi, mid, low


def pool_x_matrix():
    row, col = iota((32, 128), 0), iota((32, 128), 1)
    cell = 4 * (row & 7) + (row >> 3)
    return jnp.where((col >> 2) == cell, 1.0, 0.0).astype(BF)


def pool_kernel(emb_ref, out_ref, block, sums, arrived):
    chunks = arrived.shape[0]
    per = 32 // chunks
    copies = [
        pltpu.make_async_copy(emb_ref.at[pl.ds(per * i, per)], block.at[pl.ds(per * i, per)], arrived.at[i])
        for i in range(chunks)
    ]
    for copy in copies:
        copy.start()
    row, col = iota((32, 256), 0), iota((32, 256), 1)
    cell = ((col >> 7) << 4) + ((col & 63) >> 2)
    pool_zy = jnp.where(cell == row, 1.0, 0.0).astype(BF)
    pool_x = pool_x_matrix()
    lane = iota((8, 128), 1)
    far, near = lane < 64, (lane & 32) == 0
    for i in range(chunks):
        copies[i].wait()
        for c in range(per * i, per * i + per):
            sums[c] = dot(pool_zy, block[c])
    for part in range(8):
        rows = jnp.concatenate([sums[:, 4 * part + i, :] for i in range(4)], axis=0)
        cells = sum(dot(pool_x, term, NT) for term in split3(rows)) * (1.0 / 32.0)
        v = [cells[8 * i : 8 * i + 8] for i in range(4)]
        a = [jnp.where(far, v[i], pltpu.roll(v[i + 2], 64, 1)) for i in range(2)]
        b = [jnp.where(far, pltpu.roll(v[i], 64, 1), v[i + 2]) for i in range(2)]
        done = []
        for lo, hi in (a, b):
            done.append(jnp.where(near, lo, pltpu.roll(hi, 32, 1)))
            done.append(jnp.where(near, pltpu.roll(lo, 96, 1), hi))
        out_ref[pl.ds(32 * part, 32), :] = jnp.concatenate(done, axis=0).astype(BF)


def pool(emb):
    chunks = 2
    return pl.pallas_call(
        pool_kernel,
        in_specs=[pl.BlockSpec(memory_space=pl.ANY)],
        out_specs=[pl.BlockSpec(memory_space=pltpu.VMEM)] * 2,
        out_shape=[pltpu.VMEM((256, 128), BF), pltpu.VMEM((32, 256, 128), BF)],
        scratch_shapes=[
            pltpu.VMEM((32, 32, 128), F32),
            pltpu.SemaphoreType.DMA((chunks,)),
        ],
        compiler_params=pltpu.CompilerParams(vmem_limit_bytes=32 << 20),
        cost_estimate=pl.CostEstimate(flops=80_000_000, bytes_accessed=2_200_000, transcendentals=0),
        name="pool",
    )(pltpu.with_memory_space_constraint(emb, pltpu.HBM))


def banded(tap, taps):
    zero = jnp.zeros_like(taps(tap, 0))
    w = [taps(tap, k) if 0 <= k < 3 else zero for k in range(-1, 4)]
    return [jnp.concatenate([w[k + 1], w[k]], axis=1) for k in range(4)]


def prepare_kernel(edge_ref, w1_ref, w2_ref, order_ref, w1a_ref, w1b_ref, w2a_ref):
    i0, i1 = iota((128, 128), 0), iota((128, 128), 1)
    label = jnp.broadcast_to(edge_ref[...], (128, 128))
    owner = ((label >> 6) & 7).astype(F32)
    local = (label & 63).astype(F32)
    ahead = jnp.where((owner == owner.T) & (i0 < i1), 1.0, 0.0)
    place = owner[0:1, :] * 16.0 + jnp.sum(ahead, axis=0, keepdims=True)
    chosen = place == i0.astype(F32)
    face = jnp.sum(jnp.where(chosen, i1.astype(F32), 0.0), axis=1, keepdims=True)
    edge = jnp.sum(jnp.where(chosen, local, 0.0), axis=1, keepdims=True)
    order_ref[0] = jnp.broadcast_to(face, (128, 128))
    order_ref[1] = jnp.broadcast_to(edge, (128, 128))
    for tap in range(9):
        bands = banded(tap, lambda t, k: w1_ref[3 * t + k])
        w1a_ref[pl.ds(128 * tap, 128), :] = jnp.concatenate(bands, axis=0)
        w1b_ref[pl.ds(128 * tap, 128), :] = jnp.concatenate(bands[2:] + bands[:2], axis=0)
        bands = banded(tap, lambda t, k: w2_ref[3 * t + k].astype(F32).T.astype(BF))
        w2a_ref[pl.ds(256 * tap, 256), :] = jnp.concatenate(bands, axis=0)


def prepare(edge, w1, w2):
    return pl.pallas_call(
        prepare_kernel,
        in_specs=[pl.BlockSpec(memory_space=pltpu.VMEM)] * 3,
        out_specs=[pl.BlockSpec(memory_space=pltpu.VMEM)] * 4,
        out_shape=[
            pltpu.VMEM((2, 128, 128), F32),
            pltpu.VMEM((1152, 128), BF),
            pltpu.VMEM((1152, 128), BF),
            pltpu.VMEM((2304, 128), BF),
        ],
        compiler_params=pltpu.CompilerParams(vmem_limit_bytes=16 << 20),
        cost_estimate=pl.CostEstimate(flops=1_000_000_000, bytes_accessed=2_000_000, transcendentals=0),
        name="prepare",
    )(edge, w1, w2)


def face_kernel(half, emb_ref, slot_ref, order_ref, before_ref, cnt_ref, after_ref, wide, cells):
    wide[...] = emb_ref[:, pl.ds(128 * half, 128), :].astype(F32).reshape(4096, 128)
    faces = order_ref[0].astype(jnp.int32)
    pool_x8 = jnp.concatenate([pool_x_matrix()] * 8, axis=1)
    sums = jnp.zeros((32, 128), F32)
    count = jnp.zeros((8, 128), F32)
    for yc in range(16):
        voxels, member = [], []
        for q in (64 * zi + 4 * yc + yy for zi in range(2) for yy in range(4)):
            voxels.append(wide[pl.ds(q, 32, stride=128), :].astype(BF))
            row = jnp.broadcast_to(slot_ref[128 * half + q : 128 * half + q + 1, :], (128, 128))
            member.append(jnp.where(row == faces, 1.0, 0.0).astype(BF))
        left = jnp.concatenate([jnp.concatenate(voxels, axis=1), pool_x8], axis=0)
        out = dot(left, jnp.concatenate(member, axis=1), NT)
        sums = sums + out[:32]
        for x4 in range(4):
            part = out[32 + 8 * x4 : 40 + 8 * x4]
            cells[x4, 8 * yc : 8 * yc + 8, :] = part
            count = count + part
    for x4 in range(4):
        cnt_ref[x4 // 2, 128 * (x4 % 2) : 128 * (x4 % 2) + 128, :] = cells[x4].T.astype(BF)
    if half == 0:
        after_ref[0:32] = sums
        after_ref[32:40] = count
    else:
        sums = sums + before_ref[0:32]
        number = jnp.sum(count + before_ref[32:40], axis=0, keepdims=True)
        stacked = jnp.concatenate([jnp.zeros((64, 128), F32), sums, jnp.broadcast_to(number, (32, 128))], axis=0)
        after_ref[...] = jnp.where(iota((128, 128), 1) == 97, order_ref[1], stacked.T)


def faces(half, emb, slot, order, before):
    return pl.pallas_call(
        functools.partial(face_kernel, half),
        in_specs=[pl.BlockSpec(memory_space=pltpu.VMEM)] * 4,
        out_specs=[pl.BlockSpec(memory_space=pltpu.VMEM)] * 2,
        out_shape=[pltpu.VMEM((2, 256, 128), BF), pltpu.VMEM((128 if half else 40, 128), F32)],
        scratch_shapes=[pltpu.VMEM((4096, 128), F32), pltpu.VMEM((4, 128, 128), F32)],
        compiler_params=pltpu.CompilerParams(vmem_limit_bytes=16 << 20),
        cost_estimate=pl.CostEstimate(flops=2_000_000_000, bytes_accessed=4_000_000, transcendentals=0),
        name="faces",
    )(keep(emb), slot, keep(order), keep(before))


ROWS1 = 6 * 20 * 16
ROWS2 = 4 * 18 * 16
HEAD = 16


def ordered(even, a, b):
    return jnp.where(even, b, a), jnp.where(even, a, b)


def taps_dot(lefts, weights, depth):
    total = None
    per = 256 // depth
    for t in range(0, 9, per):
        group = lefts[t : t + per]
        left = group[0] if len(group) == 1 else jnp.concatenate(group, axis=1)
        term = dot(left, weights[pl.ds(depth * t, depth * len(group)), :])
        total = term if total is None else total + term
    return total


def inner_kernel(spot_ref, own_ref, za_ref, zb_ref, ya_ref, yb_ref, w1a_ref, w1b_ref, b1_ref, w2_ref, b2_ref, cnt0_ref,
                 cnt1_ref, fine_ref, sums_ref, ends_ref, near_ref, field, this, mixed, h0f, h1f, h0b, h0n, h1b):
    gz, gy = spot_ref[0], spot_ref[1]
    z_even, y_even = (gz & 1) == 0, (gy & 1) == 0
    z_low, z_high = ordered(z_even, za_ref[...].astype(F32), zb_ref[...].astype(F32))
    zs = (z_low, own_ref[...].astype(F32), z_high)
    ya, yb = ya_ref[...].astype(F32), yb_ref[...].astype(F32)
    ys = []
    for whole in ordered(y_even, ya, yb):
        low, high = ordered(z_even, whole[0:32], whole[64:96])
        ys.append((low, whole[32:64], high))
    for part in range(3):
        for i in range(2):
            plane = 2 * part + i
            base = HEAD + plane * 320
            for y in range(16):
                field[pl.ds(base + 32 + 16 * y, 8), :] = zs[part][128 * i + 8 * y : 128 * i + 8 * y + 8]
            for y in range(2):
                field[pl.ds(base + 16 * y, 8), :] = ys[0][part][16 * i + 8 * y : 16 * i + 8 * y + 8]
                field[pl.ds(base + 288 + 16 * y, 8), :] = ys[1][part][16 * i + 8 * y : 16 * i + 8 * y + 8]
            for k, g in enumerate((0, 7)):
                ends_ref[k, pl.ds(24 * plane, 20), :] = field[pl.ds(base + g, 20, stride=16), :]

    lane = iota((320, 128), 1)
    for z in range(6):
        now = field[pl.ds(HEAD + 320 * z, 320), :]
        before = field[pl.ds(HEAD + 320 * z - 1, 320), :]
        this[pl.ds(320 * z, 320), :] = now.astype(BF)
        mixed[pl.ds(320 * z, 320), :] = jnp.where(lane < 64, now, before).astype(BF)

    row = iota((288, 128), 0)
    stay = jnp.where((row < 16) & (gy == 0), 0.0, 1.0)
    stay = jnp.where((row >= 272) & (gy == 3), 0.0, stay)
    b1, b2 = b1_ref[...], b2_ref[...]

    def conv1(source, weights, z):
        lefts = [source[pl.ds(((z + tap // 3) * 20 + tap % 3) * 16, 288), :] for tap in range(9)]
        return jnp.maximum(taps_dot(lefts, weights, 128) + b1, 0.0)

    for z in range(4):
        inside = 1.0
        if z == 0:
            inside = jnp.where(gz == 0, 0.0, 1.0)
        if z == 3:
            inside = jnp.where(gz == 7, 0.0, 1.0)
        h0f[pl.ds(288 * z, 288), :] = conv1(mixed, w1b_ref, z) * (stay * inside)
        h1 = conv1(this, w1a_ref, z) * (stay * inside)
        h1f[pl.ds(288 * z, 288), :] = h1
        h1b[pl.ds(288 * z, 288), :] = h1.astype(BF)
        for k, g in enumerate((0, 7)):
            near_ref[k, pl.ds(24 * z, 18), :] = h1f[pl.ds(288 * z + g, 18, stride=16), :]
    for z in range(4):
        h0b[pl.ds(288 * z, 288), :] = h0f[pl.ds(288 * z, 288), :].astype(BF)
        h0n[pl.ds(288 * z, 288), :] = h0f[pl.ds(288 * z + 1, 288), :].astype(BF)

    group = iota((128, 128), 0) & 7
    sums = None
    for z in range(2):
        for p, (first, second) in enumerate(((h0b, h1b), (h1b, h0n))):
            at = [((z + tap // 3) * 18 + tap % 3) * 16 for tap in range(9)]
            lefts = [jnp.concatenate([first[pl.ds(r, 256), :], second[pl.ds(r, 256), :]], axis=1) for r in at]
            total = taps_dot(lefts, w2_ref, 256).reshape(16, 16, 128)[:, :8, :].reshape(128, 128)
            ctx = jnp.where(group == 7 * p, 0.0, total + b2).astype(BF)
            wide = ctx.astype(F32)
            fine_ref[pl.ds(512 * z + 2 * p, 128, stride=4), :] = wide
            fine_ref[pl.ds(512 * z + 2 * p + 1, 128, stride=4), :] = pltpu.roll(wide, 64, 1)
            term = dot((cnt0_ref, cnt1_ref)[z][p], ctx)
            sums = term if sums is None else sums + term
    sums_ref[...] = sums


def inner(spot, *arrays):
    return pl.pallas_call(
        inner_kernel,
        in_specs=[pl.BlockSpec(memory_space=pltpu.SMEM)] + [pl.BlockSpec(memory_space=pltpu.VMEM)] * len(arrays),
        out_specs=[pl.BlockSpec(memory_space=pltpu.VMEM)] * 4,
        out_shape=[
            pltpu.VMEM((1024, 128), F32),
            pltpu.VMEM((256, 128), F32),
            pltpu.VMEM((2, 144, 128), F32),
            pltpu.VMEM((2, 96, 128), F32),
        ],
        scratch_shapes=[
            pltpu.VMEM((HEAD + ROWS1, 128), F32),
            pltpu.VMEM((ROWS1, 128), BF),
            pltpu.VMEM((ROWS1, 128), BF),
            pltpu.VMEM((ROWS2 + 16, 128), F32),
            pltpu.VMEM((ROWS2, 128), F32),
            pltpu.VMEM((ROWS2, 128), BF),
            pltpu.VMEM((ROWS2, 128), BF),
            pltpu.VMEM((ROWS2, 128), BF),
        ],
        compiler_params=pltpu.CompilerParams(vmem_limit_bytes=16 << 20),
        cost_estimate=pl.CostEstimate(flops=3_000_000_000, bytes_accessed=3_000_000, transcendentals=0),
        name="inner",
    )(spot, *arrays)


def outer_kernel(spot_ref, xb_ref, xa_ref, ends_ref, near_ref, fine_ref, sums_ref, w1b_ref, b1_ref, w2_ref, b2_ref, cnt0_ref,
                 cnt1_ref, face_ref, ctx_ref, send_ref, column, hidden, patch, sparse):
    gz, gy, gx = spot_ref[0], spot_ref[1], spot_ref[2]
    z_even, y_even, x_even = (gz & 1) == 0, (gy & 1) == 0, (gx & 1) == 0
    lane = iota((24, 128), 1)
    column[...] = jnp.zeros_like(column)
    patch[...] = fine_ref[...]
    sparse[...] = jnp.zeros_like(sparse)
    for k, whole in enumerate(ordered(x_even, xa_ref[...].astype(F32), xb_ref[...].astype(F32))):
        low, high = ordered(z_even, whole[0:2], whole[4:6])
        for plane, rows in enumerate((low[0], low[1], whole[2], whole[3], high[0], high[1])):
            first, last = ordered(y_even, rows[16:18], rows[18:20])
            halo = jnp.concatenate([first, rows[0:16], last, jnp.zeros((4, 128), F32)], axis=0)
            own = ends_ref[k, pl.ds(24 * plane, 24), :]
            left, right = (own, halo) if k == 0 else (halo, own)
            column[k, pl.ds(24 * plane, 24), :] = jnp.where(lane < 64, left, right)

    row, lane = iota((96, 128), 0), iota((96, 128), 1)
    z_of = jnp.where(row < 24, 0, jnp.where(row < 48, 1, jnp.where(row < 72, 2, 3)))
    y_of = row - 24 * z_of
    gone = ((z_of == 0) & (gz == 0)) | ((z_of == 3) & (gz == 7)) | ((y_of == 0) & (gy == 0)) | ((y_of == 17) & (gy == 3))
    out0 = gone | ((lane < 64) & (gx == 0))
    out1 = gone | ((lane >= 64) & (gx == 7))
    at = [24 * (tap // 3) + tap % 3 for tap in range(9)]
    lefts = [jnp.concatenate([column[k, pl.ds(r, 96), :] for k in range(2)], axis=0).astype(BF) for r in at]
    total = jnp.maximum(taps_dot(lefts, w1b_ref, 128) + b1_ref[...], 0.0)
    hidden[0, 0:96] = jnp.where(out0, 0.0, total[0:96])
    hidden[1, 0:96] = near_ref[0]
    hidden[2, 0:96] = near_ref[1]
    hidden[3, 0:96] = jnp.where(out1, 0.0, total[96:192])

    lefts = []
    for r in at:
        h = [hidden[k, pl.ds(r, 40), :].astype(BF) for k in range(4)]
        h = [jnp.concatenate(h[2 * k : 2 * k + 2], axis=1) for k in range(2)]
        lefts.append(jnp.concatenate(h, axis=0))
    ctx = (taps_dot(lefts, w2_ref, 256) + b2_ref[...]).astype(BF).astype(F32)
    for k, (x, g) in enumerate(((0, 0), (30, 7))):
        for z in range(2):
            wide = ctx[40 * k + 24 * z : 40 * k + 24 * z + 16]
            patch[pl.ds(512 * z + x, 16, stride=32), :] = wide
            patch[pl.ds(512 * z + x + 1, 16, stride=32), :] = pltpu.roll(wide, 64, 1)
            sparse[pl.ds(128 * (2 * k + z) + g, 16, stride=8), :] = wide
    left = jnp.concatenate([cnt0_ref[0], cnt1_ref[0], cnt0_ref[1], cnt1_ref[1]], axis=1)
    sums = sums_ref[...] + dot(left, sparse[...].astype(BF))
    ctx_ref[...] = patch[...][:, :64].astype(BF)
    both = sums[:128] + pltpu.roll(sums[128:], 64, 1)
    send_ref[...] = jnp.where(iota((128, 128), 1) < 64, both, face_ref[...])


def outer(spot, *arrays):
    return pl.pallas_call(
        outer_kernel,
        in_specs=[pl.BlockSpec(memory_space=pltpu.SMEM)] + [pl.BlockSpec(memory_space=pltpu.VMEM)] * len(arrays),
        out_specs=[pl.BlockSpec(memory_space=pltpu.VMEM)] * 2,
        out_shape=[pltpu.VMEM((1024, 64), BF), pltpu.VMEM((128, 128), F32)],
        scratch_shapes=[
            pltpu.VMEM((2, 152, 128), F32),
            pltpu.VMEM((4, 96, 128), F32),
            pltpu.VMEM((1024, 128), F32),
            pltpu.VMEM((512, 128), F32),
        ],
        compiler_params=pltpu.CompilerParams(vmem_limit_bytes=16 << 20),
        cost_estimate=pl.CostEstimate(flops=200_000_000, bytes_accessed=3_000_000, transcendentals=0),
        name="outer",
    )(spot, *arrays)


def edge_kernel(rows_ref, ctx_ref, edge_emb_ref, edge_ctx_ref, out_ref, sent):
    copy = pltpu.make_async_copy(ctx_ref, out_ref, sent)
    copy.start()
    rows = rows_ref[...]
    hits = jnp.where(rows[:, 97:98] == iota((128, 64), 1).astype(F32), 1.0, 0.0).astype(BF)
    sums = sum(dot(part, hits) for part in split3(rows.T))
    scale = jnp.maximum(sums[96:97], 1.0)
    edge_ctx_ref[...] = sums[:64] / scale
    edge_emb_ref[...] = sums[64:96] / scale
    copy.wait()


def edges(rows, context):
    return pl.pallas_call(
        edge_kernel,
        in_specs=[pl.BlockSpec(memory_space=pltpu.VMEM)] * 2,
        out_specs=[pl.BlockSpec(memory_space=pltpu.VMEM)] * 2 + [pl.BlockSpec(memory_space=pl.ANY)],
        out_shape=[
            jax.ShapeDtypeStruct((32, 64), F32),
            jax.ShapeDtypeStruct((64, 64), F32),
            jax.ShapeDtypeStruct((1024, 64), BF),
        ],
        scratch_shapes=[pltpu.SemaphoreType.DMA],
        name="edges",
    )(rows, keep(context))


def pairs(first, count):
    return [pair for i in range(first, count - 1, 2) for pair in ((i, i + 1), (i + 1, i))]


def per_device(embedding, face_slot, face_edge, conv1_w, conv1_b, conv2_w, conv2_b):
    emb = embedding.reshape(32, 256, 128)
    gz, gy, gx = (lax.axis_index(a) for a in ("gz", "gy", "gx"))
    slot = face_slot.reshape(256, 128)
    own, voxels = pool(emb)
    zb = lax.ppermute(own, "gz", pairs(1, 8))
    za = lax.ppermute(own, "gz", pairs(0, 8))
    order, w1a, w1b, w2a = prepare(
        face_edge.reshape(1, 128),
        jnp.swapaxes(conv1_w, 3, 4).reshape(27, 32, 64),
        conv2_w.reshape(27, 64, 64),
    )
    za, zb, order = lax.optimization_barrier((za, zb, order))
    planes = [a.reshape(2, 16, 8, 128) for a in (za, own, zb)]
    y_even, x_even = (gy & 1) == 0, (gx & 1) == 0

    def y_edge(high):
        first = jnp.where(high, 14, 0)
        return jnp.concatenate([lax.dynamic_slice_in_dim(a, first, 2, axis=1) for a in planes], axis=0)

    yb = lax.ppermute(y_edge(jnp.logical_not(y_even)), "gy", pairs(1, 4))
    ya = lax.ppermute(y_edge(y_even), "gy", pairs(0, 4))
    cnt0, half = faces(0, voxels, slot, order, order[0, :40])
    ya, yb, half = lax.optimization_barrier((ya, yb, half))

    def x_edge(g):
        mid = jnp.concatenate([a[:, :, g] for a in planes], axis=0)
        return jnp.concatenate([mid, ya[:, :, g], yb[:, :, g]], axis=1)

    low, high = x_edge(0), x_edge(7)
    to_b, half, x_even = lax.optimization_barrier((jnp.where(x_even, low, high), half, x_even))
    xb = lax.ppermute(to_b, "gx", pairs(1, 8))
    to_a, half = lax.optimization_barrier((jnp.where(x_even, high, low), half))
    xa = lax.ppermute(to_a, "gx", pairs(0, 8))
    cnt1, face = faces(1, voxels, slot, order, half)
    spot = jnp.stack([gz, gy, gx]).astype(jnp.int32)
    twice = lambda b: jnp.concatenate([b, b]).reshape(1, 128)
    b1, b2 = twice(conv1_b), twice(conv2_b)
    w1a, w1b, w2a, cnt0, cnt1 = (keep(a) for a in (w1a, w1b, w2a, cnt0, cnt1))
    fine, sums, ends, near = inner(
        spot, own, za, zb, ya.reshape(96, 128), yb.reshape(96, 128), w1a, w1b, b1, w2a, b2, cnt0, cnt1
    )
    context, send = outer(
        spot, xb, xa, keep(ends), keep(near), keep(fine), keep(sums), w1b, b1, w2a, b2, cnt0, cnt1, keep(face)
    )
    rows = lax.all_to_all(send, "gx", 0, 0, tiled=True)
    edge_emb, edge_ctx, context = edges(rows, context)
    context = jnp.transpose(context.reshape(2, 16, 32, 64), (3, 0, 1, 2))
    return (context, edge_emb, edge_ctx)


def solution(mesh):
    in_specs = (P(None, "gz", "gy", "gx"), P("gz", "gy", "gx"), P(("gz", "gy", "gx")), P(), P(), P(), P())
    out_specs = (P(None, "gz", "gy", "gx"), P(None, ("gz", "gy", "gx")), P(None, ("gz", "gy", "gx")))
    return jax.shard_map(per_device, mesh=mesh, in_specs=in_specs, out_specs=out_specs, check_vma=False)
```

```python
import functools

import jax
import jax.numpy as jnp
from jax import lax
from jax.experimental import pallas as pl
from jax.experimental.pallas import tpu as pltpu
from jax.sharding import PartitionSpec as P

BF = jnp.bfloat16
F32 = jnp.float32
NT = (((1,), (1,)), ((), ()))
NN = (((1,), (0,)), ((), ()))


def dot(a, b, dims=NN):
    return lax.dot_general(a, b, dims, preferred_element_type=F32)


def keep(array):
    return pltpu.with_memory_space_constraint(array, pltpu.VMEM)


def iota(shape, dim):
    return lax.broadcasted_iota(jnp.int32, shape, dim)


def split3(x):
    hi = x.astype(BF)
    rest = x - hi.astype(F32)
    mid = rest.astype(BF)
    low = (rest - mid.astype(F32)).astype(BF)
    return hi, mid, low


def pool_x_matrix():
    row, col = iota((32, 128), 0), iota((32, 128), 1)
    cell = 4 * (row & 7) + (row >> 3)
    return jnp.where((col >> 2) == cell, 1.0, 0.0).astype(BF)


def pool_kernel(emb_ref, out_ref, block, sums, arrived):
    chunks = arrived.shape[0]
    per = 32 // chunks
    copies = [
        pltpu.make_async_copy(emb_ref.at[pl.ds(per * i, per)], block.at[pl.ds(per * i, per)], arrived.at[i])
        for i in range(chunks)
    ]
    for copy in copies:
        copy.start()
    row, col = iota((32, 256), 0), iota((32, 256), 1)
    cell = ((col >> 7) << 4) + ((col & 63) >> 2)
    pool_zy = jnp.where(cell == row, 1.0, 0.0).astype(BF)
    pool_x = jnp.concatenate([pool_x_matrix()] * 3, axis=1)
    lane = iota((8, 128), 1)
    far, near = lane < 64, (lane & 32) == 0
    for i in range(chunks):
        copies[i].wait()
        for c in range(per * i, per * i + per):
            sums[pl.ds(32 * c, 32), :] = dot(pool_zy, block[c])
    for part in range(8):
        rows = jnp.concatenate([sums[pl.ds(4 * part + i, 32, stride=32), :] for i in range(4)], axis=0)
        cells = dot(pool_x, jnp.concatenate(split3(rows), axis=1), NT) * (1.0 / 32.0)
        v = [cells[8 * i : 8 * i + 8] for i in range(4)]
        a = [jnp.where(far, v[i], pltpu.roll(v[i + 2], 64, 1)) for i in range(2)]
        b = [jnp.where(far, pltpu.roll(v[i], 64, 1), v[i + 2]) for i in range(2)]
        done = []
        for lo, hi in (a, b):
            done.append(jnp.where(near, lo, pltpu.roll(hi, 32, 1)))
            done.append(jnp.where(near, pltpu.roll(lo, 96, 1), hi))
        out_ref[pl.ds(32 * part, 32), :] = jnp.concatenate(done, axis=0).astype(BF)


def pool(emb):
    chunks = 2
    return pl.pallas_call(
        pool_kernel,
        in_specs=[pl.BlockSpec(memory_space=pl.ANY)],
        out_specs=[pl.BlockSpec(memory_space=pltpu.VMEM)] * 2,
        out_shape=[pltpu.VMEM((256, 128), BF), pltpu.VMEM((32, 256, 128), BF)],
        scratch_shapes=[
            pltpu.VMEM((1024, 128), F32),
            pltpu.SemaphoreType.DMA((chunks,)),
        ],
        compiler_params=pltpu.CompilerParams(vmem_limit_bytes=32 << 20),
        cost_estimate=pl.CostEstimate(flops=80_000_000, bytes_accessed=2_200_000, transcendentals=0),
        name="pool",
    )(pltpu.with_memory_space_constraint(emb, pltpu.HBM))


def banded(tap, taps):
    zero = jnp.zeros_like(taps(tap, 0))
    w = [taps(tap, k) if 0 <= k < 3 else zero for k in range(-1, 4)]
    return [jnp.concatenate([w[k + 1], w[k]], axis=1) for k in range(4)]


def prepare_kernel(edge_ref, w1_ref, w2_ref, order_ref, w1a_ref, w1b_ref, w2a_ref):
    i0, i1 = iota((128, 128), 0), iota((128, 128), 1)
    label = jnp.broadcast_to(edge_ref[...], (128, 128))
    owner = ((label >> 6) & 7).astype(F32)
    local = (label & 63).astype(F32)
    ahead = jnp.where((owner == owner.T) & (i0 < i1), 1.0, 0.0)
    place = owner[0:1, :] * 16.0 + jnp.sum(ahead, axis=0, keepdims=True)
    chosen = place == i0.astype(F32)
    face = jnp.sum(jnp.where(chosen, i1.astype(F32), 0.0), axis=1, keepdims=True)
    edge = jnp.sum(jnp.where(chosen, local, 0.0), axis=1, keepdims=True)
    order_ref[0] = jnp.broadcast_to(face, (128, 128))
    order_ref[1] = jnp.broadcast_to(edge, (128, 128))
    for tap in range(9):
        bands = banded(tap, lambda t, k: w1_ref[3 * t + k])
        w1a_ref[pl.ds(128 * tap, 128), :] = jnp.concatenate(bands, axis=0)
        w1b_ref[pl.ds(128 * tap, 128), :] = jnp.concatenate(bands[2:] + bands[:2], axis=0)
        bands = banded(tap, lambda t, k: w2_ref[3 * t + k].astype(F32).T.astype(BF))
        w2a_ref[pl.ds(256 * tap, 256), :] = jnp.concatenate(bands, axis=0)


def prepare(edge, w1, w2):
    return pl.pallas_call(
        prepare_kernel,
        in_specs=[pl.BlockSpec(memory_space=pltpu.VMEM)] * 3,
        out_specs=[pl.BlockSpec(memory_space=pltpu.VMEM)] * 4,
        out_shape=[
            pltpu.VMEM((2, 128, 128), F32),
            pltpu.VMEM((1152, 128), BF),
            pltpu.VMEM((1152, 128), BF),
            pltpu.VMEM((2304, 128), BF),
        ],
        compiler_params=pltpu.CompilerParams(vmem_limit_bytes=16 << 20),
        cost_estimate=pl.CostEstimate(flops=1_000_000, bytes_accessed=10_000, transcendentals=0),
        name="prepare",
    )(edge, w1, w2)


def face_kernel(half, emb_ref, slot_ref, order_ref, before_ref, cnt_ref, after_ref, wide, cells):
    wide[...] = emb_ref[:, pl.ds(128 * half, 128), :].astype(F32).reshape(4096, 128)
    faces = order_ref[0].astype(jnp.int32)
    pool_x8 = jnp.concatenate([pool_x_matrix()] * 8, axis=1)
    sums = jnp.zeros((32, 128), F32)
    count = jnp.zeros((8, 128), F32)
    for yc in range(16):
        voxels, member = [], []
        for q in (64 * zi + 4 * yc + yy for zi in range(2) for yy in range(4)):
            voxels.append(wide[pl.ds(q, 32, stride=128), :].astype(BF))
            row = jnp.broadcast_to(slot_ref[128 * half + q : 128 * half + q + 1, :], (128, 128))
            member.append(jnp.where(row == faces, 1.0, 0.0).astype(BF))
        left = jnp.concatenate([jnp.concatenate(voxels, axis=1), pool_x8], axis=0)
        out = dot(left, jnp.concatenate(member, axis=1), NT)
        sums = sums + out[:32]
        for x4 in range(4):
            part = out[32 + 8 * x4 : 40 + 8 * x4]
            cells[x4, 8 * yc : 8 * yc + 8, :] = part
            count = count + part
    for x4 in range(4):
        cnt_ref[x4 // 2, 128 * (x4 % 2) : 128 * (x4 % 2) + 128, :] = cells[x4].T.astype(BF)
    if half == 0:
        after_ref[0:32] = sums
        after_ref[32:40] = count
    else:
        sums = sums + before_ref[0:32]
        number = jnp.sum(count + before_ref[32:40], axis=0, keepdims=True)
        stacked = jnp.concatenate([jnp.zeros((64, 128), F32), sums, jnp.broadcast_to(number, (32, 128))], axis=0)
        after_ref[...] = jnp.where(iota((128, 128), 1) == 97, order_ref[1], stacked.T)


def faces(half, emb, slot, order, before):
    return pl.pallas_call(
        functools.partial(face_kernel, half),
        in_specs=[pl.BlockSpec(memory_space=pltpu.VMEM)] * 4,
        out_specs=[pl.BlockSpec(memory_space=pltpu.VMEM)] * 2,
        out_shape=[pltpu.VMEM((2, 256, 128), BF), pltpu.VMEM((128 if half else 40, 128), F32)],
        scratch_shapes=[pltpu.VMEM((4096, 128), F32), pltpu.VMEM((4, 128, 128), F32)],
        compiler_params=pltpu.CompilerParams(vmem_limit_bytes=16 << 20),
        cost_estimate=pl.CostEstimate(flops=1_000_000, bytes_accessed=10_000, transcendentals=0),
        name="faces",
    )(keep(emb), slot, keep(order), keep(before))


ROWS1 = 6 * 20 * 8
ROWS2 = 4 * 18 * 8
HEAD = 8


def ordered(even, a, b):
    return jnp.where(even, b, a), jnp.where(even, a, b)


def taps_dot(lefts, weights, depth):
    total = None
    per = 256 // depth
    for t in range(0, 9, per):
        group = lefts[t : t + per]
        left = group[0] if len(group) == 1 else jnp.concatenate(group, axis=1)
        term = dot(left, weights[pl.ds(depth * t, depth * len(group)), :])
        total = term if total is None else total + term
    return total


def window(source, tap, z, plane, rows):
    return source[tap % 3 & 1, pl.ds((z + tap // 3) * plane + 16 * (tap % 3 >> 1), rows), :]


def inner_kernel(own_ref, za_ref, zb_ref, ya_ref, yb_ref, w1a_ref, w1b_ref, b1_ref, w2_ref, b2_ref, cnt0_ref,
                 cnt1_ref, fine_ref, sums_ref, ends_ref, near_ref, field, this, mixed, h0f, h1f, h0b, h0n, h1b):
    gz, gy = lax.axis_index("gz"), lax.axis_index("gy")
    z_even, y_even = (gz & 1) == 0, (gy & 1) == 0
    z_low, z_high = ordered(z_even, za_ref[...].astype(F32), zb_ref[...].astype(F32))
    zs = (z_low, own_ref[...].astype(F32), z_high)
    ya, yb = ya_ref[...].astype(F32), yb_ref[...].astype(F32)
    ys = []
    for whole in ordered(y_even, ya, yb):
        low, high = ordered(z_even, whole[0:32], whole[64:96])
        ys.append((low, whole[32:64], high))
    for plane in range(6):
        part, i = plane // 2, plane % 2
        base = HEAD + plane * 160
        field[pl.ds(base, 16), :] = ys[0][part][16 * i : 16 * i + 16]
        field[pl.ds(base + 16, 128), :] = zs[part][128 * i : 128 * i + 128]
        field[pl.ds(base + 144, 16), :] = ys[1][part][16 * i : 16 * i + 16]
        for k, g in enumerate((0, 7)):
            ends_ref[k, pl.ds(24 * plane, 20), :] = field[pl.ds(base + g, 20, stride=8), :]

    lane = iota((160, 128), 1)
    for z in range(6):
        for shift in range(2):
            now = field[pl.ds(HEAD + 160 * z + 8 * shift, 160), :]
            before = field[pl.ds(HEAD + 160 * z + 8 * shift - 1, 160), :]
            this[shift, pl.ds(160 * z, 160), :] = now.astype(BF)
            mixed[shift, pl.ds(160 * z, 160), :] = jnp.where(lane < 64, now, before).astype(BF)

    row = iota((144, 128), 0)
    stay = jnp.where((row < 8) & (gy == 0), 0.0, 1.0)
    stay = jnp.where((row >= 136) & (gy == 3), 0.0, stay)
    b1, b2 = b1_ref[...], b2_ref[...]

    def conv1(source, weights, z):
        lefts = [window(source, tap, z, 160, 144) for tap in range(9)]
        return jnp.maximum(taps_dot(lefts, weights, 128) + b1, 0.0)

    for z in range(4):
        inside = 1.0
        if z == 0:
            inside = jnp.where(gz == 0, 0.0, 1.0)
        if z == 3:
            inside = jnp.where(gz == 7, 0.0, 1.0)
        h0f[pl.ds(144 * z, 144), :] = conv1(mixed, w1b_ref, z) * (stay * inside)
        h1f[pl.ds(144 * z, 144), :] = conv1(this, w1a_ref, z) * (stay * inside)
    for z in range(4):
        for k, g in enumerate((0, 7)):
            near_ref[k, pl.ds(24 * z, 18), :] = h1f[pl.ds(144 * z + g, 18, stride=8), :]
        for shift in range(2):
            at = 144 * z + 8 * shift
            h0b[shift, pl.ds(144 * z, 144), :] = h0f[pl.ds(at, 144), :].astype(BF)
            h0n[shift, pl.ds(144 * z, 144), :] = h0f[pl.ds(at + 1, 144), :].astype(BF)
            h1b[shift, pl.ds(144 * z, 144), :] = h1f[pl.ds(at, 144), :].astype(BF)

    group = iota((128, 128), 0) & 7
    sums = None
    for z in range(2):
        lefts = []
        for tap in range(9):
            h = [window(source, tap, z, 144, 128) for source in (h0b, h1b, h0n)]
            lefts.append(jnp.concatenate([jnp.concatenate(h[p : p + 2], axis=1) for p in range(2)], axis=0))
        both = taps_dot(lefts, w2_ref, 256) + b2
        for p in range(2):
            ctx = jnp.where(group == 7 * p, 0.0, both[128 * p : 128 * p + 128]).astype(BF)
            wide = ctx.astype(F32)
            fine_ref[pl.ds(512 * z + 2 * p, 128, stride=4), :] = wide
            fine_ref[pl.ds(512 * z + 2 * p + 1, 128, stride=4), :] = pltpu.roll(wide, 64, 1)
            term = dot((cnt0_ref, cnt1_ref)[z][p], ctx)
            sums = term if sums is None else sums + term
    sums_ref[...] = sums


def inner(*arrays):
    return pl.pallas_call(
        inner_kernel,
        in_specs=[pl.BlockSpec(memory_space=pltpu.VMEM)] * len(arrays),
        out_specs=[pl.BlockSpec(memory_space=pltpu.VMEM)] * 4,
        out_shape=[
            pltpu.VMEM((1024, 128), F32),
            pltpu.VMEM((256, 128), F32),
            pltpu.VMEM((2, 144, 128), F32),
            pltpu.VMEM((2, 96, 128), F32),
        ],
        scratch_shapes=[
            pltpu.VMEM((HEAD + ROWS1 + 8, 128), F32),
            pltpu.VMEM((2, ROWS1, 128), BF),
            pltpu.VMEM((2, ROWS1, 128), BF),
            pltpu.VMEM((ROWS2 + 16, 128), F32),
            pltpu.VMEM((ROWS2 + 16, 128), F32),
            pltpu.VMEM((2, ROWS2, 128), BF),
            pltpu.VMEM((2, ROWS2, 128), BF),
            pltpu.VMEM((2, ROWS2, 128), BF),
        ],
        compiler_params=pltpu.CompilerParams(vmem_limit_bytes=16 << 20),
        cost_estimate=pl.CostEstimate(flops=1_000_000, bytes_accessed=10_000, transcendentals=0),
        name="inner",
    )(*arrays)


def outer_kernel(xb_ref, xa_ref, ends_ref, near_ref, fine_ref, sums_ref, w1b_ref, b1_ref, w2_ref, b2_ref, cnt0_ref,
                 cnt1_ref, face_ref, ctx_ref, send_ref, column, hidden, patch, sparse):
    gz, gy, gx = (lax.axis_index(a) for a in ("gz", "gy", "gx"))
    z_even, y_even, x_even = (gz & 1) == 0, (gy & 1) == 0, (gx & 1) == 0
    lane = iota((24, 128), 1)
    column[...] = jnp.zeros_like(column)
    patch[...] = fine_ref[...]
    sparse[...] = jnp.zeros_like(sparse)
    for k, whole in enumerate(ordered(x_even, xa_ref[...].astype(F32), xb_ref[...].astype(F32))):
        low, high = ordered(z_even, whole[0:2], whole[4:6])
        for plane, rows in enumerate((low[0], low[1], whole[2], whole[3], high[0], high[1])):
            first, last = ordered(y_even, rows[16:18], rows[18:20])
            halo = jnp.concatenate([first, rows[0:16], last, jnp.zeros((4, 128), F32)], axis=0)
            own = ends_ref[k, pl.ds(24 * plane, 24), :]
            left, right = (own, halo) if k == 0 else (halo, own)
            column[k, pl.ds(24 * plane, 24), :] = jnp.where(lane < 64, left, right)

    row, lane = iota((96, 128), 0), iota((96, 128), 1)
    z_of = jnp.where(row < 24, 0, jnp.where(row < 48, 1, jnp.where(row < 72, 2, 3)))
    y_of = row - 24 * z_of
    gone = ((z_of == 0) & (gz == 0)) | ((z_of == 3) & (gz == 7)) | ((y_of == 0) & (gy == 0)) | ((y_of == 17) & (gy == 3))
    out0 = gone | ((lane < 64) & (gx == 0))
    out1 = gone | ((lane >= 64) & (gx == 7))
    at = [24 * (tap // 3) + tap % 3 for tap in range(9)]
    lefts = [jnp.concatenate([column[k, pl.ds(r, 96), :] for k in range(2)], axis=0).astype(BF) for r in at]
    total = jnp.maximum(taps_dot(lefts, w1b_ref, 128) + b1_ref[...], 0.0)
    hidden[0, 0:96] = jnp.where(out0, 0.0, total[0:96])
    hidden[1, 0:96] = near_ref[0]
    hidden[2, 0:96] = near_ref[1]
    hidden[3, 0:96] = jnp.where(out1, 0.0, total[96:192])

    lefts = []
    for r in at:
        h = [hidden[k, pl.ds(r, 40), :].astype(BF) for k in range(4)]
        h = [jnp.concatenate(h[2 * k : 2 * k + 2], axis=1) for k in range(2)]
        lefts.append(jnp.concatenate(h, axis=0))
    ctx = (taps_dot(lefts, w2_ref, 256) + b2_ref[...]).astype(BF).astype(F32)
    for k, (x, g) in enumerate(((0, 0), (30, 7))):
        for z in range(2):
            wide = ctx[40 * k + 24 * z : 40 * k + 24 * z + 16]
            patch[pl.ds(512 * z + x, 16, stride=32), :] = wide
            patch[pl.ds(512 * z + x + 1, 16, stride=32), :] = pltpu.roll(wide, 64, 1)
            sparse[pl.ds(128 * (2 * k + z) + g, 16, stride=8), :] = wide
    left = jnp.concatenate([cnt0_ref[0], cnt1_ref[0], cnt0_ref[1], cnt1_ref[1]], axis=1)
    sums = sums_ref[...] + dot(left, sparse[...].astype(BF))
    ctx_ref[...] = patch[...][:, :64].astype(BF)
    both = sums[:128] + pltpu.roll(sums[128:], 64, 1)
    send_ref[...] = jnp.where(iota((128, 128), 1) < 64, both, face_ref[...])


def outer(*arrays):
    return pl.pallas_call(
        outer_kernel,
        in_specs=[pl.BlockSpec(memory_space=pltpu.VMEM)] * len(arrays),
        out_specs=[pl.BlockSpec(memory_space=pltpu.VMEM)] * 2,
        out_shape=[pltpu.VMEM((1024, 64), BF), pltpu.VMEM((128, 128), F32)],
        scratch_shapes=[
            pltpu.VMEM((2, 152, 128), F32),
            pltpu.VMEM((4, 96, 128), F32),
            pltpu.VMEM((1024, 128), F32),
            pltpu.VMEM((512, 128), F32),
        ],
        compiler_params=pltpu.CompilerParams(vmem_limit_bytes=16 << 20),
        cost_estimate=pl.CostEstimate(flops=200_000_000, bytes_accessed=3_000_000, transcendentals=0),
        name="outer",
    )(*arrays)


def edge_kernel(rows_ref, ctx_ref, edge_emb_ref, edge_ctx_ref, out_ref, sent):
    copy = pltpu.make_async_copy(ctx_ref, out_ref, sent)
    copy.start()
    rows = rows_ref[...]
    hits = jnp.where(rows[:, 97:98] == iota((128, 64), 1).astype(F32), 1.0, 0.0).astype(BF)
    sums = sum(dot(part, hits) for part in split3(rows.T))
    scale = jnp.maximum(sums[96:97], 1.0)
    edge_ctx_ref[...] = sums[:64] / scale
    edge_emb_ref[...] = sums[64:96] / scale
    copy.wait()


def edges(rows, context):
    return pl.pallas_call(
        edge_kernel,
        in_specs=[pl.BlockSpec(memory_space=pltpu.VMEM)] * 2,
        out_specs=[pl.BlockSpec(memory_space=pltpu.VMEM)] * 2 + [pl.BlockSpec(memory_space=pl.ANY)],
        out_shape=[
            jax.ShapeDtypeStruct((32, 64), F32),
            jax.ShapeDtypeStruct((64, 64), F32),
            jax.ShapeDtypeStruct((1024, 64), BF),
        ],
        scratch_shapes=[pltpu.SemaphoreType.DMA],
        name="edges",
    )(keep(rows), keep(context))


def pairs(first, count):
    return [pair for i in range(first, count - 1, 2) for pair in ((i, i + 1), (i + 1, i))]


def per_device(embedding, face_slot, face_edge, conv1_w, conv1_b, conv2_w, conv2_b):
    emb = embedding.reshape(32, 256, 128)
    gy, gx = lax.axis_index("gy"), lax.axis_index("gx")
    slot = face_slot.reshape(256, 128)
    own, voxels = pool(emb)
    zb = lax.ppermute(own, "gz", pairs(1, 8))
    za = lax.ppermute(own, "gz", pairs(0, 8))
    order, w1a, w1b, w2a = prepare(
        face_edge.reshape(1, 128),
        jnp.swapaxes(conv1_w, 3, 4).reshape(27, 32, 64),
        conv2_w.reshape(27, 64, 64),
    )
    za, zb, order = lax.optimization_barrier((za, zb, order))
    planes = [a.reshape(2, 16, 8, 128) for a in (za, own, zb)]
    y_even, x_even = (gy & 1) == 0, (gx & 1) == 0

    def y_edge(high):
        first = jnp.where(high, 14, 0)
        return jnp.concatenate([lax.dynamic_slice_in_dim(a, first, 2, axis=1) for a in planes], axis=0)

    to_a, to_b = lax.optimization_barrier((y_edge(y_even), y_edge(jnp.logical_not(y_even))))
    ya = lax.ppermute(to_a, "gy", pairs(0, 4))
    yb = lax.ppermute(to_b, "gy", pairs(1, 4))
    cnt0, half = faces(0, voxels, slot, order, order[0, :40])
    ya, yb, half = lax.optimization_barrier((ya, yb, half))

    def x_edge(g):
        mid = jnp.concatenate([a[:, :, g] for a in planes], axis=0)
        return jnp.concatenate([mid, ya[:, :, g], yb[:, :, g]], axis=1)

    low, high = x_edge(0), x_edge(7)
    to_b, to_a, half = lax.optimization_barrier((jnp.where(x_even, low, high), jnp.where(x_even, high, low), half))
    xa = lax.ppermute(to_a, "gx", pairs(0, 8))
    xb = lax.ppermute(to_b, "gx", pairs(1, 8))
    cnt1, face = faces(1, voxels, slot, order, half)
    twice = lambda b: jnp.concatenate([b, b]).reshape(1, 128)
    b1, b2 = twice(conv1_b), twice(conv2_b)
    w1a, w1b, w2a, cnt0, cnt1 = (keep(a) for a in (w1a, w1b, w2a, cnt0, cnt1))
    fine, sums, ends, near = inner(
        own, za, zb, ya.reshape(96, 128), yb.reshape(96, 128), w1a, w1b, b1, w2a, b2, cnt0, cnt1
    )
    context, send = outer(
        xb, xa, keep(ends), keep(near), keep(fine), keep(sums), w1b, b1, w2a, b2, cnt0, cnt1, keep(face)
    )
    rows = lax.all_to_all(send, "gx", 0, 0, tiled=True)
    edge_emb, edge_ctx, context = edges(rows, context)
    context = jnp.transpose(context.reshape(2, 16, 32, 64), (3, 0, 1, 2))
    return (context, edge_emb, edge_ctx)


def solution(mesh):
    in_specs = (P(None, "gz", "gy", "gx"), P("gz", "gy", "gx"), P(("gz", "gy", "gx")), P(), P(), P(), P())
    out_specs = (P(None, "gz", "gy", "gx"), P(None, ("gz", "gy", "gx")), P(None, ("gz", "gy", "gx")))
    return jax.shard_map(per_device, mesh=mesh, in_specs=in_specs, out_specs=out_specs, check_vma=False)
```

```python
import functools

import jax
import jax.numpy as jnp
from jax import lax
from jax.experimental import pallas as pl
from jax.experimental.pallas import tpu as pltpu
from jax.sharding import PartitionSpec as P

BF = jnp.bfloat16
F32 = jnp.float32
NT = (((1,), (1,)), ((), ()))
NN = (((1,), (0,)), ((), ()))


def dot(a, b, dims=NN):
    return lax.dot_general(a, b, dims, preferred_element_type=F32)


def keep(array):
    return pltpu.with_memory_space_constraint(array, pltpu.VMEM)


def iota(shape, dim):
    return lax.broadcasted_iota(jnp.int32, shape, dim)


def split3(x):
    hi = x.astype(BF)
    rest = x - hi.astype(F32)
    mid = rest.astype(BF)
    low = (rest - mid.astype(F32)).astype(BF)
    return hi, mid, low


def pool_x_matrix():
    row, col = iota((32, 128), 0), iota((32, 128), 1)
    cell = 4 * (row & 7) + (row >> 3)
    return jnp.where((col >> 2) == cell, 1.0, 0.0).astype(BF)


def pool_kernel(emb_ref, out_ref, block, sums, arrived):
    chunks = arrived.shape[0]
    per = 32 // chunks
    copies = [
        pltpu.make_async_copy(emb_ref.at[pl.ds(per * i, per)], block.at[pl.ds(per * i, per)], arrived.at[i])
        for i in range(chunks)
    ]
    for copy in copies:
        copy.start()
    row, col = iota((32, 256), 0), iota((32, 256), 1)
    cell = ((col >> 7) << 4) + ((col & 63) >> 2)
    pool_zy = jnp.where(cell == row, 1.0, 0.0).astype(BF)
    pool_x = jnp.concatenate([pool_x_matrix()] * 3, axis=1)
    lane = iota((8, 128), 1)
    far, near = lane < 64, (lane & 32) == 0
    for i in range(chunks):
        copies[i].wait()
        for c in range(per * i, per * i + per):
            sums[pl.ds(32 * c, 32), :] = dot(pool_zy, block[c])
    for part in range(8):
        rows = jnp.concatenate([sums[pl.ds(4 * part + i, 32, stride=32), :] for i in range(4)], axis=0)
        cells = dot(pool_x, jnp.concatenate(split3(rows), axis=1), NT) * (1.0 / 32.0)
        v = [cells[8 * i : 8 * i + 8] for i in range(4)]
        a = [jnp.where(far, v[i], pltpu.roll(v[i + 2], 64, 1)) for i in range(2)]
        b = [jnp.where(far, pltpu.roll(v[i], 64, 1), v[i + 2]) for i in range(2)]
        done = []
        for lo, hi in (a, b):
            done.append(jnp.where(near, lo, pltpu.roll(hi, 32, 1)))
            done.append(jnp.where(near, pltpu.roll(lo, 96, 1), hi))
        out_ref[pl.ds(32 * part, 32), :] = jnp.concatenate(done, axis=0).astype(BF)


def pool(emb):
    chunks = 2
    return pl.pallas_call(
        pool_kernel,
        in_specs=[pl.BlockSpec(memory_space=pl.ANY)],
        out_specs=[pl.BlockSpec(memory_space=pltpu.VMEM)] * 2,
        out_shape=[pltpu.VMEM((256, 128), BF), pltpu.VMEM((32, 256, 128), BF)],
        scratch_shapes=[
            pltpu.VMEM((1024, 128), F32),
            pltpu.SemaphoreType.DMA((chunks,)),
        ],
        compiler_params=pltpu.CompilerParams(vmem_limit_bytes=32 << 20),
        cost_estimate=pl.CostEstimate(flops=80_000_000, bytes_accessed=2_200_000, transcendentals=0),
        name="pool",
    )(pltpu.with_memory_space_constraint(emb, pltpu.HBM))


def banded(tap, taps):
    zero = jnp.zeros_like(taps(tap, 0))
    w = [taps(tap, k) if 0 <= k < 3 else zero for k in range(-1, 4)]
    return [jnp.concatenate([w[k + 1], w[k]], axis=1) for k in range(4)]


def bands_kernel(w1_ref, w2_ref, w1a_ref, w1b_ref, w2a_ref):
    for tap in range(9):
        bands = banded(tap, lambda t, k: w1_ref[3 * t + k])
        w1a_ref[pl.ds(128 * tap, 128), :] = jnp.concatenate(bands, axis=0)
        w1b_ref[pl.ds(128 * tap, 128), :] = jnp.concatenate(bands[2:] + bands[:2], axis=0)
        bands = banded(tap, lambda t, k: w2_ref[3 * t + k].astype(F32).T.astype(BF))
        w2a_ref[pl.ds(256 * tap, 256), :] = jnp.concatenate(bands, axis=0)


def bands(w1, w2):
    return pl.pallas_call(
        bands_kernel,
        in_specs=[pl.BlockSpec(memory_space=pltpu.VMEM)] * 2,
        out_specs=[pl.BlockSpec(memory_space=pltpu.VMEM)] * 3,
        out_shape=[pltpu.VMEM((1152, 128), BF), pltpu.VMEM((1152, 128), BF), pltpu.VMEM((2304, 128), BF)],
        compiler_params=pltpu.CompilerParams(vmem_limit_bytes=16 << 20),
        cost_estimate=pl.CostEstimate(flops=1_000_000, bytes_accessed=10_000, transcendentals=0),
        name="bands",
    )(w1, w2)


def ordering(edge):
    i0, i1 = iota((128, 128), 0), iota((128, 128), 1)
    label = jnp.broadcast_to(edge, (128, 128))
    owner = ((label >> 6) & 7).astype(F32)
    local = (label & 63).astype(F32)
    ahead = jnp.where((owner == owner.T) & (i0 < i1), 1.0, 0.0)
    place = owner[0:1, :] * 16.0 + jnp.sum(ahead, axis=0, keepdims=True)
    chosen = place == i0.astype(F32)
    face = jnp.sum(jnp.where(chosen, i1.astype(F32), 0.0), axis=1, keepdims=True)
    edge = jnp.sum(jnp.where(chosen, local, 0.0), axis=1, keepdims=True)
    return jnp.broadcast_to(face, (128, 128)), jnp.broadcast_to(edge, (128, 128))


def face_kernel(half, emb_ref, slot_ref, given_ref, *refs):
    cnt_ref, after_ref, wide, cells = refs
    wide[...] = emb_ref[:, pl.ds(128 * half, 128), :].astype(F32).reshape(4096, 128)
    if half == 0:
        face, edge = ordering(given_ref[...])
        after_ref[0:128] = face
        after_ref[128:256] = edge
    else:
        face, edge = given_ref[0:128], given_ref[128:256]
    faces = face.astype(jnp.int32)
    pool_x8 = jnp.concatenate([pool_x_matrix()] * 8, axis=1)
    sums = jnp.zeros((32, 128), F32)
    count = jnp.zeros((8, 128), F32)
    for yc in range(16):
        voxels, member = [], []
        for q in (64 * zi + 4 * yc + yy for zi in range(2) for yy in range(4)):
            voxels.append(wide[pl.ds(q, 32, stride=128), :].astype(BF))
            row = jnp.broadcast_to(slot_ref[128 * half + q : 128 * half + q + 1, :], (128, 128))
            member.append(jnp.where(row == faces, 1.0, 0.0).astype(BF))
        left = jnp.concatenate([jnp.concatenate(voxels, axis=1), pool_x8], axis=0)
        out = dot(left, jnp.concatenate(member, axis=1), NT)
        sums = sums + out[:32]
        for x4 in range(4):
            part = out[32 + 8 * x4 : 40 + 8 * x4]
            cells[x4, 8 * yc : 8 * yc + 8, :] = part
            count = count + part
    for x4 in range(4):
        cnt_ref[x4 // 2, 128 * (x4 % 2) : 128 * (x4 % 2) + 128, :] = cells[x4].T.astype(BF)
    if half == 0:
        after_ref[256:288] = sums
        after_ref[288:296] = count
    else:
        sums = sums + given_ref[256:288]
        number = jnp.sum(count + given_ref[288:296], axis=0, keepdims=True)
        stacked = jnp.concatenate([jnp.zeros((64, 128), F32), sums, jnp.broadcast_to(number, (32, 128))], axis=0)
        after_ref[...] = jnp.where(iota((128, 128), 1) == 97, edge, stacked.T)


def faces(half, emb, slot, given):
    return pl.pallas_call(
        functools.partial(face_kernel, half),
        in_specs=[pl.BlockSpec(memory_space=pltpu.VMEM)] * 3,
        out_specs=[pl.BlockSpec(memory_space=pltpu.VMEM)] * 2,
        out_shape=[pltpu.VMEM((2, 256, 128), BF), pltpu.VMEM((128 if half else 296, 128), F32)],
        scratch_shapes=[pltpu.VMEM((4096, 128), F32), pltpu.VMEM((4, 128, 128), F32)],
        compiler_params=pltpu.CompilerParams(vmem_limit_bytes=16 << 20),
        cost_estimate=pl.CostEstimate(flops=1_000_000, bytes_accessed=10_000, transcendentals=0),
        name="faces",
    )(keep(emb), slot, keep(given) if half else given)


ROWS1 = 6 * 20 * 8
ROWS2 = 4 * 18 * 8
HEAD = 8


def ordered(even, a, b):
    return jnp.where(even, b, a), jnp.where(even, a, b)


def taps_dot(lefts, weights, depth):
    total = None
    per = 256 // depth
    for t in range(0, 9, per):
        group = lefts[t : t + per]
        left = group[0] if len(group) == 1 else jnp.concatenate(group, axis=1)
        term = dot(left, weights[pl.ds(depth * t, depth * len(group)), :])
        total = term if total is None else total + term
    return total


def window(source, tap, z, plane, rows):
    return source[tap % 3 & 1, pl.ds((z + tap // 3) * plane + 16 * (tap % 3 >> 1), rows), :]


def inner_kernel(own_ref, za_ref, zb_ref, ya_ref, yb_ref, w1a_ref, w1b_ref, b1_ref, w2_ref, b2_ref, cnt0_ref,
                 cnt1_ref, fine_ref, sums_ref, ends_ref, near_ref, rim_ref, field, this, mixed, h0f, h1f, h0b, h0n, h1b):
    gz, gy = lax.axis_index("gz"), lax.axis_index("gy")
    z_even, y_even = (gz & 1) == 0, (gy & 1) == 0
    z_low, z_high = ordered(z_even, za_ref[...].astype(F32), zb_ref[...].astype(F32))
    zs = (z_low, own_ref[...].astype(F32), z_high)
    ya, yb = ya_ref[...].astype(F32), yb_ref[...].astype(F32)
    ys = []
    for whole in ordered(y_even, ya, yb):
        low, high = ordered(z_even, whole[0:32], whole[64:96])
        ys.append((low, whole[32:64], high))
    for plane in range(6):
        part, i = plane // 2, plane % 2
        base = HEAD + plane * 160
        field[pl.ds(base, 16), :] = ys[0][part][16 * i : 16 * i + 16]
        field[pl.ds(base + 16, 128), :] = zs[part][128 * i : 128 * i + 128]
        field[pl.ds(base + 144, 16), :] = ys[1][part][16 * i : 16 * i + 16]
        for k, g in enumerate((0, 7)):
            ends_ref[k, pl.ds(24 * plane, 20), :] = field[pl.ds(base + g, 20, stride=8), :]

    lane = iota((160, 128), 1)
    for z in range(6):
        for shift in range(2):
            now = field[pl.ds(HEAD + 160 * z + 8 * shift, 160), :]
            before = field[pl.ds(HEAD + 160 * z + 8 * shift - 1, 160), :]
            this[shift, pl.ds(160 * z, 160), :] = now.astype(BF)
            mixed[shift, pl.ds(160 * z, 160), :] = jnp.where(lane < 64, now, before).astype(BF)

    row = iota((144, 128), 0)
    stay = jnp.where((row < 8) & (gy == 0), 0.0, 1.0)
    stay = jnp.where((row >= 136) & (gy == 3), 0.0, stay)
    b1, b2 = b1_ref[...], b2_ref[...]

    def conv1(source, weights, z):
        lefts = [window(source, tap, z, 160, 144) for tap in range(9)]
        return jnp.maximum(taps_dot(lefts, weights, 128) + b1, 0.0)

    for z in range(4):
        inside = 1.0
        if z == 0:
            inside = jnp.where(gz == 0, 0.0, 1.0)
        if z == 3:
            inside = jnp.where(gz == 7, 0.0, 1.0)
        h0f[pl.ds(144 * z, 144), :] = conv1(mixed, w1b_ref, z) * (stay * inside)
        h1f[pl.ds(144 * z, 144), :] = conv1(this, w1a_ref, z) * (stay * inside)
    for z in range(4):
        for k, g in enumerate((0, 7)):
            near_ref[k, pl.ds(24 * z, 18), :] = h1f[pl.ds(144 * z + g, 18, stride=8), :]
        for shift in range(2):
            at = 144 * z + 8 * shift
            h0b[shift, pl.ds(144 * z, 144), :] = h0f[pl.ds(at, 144), :].astype(BF)
            h0n[shift, pl.ds(144 * z, 144), :] = h0f[pl.ds(at + 1, 144), :].astype(BF)
            h1b[shift, pl.ds(144 * z, 144), :] = h1f[pl.ds(at, 144), :].astype(BF)

    group = iota((128, 128), 0) & 7
    sums = None
    for z in range(2):
        lefts = []
        for tap in range(9):
            h = [window(source, tap, z, 144, 128) for source in (h0b, h1b, h0n)]
            lefts.append(jnp.concatenate([jnp.concatenate(h[p : p + 2], axis=1) for p in range(2)], axis=0))
        both = taps_dot(lefts, w2_ref, 256) + b2
        for p in range(2):
            ctx = jnp.where(group == 7 * p, 0.0, both[128 * p : 128 * p + 128]).astype(BF)
            wide = ctx.astype(F32)
            fine_ref[pl.ds(512 * z + 2 * p, 128, stride=4), :] = wide
            fine_ref[pl.ds(512 * z + 2 * p + 1, 128, stride=4), :] = pltpu.roll(wide, 64, 1)
            term = dot((cnt0_ref, cnt1_ref)[z][p], ctx)
            sums = term if sums is None else sums + term
    sums_ref[...] = sums
    row, col = iota((512, 128), 0), iota((512, 128), 1)
    cell = ((row >> 7) << 4) + ((row & 127) >> 3)
    pick = jnp.where((cell == col) & ((row & 7) == 7 * (row >> 8)), 1.0, 0.0).astype(BF)
    left = jnp.concatenate([cnt0_ref[0], cnt1_ref[0], cnt0_ref[1], cnt1_ref[1]], axis=1)
    rim_ref[...] = dot(left, pick).astype(BF)


def inner(*arrays):
    return pl.pallas_call(
        inner_kernel,
        in_specs=[pl.BlockSpec(memory_space=pltpu.VMEM)] * len(arrays),
        out_specs=[pl.BlockSpec(memory_space=pltpu.VMEM)] * 5,
        out_shape=[
            pltpu.VMEM((1024, 128), F32),
            pltpu.VMEM((256, 128), F32),
            pltpu.VMEM((2, 144, 128), F32),
            pltpu.VMEM((2, 96, 128), F32),
            pltpu.VMEM((256, 128), BF),
        ],
        scratch_shapes=[
            pltpu.VMEM((HEAD + ROWS1 + 8, 128), F32),
            pltpu.VMEM((2, ROWS1, 128), BF),
            pltpu.VMEM((2, ROWS1, 128), BF),
            pltpu.VMEM((ROWS2 + 16, 128), F32),
            pltpu.VMEM((ROWS2 + 16, 128), F32),
            pltpu.VMEM((2, ROWS2, 128), BF),
            pltpu.VMEM((2, ROWS2, 128), BF),
            pltpu.VMEM((2, ROWS2, 128), BF),
        ],
        compiler_params=pltpu.CompilerParams(vmem_limit_bytes=16 << 20),
        cost_estimate=pl.CostEstimate(flops=1_000_000, bytes_accessed=10_000, transcendentals=0),
        name="inner",
    )(*arrays)


def outer_kernel(xb_ref, xa_ref, ends_ref, near_ref, fine_ref, sums_ref, w1b_ref, b1_ref, w2_ref, b2_ref, rim_ref,
                 face_ref, ctx_ref, send_ref, column, hidden, patch):
    gz, gy, gx = (lax.axis_index(a) for a in ("gz", "gy", "gx"))
    z_even, y_even, x_even = (gz & 1) == 0, (gy & 1) == 0, (gx & 1) == 0
    lane = iota((24, 128), 1)
    column[...] = jnp.zeros_like(column)
    patch[...] = fine_ref[...]
    for k, whole in enumerate(ordered(x_even, xa_ref[...].astype(F32), xb_ref[...].astype(F32))):
        low, high = ordered(z_even, whole[0:2], whole[4:6])
        for plane, rows in enumerate((low[0], low[1], whole[2], whole[3], high[0], high[1])):
            first, last = ordered(y_even, rows[16:18], rows[18:20])
            halo = jnp.concatenate([first, rows[0:16], last, jnp.zeros((4, 128), F32)], axis=0)
            own = ends_ref[k, pl.ds(24 * plane, 24), :]
            left, right = (own, halo) if k == 0 else (halo, own)
            column[k, pl.ds(24 * plane, 24), :] = jnp.where(lane < 64, left, right)

    row, lane = iota((96, 128), 0), iota((96, 128), 1)
    z_of = jnp.where(row < 24, 0, jnp.where(row < 48, 1, jnp.where(row < 72, 2, 3)))
    y_of = row - 24 * z_of
    gone = ((z_of == 0) & (gz == 0)) | ((z_of == 3) & (gz == 7)) | ((y_of == 0) & (gy == 0)) | ((y_of == 17) & (gy == 3))
    out0 = gone | ((lane < 64) & (gx == 0))
    out1 = gone | ((lane >= 64) & (gx == 7))
    at = [24 * (tap // 3) + tap % 3 for tap in range(9)]
    lefts = [jnp.concatenate([column[k, pl.ds(r, 96), :] for k in range(2)], axis=0).astype(BF) for r in at]
    total = jnp.maximum(taps_dot(lefts, w1b_ref, 128) + b1_ref[...], 0.0)
    hidden[0, 0:96] = jnp.where(out0, 0.0, total[0:96])
    hidden[1, 0:96] = near_ref[0]
    hidden[2, 0:96] = near_ref[1]
    hidden[3, 0:96] = jnp.where(out1, 0.0, total[96:192])

    lefts = []
    for r in at:
        h = [hidden[k, pl.ds(r, 40), :].astype(BF) for k in range(4)]
        h = [jnp.concatenate(h[2 * k : 2 * k + 2], axis=1) for k in range(2)]
        lefts.append(jnp.concatenate(h, axis=0))
    ctx = (taps_dot(lefts, w2_ref, 256) + b2_ref[...]).astype(BF).astype(F32)
    rows = []
    for k, x in enumerate((0, 30)):
        for z in range(2):
            wide = ctx[40 * k + 24 * z : 40 * k + 24 * z + 16]
            patch[pl.ds(512 * z + x, 16, stride=32), :] = wide
            patch[pl.ds(512 * z + x + 1, 16, stride=32), :] = pltpu.roll(wide, 64, 1)
            rows.append(wide)
    sums = sums_ref[...] + dot(rim_ref[:, :64], jnp.concatenate(rows, axis=0).astype(BF))
    ctx_ref[...] = patch[...][:, :64].astype(BF)
    both = sums[:128] + pltpu.roll(sums[128:], 64, 1)
    send_ref[...] = jnp.where(iota((128, 128), 1) < 64, both, face_ref[...])


def outer(*arrays):
    return pl.pallas_call(
        outer_kernel,
        in_specs=[pl.BlockSpec(memory_space=pltpu.VMEM)] * len(arrays),
        out_specs=[pl.BlockSpec(memory_space=pltpu.VMEM)] * 2,
        out_shape=[pltpu.VMEM((1024, 64), BF), pltpu.VMEM((128, 128), F32)],
        scratch_shapes=[
            pltpu.VMEM((2, 152, 128), F32),
            pltpu.VMEM((4, 96, 128), F32),
            pltpu.VMEM((1024, 128), F32),
        ],
        compiler_params=pltpu.CompilerParams(vmem_limit_bytes=16 << 20),
        cost_estimate=pl.CostEstimate(flops=200_000_000, bytes_accessed=3_000_000, transcendentals=0),
        name="outer",
    )(*arrays)


def edge_kernel(rows_ref, ctx_ref, edge_emb_ref, edge_ctx_ref, out_ref, sent):
    copy = pltpu.make_async_copy(ctx_ref, out_ref, sent)
    copy.start()
    rows = rows_ref[...]
    hits = jnp.where(rows[:, 97:98] == iota((128, 64), 1).astype(F32), 1.0, 0.0).astype(BF)
    sums = sum(dot(part, hits) for part in split3(rows.T))
    scale = jnp.maximum(sums[96:97], 1.0)
    edge_ctx_ref[...] = sums[:64] / scale
    edge_emb_ref[...] = sums[64:96] / scale
    copy.wait()


def edges(rows, context):
    return pl.pallas_call(
        edge_kernel,
        in_specs=[pl.BlockSpec(memory_space=pltpu.VMEM)] * 2,
        out_specs=[pl.BlockSpec(memory_space=pltpu.VMEM)] * 2 + [pl.BlockSpec(memory_space=pl.ANY)],
        out_shape=[
            jax.ShapeDtypeStruct((32, 64), F32),
            jax.ShapeDtypeStruct((64, 64), F32),
            jax.ShapeDtypeStruct((1024, 64), BF),
        ],
        scratch_shapes=[pltpu.SemaphoreType.DMA],
        name="edges",
    )(keep(rows), keep(context))


def pairs(first, count):
    return [pair for i in range(first, count - 1, 2) for pair in ((i, i + 1), (i + 1, i))]


def per_device(embedding, face_slot, face_edge, conv1_w, conv1_b, conv2_w, conv2_b):
    emb = embedding.reshape(32, 256, 128)
    gy, gx = lax.axis_index("gy"), lax.axis_index("gx")
    slot = face_slot.reshape(256, 128)
    own, voxels = pool(emb)
    zb = lax.ppermute(own, "gz", pairs(1, 8))
    za = lax.ppermute(own, "gz", pairs(0, 8))
    cnt0, half = faces(0, voxels, slot, face_edge.reshape(1, 128))
    w1, w2 = jnp.swapaxes(conv1_w, 3, 4).reshape(27, 32, 64), conv2_w.reshape(27, 64, 64)
    zb, za, half = lax.optimization_barrier((zb, za, half))
    planes = [a.reshape(2, 16, 8, 128) for a in (za, own, zb)]
    y_even, x_even = (gy & 1) == 0, (gx & 1) == 0

    def y_edge(high):
        first = jnp.where(high, 14, 0)
        return jnp.concatenate([lax.dynamic_slice_in_dim(a, first, 2, axis=1) for a in planes], axis=0)

    to_a, to_b = lax.optimization_barrier((y_edge(y_even), y_edge(jnp.logical_not(y_even))))
    ya = lax.ppermute(to_a, "gy", pairs(0, 4))
    yb = lax.ppermute(to_b, "gy", pairs(1, 4))
    cnt1, face = faces(1, voxels, slot, half)
    ya, yb, face = lax.optimization_barrier((ya, yb, face))

    def x_edge(g):
        mid = jnp.concatenate([a[:, :, g] for a in planes], axis=0)
        return jnp.concatenate([mid, ya[:, :, g], yb[:, :, g]], axis=1)

    low, high = x_edge(0), x_edge(7)
    to_b, to_a, w1 = lax.optimization_barrier((jnp.where(x_even, low, high), jnp.where(x_even, high, low), w1))
    w1a, w1b, w2a = bands(w1, w2)
    xa = lax.ppermute(to_a, "gx", pairs(0, 8))
    xb = lax.ppermute(to_b, "gx", pairs(1, 8))
    twice = lambda b: jnp.concatenate([b, b]).reshape(1, 128)
    b1, b2 = twice(conv1_b), twice(conv2_b)
    w1a, w1b, w2a, cnt0, cnt1 = (keep(a) for a in (w1a, w1b, w2a, cnt0, cnt1))
    fine, sums, ends, near, rim = inner(
        own, za, zb, ya.reshape(96, 128), yb.reshape(96, 128), w1a, w1b, b1, w2a, b2, cnt0, cnt1
    )
    context, send = outer(
        xb, xa, keep(ends), keep(near), keep(fine), keep(sums), w1b, b1, w2a, b2, keep(rim), keep(face)
    )
    rows = lax.all_to_all(send, "gx", 0, 0, tiled=True)
    edge_emb, edge_ctx, context = edges(rows, context)
    context = jnp.transpose(context.reshape(2, 16, 32, 64), (3, 0, 1, 2))
    return (context, edge_emb, edge_ctx)


def solution(mesh):
    in_specs = (P(None, "gz", "gy", "gx"), P("gz", "gy", "gx"), P(("gz", "gy", "gx")), P(), P(), P(), P())
    out_specs = (P(None, "gz", "gy", "gx"), P(None, ("gz", "gy", "gx")), P(None, ("gz", "gy", "gx")))
    return jax.shard_map(per_device, mesh=mesh, in_specs=in_specs, out_specs=out_specs, check_vma=False)
```

```python
import functools

import jax
import jax.numpy as jnp
from jax import lax
from jax.experimental import pallas as pl
from jax.experimental.pallas import tpu as pltpu
from jax.sharding import PartitionSpec as P

BF = jnp.bfloat16
F32 = jnp.float32
NT = (((1,), (1,)), ((), ()))
NN = (((1,), (0,)), ((), ()))


def dot(a, b, dims=NN):
    return lax.dot_general(a, b, dims, preferred_element_type=F32)


def keep(array):
    return pltpu.with_memory_space_constraint(array, pltpu.VMEM)


def iota(shape, dim):
    return lax.broadcasted_iota(jnp.int32, shape, dim)


def split3(x):
    hi = x.astype(BF)
    rest = x - hi.astype(F32)
    mid = rest.astype(BF)
    low = (rest - mid.astype(F32)).astype(BF)
    return hi, mid, low


def pool_x_matrix():
    row, col = iota((32, 128), 0), iota((32, 128), 1)
    cell = 4 * (row & 7) + (row >> 3)
    return jnp.where((col >> 2) == cell, 1.0, 0.0).astype(BF)


def pool_kernel(emb_ref, out_ref, block, sums, arrived):
    chunks = arrived.shape[0]
    per = 32 // chunks
    copies = [
        pltpu.make_async_copy(emb_ref.at[pl.ds(per * i, per)], block.at[pl.ds(per * i, per)], arrived.at[i])
        for i in range(chunks)
    ]
    for copy in copies:
        copy.start()
    row, col = iota((32, 256), 0), iota((32, 256), 1)
    cell = ((col >> 7) << 4) + ((col & 63) >> 2)
    pool_zy = jnp.where(cell == row, 1.0, 0.0).astype(BF)
    pool_x = jnp.concatenate([pool_x_matrix()] * 3, axis=1)
    lane = iota((8, 128), 1)
    far, near = lane < 64, (lane & 32) == 0
    for i in range(chunks):
        copies[i].wait()
        for c in range(per * i, per * i + per):
            sums[pl.ds(32 * c, 32), :] = dot(pool_zy, block[c])
    for part in range(8):
        rows = jnp.concatenate([sums[pl.ds(4 * part + i, 32, stride=32), :] for i in range(4)], axis=0)
        cells = dot(pool_x, jnp.concatenate(split3(rows), axis=1), NT) * (1.0 / 32.0)
        v = [cells[8 * i : 8 * i + 8] for i in range(4)]
        a = [jnp.where(far, v[i], pltpu.roll(v[i + 2], 64, 1)) for i in range(2)]
        b = [jnp.where(far, pltpu.roll(v[i], 64, 1), v[i + 2]) for i in range(2)]
        done = []
        for lo, hi in (a, b):
            done.append(jnp.where(near, lo, pltpu.roll(hi, 32, 1)))
            done.append(jnp.where(near, pltpu.roll(lo, 96, 1), hi))
        out_ref[pl.ds(32 * part, 32), :] = jnp.concatenate(done, axis=0).astype(BF)


def pool(emb):
    chunks = 2
    return pl.pallas_call(
        pool_kernel,
        in_specs=[pl.BlockSpec(memory_space=pl.ANY)],
        out_specs=[pl.BlockSpec(memory_space=pltpu.VMEM)] * 2,
        out_shape=[pltpu.VMEM((256, 128), BF), pltpu.VMEM((32, 256, 128), BF)],
        scratch_shapes=[
            pltpu.VMEM((1024, 128), F32),
            pltpu.SemaphoreType.DMA((chunks,)),
        ],
        compiler_params=pltpu.CompilerParams(vmem_limit_bytes=32 << 20),
        cost_estimate=pl.CostEstimate(flops=80_000_000, bytes_accessed=2_200_000, transcendentals=0),
        name="pool",
    )(pltpu.with_memory_space_constraint(emb, pltpu.HBM))


def banded(tap, taps):
    zero = jnp.zeros_like(taps(tap, 0))
    w = [taps(tap, k) if 0 <= k < 3 else zero for k in range(-1, 4)]
    return [jnp.concatenate([w[k + 1], w[k]], axis=1) for k in range(4)]


def bands_kernel(w1_ref, w2_ref, w1a_ref, w1b_ref, w2a_ref):
    for tap in range(9):
        bands = banded(tap, lambda t, k: w1_ref[3 * t + k])
        w1a_ref[pl.ds(128 * tap, 128), :] = jnp.concatenate(bands, axis=0)
        w1b_ref[pl.ds(128 * tap, 128), :] = jnp.concatenate(bands[2:] + bands[:2], axis=0)
        bands = banded(tap, lambda t, k: w2_ref[3 * t + k].astype(F32).T.astype(BF))
        w2a_ref[pl.ds(256 * tap, 256), :] = jnp.concatenate(bands, axis=0)


def bands(w1, w2):
    return pl.pallas_call(
        bands_kernel,
        in_specs=[pl.BlockSpec(memory_space=pltpu.VMEM)] * 2,
        out_specs=[pl.BlockSpec(memory_space=pltpu.VMEM)] * 3,
        out_shape=[pltpu.VMEM((1152, 128), BF), pltpu.VMEM((1152, 128), BF), pltpu.VMEM((2304, 128), BF)],
        compiler_params=pltpu.CompilerParams(vmem_limit_bytes=16 << 20),
        cost_estimate=pl.CostEstimate(flops=1_000_000, bytes_accessed=10_000, transcendentals=0),
        name="bands",
    )(w1, w2)


def ordering(edge):
    i0, i1 = iota((128, 128), 0), iota((128, 128), 1)
    label = jnp.broadcast_to(edge, (128, 128))
    owner = ((label >> 6) & 7).astype(F32)
    local = (label & 63).astype(F32)
    ahead = jnp.where((owner == owner.T) & (i0 < i1), 1.0, 0.0)
    place = owner[0:1, :] * 16.0 + jnp.sum(ahead, axis=0, keepdims=True)
    chosen = place == i0.astype(F32)
    face = jnp.sum(jnp.where(chosen, i1.astype(F32), 0.0), axis=1, keepdims=True)
    edge = jnp.sum(jnp.where(chosen, local, 0.0), axis=1, keepdims=True)
    return jnp.broadcast_to(face, (128, 128)), jnp.broadcast_to(edge, (128, 128))


def face_kernel(half, emb_ref, slot_ref, given_ref, *refs):
    cnt_ref, after_ref, side_ref, wide, cells = refs
    wide[...] = emb_ref[:, pl.ds(128 * half, 128), :].astype(F32).reshape(4096, 128)
    if half == 0:
        face, edge = ordering(given_ref[...])
        after_ref[0:128] = face
        after_ref[128:256] = edge
    else:
        face, edge = given_ref[0:128], given_ref[128:256]
    faces = face.astype(jnp.int32)
    pool_x8 = jnp.concatenate([pool_x_matrix()] * 8, axis=1)
    sums = jnp.zeros((32, 128), F32)
    count = jnp.zeros((8, 128), F32)
    for yc in range(16):
        voxels, member = [], []
        for q in (64 * zi + 4 * yc + yy for zi in range(2) for yy in range(4)):
            voxels.append(wide[pl.ds(q, 32, stride=128), :].astype(BF))
            row = jnp.broadcast_to(slot_ref[128 * half + q : 128 * half + q + 1, :], (128, 128))
            member.append(jnp.where(row == faces, 1.0, 0.0).astype(BF))
        left = jnp.concatenate([jnp.concatenate(voxels, axis=1), pool_x8], axis=0)
        out = dot(left, jnp.concatenate(member, axis=1), NT)
        sums = sums + out[:32]
        for x4 in range(4):
            part = out[32 + 8 * x4 : 40 + 8 * x4]
            cells[x4, 8 * yc : 8 * yc + 8, :] = part
            count = count + part
    for x4 in range(4):
        cnt_ref[x4 // 2, 128 * (x4 % 2) : 128 * (x4 % 2) + 128, :] = cells[x4].T.astype(BF)
    for x2 in range(2):
        side_ref[pl.ds(16 * x2, 16), :] = cells[x2, pl.ds(0, 16, stride=8), :].astype(BF)
    if half == 0:
        after_ref[256:288] = sums
        after_ref[288:296] = count
    else:
        sums = sums + given_ref[256:288]
        number = jnp.sum(count + given_ref[288:296], axis=0, keepdims=True)
        stacked = jnp.concatenate([jnp.zeros((64, 128), F32), sums, jnp.broadcast_to(number, (32, 128))], axis=0)
        side_ref[pl.ds(32, 16), :] = edge.T[:16].astype(BF)
        lane = iota((128, 128), 1)
        rows = stacked.T
        high = jnp.floor(rows * (1.0 / 256.0)) * 256.0
        rows = jnp.where(lane == 96, high, jnp.where(lane == 98, rows - high, rows))
        after_ref[...] = jnp.where(lane == 97, edge, rows)


def faces(half, emb, slot, given):
    return pl.pallas_call(
        functools.partial(face_kernel, half),
        in_specs=[pl.BlockSpec(memory_space=pltpu.VMEM)] * 3,
        out_specs=[pl.BlockSpec(memory_space=pltpu.VMEM)] * 3,
        out_shape=[
            pltpu.VMEM((2, 256, 128), BF),
            pltpu.VMEM((128 if half else 296, 128), F32),
            pltpu.VMEM((48 if half else 32, 128), BF),
        ],
        scratch_shapes=[pltpu.VMEM((4096, 128), F32), pltpu.VMEM((4, 128, 128), F32)],
        compiler_params=pltpu.CompilerParams(vmem_limit_bytes=16 << 20),
        cost_estimate=pl.CostEstimate(flops=1_000_000, bytes_accessed=10_000, transcendentals=0),
        name="faces",
    )(keep(emb), slot, keep(given) if half else given)


ROWS1 = 6 * 20 * 8
ROWS2 = 4 * 18 * 8
HEAD = 8


def ordered(even, a, b):
    return jnp.where(even, b, a), jnp.where(even, a, b)


def taps_dot(lefts, weights, depth):
    total = None
    per = 256 // depth
    for t in range(0, 9, per):
        group = lefts[t : t + per]
        left = group[0] if len(group) == 1 else jnp.concatenate(group, axis=1)
        term = dot(left, weights[pl.ds(depth * t, depth * len(group)), :])
        total = term if total is None else total + term
    return total


def window(source, tap, z, plane, rows):
    return source[tap % 3 & 1, pl.ds((z + tap // 3) * plane + 16 * (tap % 3 >> 1), rows), :]


def inner_kernel(own_ref, za_ref, zb_ref, ya_ref, yb_ref, w1a_ref, w1b_ref, b1_ref, w2_ref, b2_ref, cnt0_ref,
                 cnt1_ref, fine_ref, sums_ref, ends_ref, near_ref, rim_ref, field, this, mixed, h0f, h1f, h0b, h0n, h1b):
    gz, gy = lax.axis_index("gz"), lax.axis_index("gy")
    z_even, y_even = (gz & 1) == 0, (gy & 1) == 0
    z_low, z_high = ordered(z_even, za_ref[...].astype(F32), zb_ref[...].astype(F32))
    zs = (z_low, own_ref[...].astype(F32), z_high)
    ya, yb = ya_ref[...].astype(F32), yb_ref[...].astype(F32)
    ys = []
    for whole in ordered(y_even, ya, yb):
        low, high = ordered(z_even, whole[0:32], whole[64:96])
        ys.append((low, whole[32:64], high))
    for plane in range(6):
        part, i = plane // 2, plane % 2
        base = HEAD + plane * 160
        field[pl.ds(base, 16), :] = ys[0][part][16 * i : 16 * i + 16]
        field[pl.ds(base + 16, 128), :] = zs[part][128 * i : 128 * i + 128]
        field[pl.ds(base + 144, 16), :] = ys[1][part][16 * i : 16 * i + 16]
        for k, g in enumerate((0, 7)):
            ends_ref[k, pl.ds(24 * plane, 20), :] = field[pl.ds(base + g, 20, stride=8), :]

    lane = iota((160, 128), 1)
    for z in range(6):
        for shift in range(2):
            now = field[pl.ds(HEAD + 160 * z + 8 * shift, 160), :]
            before = field[pl.ds(HEAD + 160 * z + 8 * shift - 1, 160), :]
            this[shift, pl.ds(160 * z, 160), :] = now.astype(BF)
            mixed[shift, pl.ds(160 * z, 160), :] = jnp.where(lane < 64, now, before).astype(BF)

    row = iota((144, 128), 0)
    stay = jnp.where((row < 8) & (gy == 0), 0.0, 1.0)
    stay = jnp.where((row >= 136) & (gy == 3), 0.0, stay)
    b1, b2 = b1_ref[...], b2_ref[...]

    def conv1(source, weights, z):
        lefts = [window(source, tap, z, 160, 144) for tap in range(9)]
        return jnp.maximum(taps_dot(lefts, weights, 128) + b1, 0.0)

    for z in range(4):
        inside = 1.0
        if z == 0:
            inside = jnp.where(gz == 0, 0.0, 1.0)
        if z == 3:
            inside = jnp.where(gz == 7, 0.0, 1.0)
        h0f[pl.ds(144 * z, 144), :] = conv1(mixed, w1b_ref, z) * (stay * inside)
        h1f[pl.ds(144 * z, 144), :] = conv1(this, w1a_ref, z) * (stay * inside)
    for z in range(4):
        for k, g in enumerate((0, 7)):
            near_ref[k, pl.ds(24 * z, 18), :] = h1f[pl.ds(144 * z + g, 18, stride=8), :]
        for shift in range(2):
            at = 144 * z + 8 * shift
            h0b[shift, pl.ds(144 * z, 144), :] = h0f[pl.ds(at, 144), :].astype(BF)
            h0n[shift, pl.ds(144 * z, 144), :] = h0f[pl.ds(at + 1, 144), :].astype(BF)
            h1b[shift, pl.ds(144 * z, 144), :] = h1f[pl.ds(at, 144), :].astype(BF)

    group = iota((128, 128), 0) & 7
    sums = None
    for z in range(2):
        lefts = []
        for tap in range(9):
            h = [window(source, tap, z, 144, 128) for source in (h0b, h1b, h0n)]
            lefts.append(jnp.concatenate([jnp.concatenate(h[p : p + 2], axis=1) for p in range(2)], axis=0))
        both = taps_dot(lefts, w2_ref, 256) + b2
        for p in range(2):
            ctx = jnp.where(group == 7 * p, 0.0, both[128 * p : 128 * p + 128]).astype(BF)
            wide = ctx.astype(F32)
            fine_ref[pl.ds(512 * z + 2 * p, 128, stride=4), :] = wide
            fine_ref[pl.ds(512 * z + 2 * p + 1, 128, stride=4), :] = pltpu.roll(wide, 64, 1)
            term = dot((cnt0_ref, cnt1_ref)[z][p], ctx)
            sums = term if sums is None else sums + term
    sums_ref[...] = sums
    row, col = iota((512, 128), 0), iota((512, 128), 1)
    cell = ((row >> 7) << 4) + ((row & 127) >> 3)
    pick = jnp.where((cell == col) & ((row & 7) == 7 * (row >> 8)), 1.0, 0.0).astype(BF)
    left = jnp.concatenate([cnt0_ref[0], cnt1_ref[0], cnt0_ref[1], cnt1_ref[1]], axis=1)
    rim_ref[...] = dot(left, pick).astype(BF)


def inner(*arrays):
    return pl.pallas_call(
        inner_kernel,
        in_specs=[pl.BlockSpec(memory_space=pltpu.VMEM)] * len(arrays),
        out_specs=[pl.BlockSpec(memory_space=pltpu.VMEM)] * 5,
        out_shape=[
            pltpu.VMEM((1024, 128), F32),
            pltpu.VMEM((256, 128), F32),
            pltpu.VMEM((2, 144, 128), F32),
            pltpu.VMEM((2, 96, 128), F32),
            pltpu.VMEM((256, 128), BF),
        ],
        scratch_shapes=[
            pltpu.VMEM((HEAD + ROWS1 + 8, 128), F32),
            pltpu.VMEM((2, ROWS1, 128), BF),
            pltpu.VMEM((2, ROWS1, 128), BF),
            pltpu.VMEM((ROWS2 + 16, 128), F32),
            pltpu.VMEM((ROWS2 + 16, 128), F32),
            pltpu.VMEM((2, ROWS2, 128), BF),
            pltpu.VMEM((2, ROWS2, 128), BF),
            pltpu.VMEM((2, ROWS2, 128), BF),
        ],
        compiler_params=pltpu.CompilerParams(vmem_limit_bytes=16 << 20),
        cost_estimate=pl.CostEstimate(flops=1_000_000, bytes_accessed=10_000, transcendentals=0),
        name="inner",
    )(*arrays)


def outer_kernel(xb_ref, xa_ref, ends_ref, near_ref, fine_ref, sums_ref, w1a_ref, w1b_ref, b1_ref, w2_ref, b2_ref, rim_ref,
                 face_ref, patch, send_ref, column, hidden):
    gz, gy, gx = (lax.axis_index(a) for a in ("gz", "gy", "gx"))
    z_even, y_even, x_even = (gz & 1) == 0, (gy & 1) == 0, (gx & 1) == 0
    lane = iota((24, 128), 1)
    column[...] = jnp.zeros_like(column)
    patch[...] = fine_ref[...]
    got = xb_ref[...].astype(F32)
    for k, whole in enumerate(ordered(x_even, xa_ref[80:200].astype(F32), got[80:200])):
        planes = [whole[20 * i : 20 * i + 20] for i in range(6)]
        low0, high0 = ordered(z_even, planes[0], planes[4])
        low1, high1 = ordered(z_even, planes[1], planes[5])
        for plane, rows in enumerate((low0, low1, planes[2], planes[3], high0, high1)):
            first, last = ordered(y_even, rows[16:18], rows[18:20])
            halo = jnp.concatenate([first, rows[0:16], last, jnp.zeros((4, 128), F32)], axis=0)
            own = ends_ref[k, pl.ds(24 * plane, 24), :]
            left, right = (own, halo) if k == 0 else (halo, own)
            column[k, pl.ds(24 * plane, 24), :] = jnp.where(lane < 64, left, right)
            if k == 1:
                column[2, pl.ds(24 * plane, 24), :] = halo

    row, lane = iota((96, 128), 0), iota((96, 128), 1)
    z_of = jnp.where(row < 24, 0, jnp.where(row < 48, 1, jnp.where(row < 72, 2, 3)))
    y_of = row - 24 * z_of
    gone = ((z_of == 0) & (gz == 0)) | ((z_of == 3) & (gz == 7)) | ((y_of == 0) & (gy == 0)) | ((y_of == 17) & (gy == 3))
    out0 = gone | ((lane < 64) & (gx == 0))
    out1 = gone | ((lane >= 64) & (gx == 7))
    at = [24 * (tap // 3) + tap % 3 for tap in range(9)]
    lefts = [jnp.concatenate([column[k, pl.ds(r, 96), :] for k in range(2)], axis=0).astype(BF) for r in at]
    total = jnp.maximum(taps_dot(lefts, w1b_ref, 128) + b1_ref[...], 0.0)
    lefts = [column[2, pl.ds(r, 96), :].astype(BF) for r in at]
    beyond = jnp.maximum(taps_dot(lefts, w1a_ref, 128) + b1_ref[...], 0.0)
    hidden[0, 0:96] = jnp.where(out0, 0.0, total[0:96])
    hidden[1, 0:96] = near_ref[0]
    hidden[2, 0:96] = near_ref[1]
    hidden[3, 0:96] = jnp.where(out1, 0.0, total[96:192])
    hidden[4, 0:96] = jnp.where(gone, 0.0, beyond)

    lefts = []
    for r in at:
        h = [hidden[k, pl.ds(r, 40), :].astype(BF) for k in range(5)]
        lefts.append(jnp.concatenate([jnp.concatenate([h[k], h[k + 1]], axis=1) for k in (0, 2, 3)], axis=0))
    ctx = (taps_dot(lefts, w2_ref, 256) + b2_ref[...]).astype(BF).astype(F32)
    rows = []
    for k, x in enumerate((0, 30)):
        for z in range(2):
            wide = ctx[40 * k + 24 * z : 40 * k + 24 * z + 16]
            patch[pl.ds(512 * z + x, 16, stride=32), :] = wide
            patch[pl.ds(512 * z + x + 1, 16, stride=32), :] = pltpu.roll(wide, 64, 1)
            rows.append(jnp.where(gx == 4, 0.0, wide) if k == 0 else wide)
    sums = sums_ref[...] + dot(rim_ref[:, :64], jnp.concatenate(rows, axis=0).astype(BF))
    both = sums[:128] + pltpu.roll(sums[128:], 64, 1)
    lane = iota((128, 128), 1)
    mine = jnp.where(lane < 64, both, face_ref[...]).astype(BF)

    next_ctx = [ctx[80 + 24 * z : 96 + 24 * z] for z in range(2)]
    right = jnp.concatenate([v for c in next_ctx for v in (c, pltpu.roll(c, 64, 1))], axis=0).astype(BF)
    other = dot(got[0:64].T.astype(BF), right)
    edge = jnp.broadcast_to(got[64:65], (128, 128)).T
    other = jnp.where(lane < 64, other, jnp.where(lane == 97, edge, 0.0))
    other = jnp.where(gx == 3, other, 0.0).astype(BF)
    next_ctx = jnp.concatenate(next_ctx, axis=0).astype(BF)
    for d in range(8):
        send_ref[pl.ds(64 * d, 16), :] = mine[16 * d : 16 * d + 16]
        send_ref[pl.ds(64 * d + 16, 16), :] = other[16 * d : 16 * d + 16]
        send_ref[pl.ds(64 * d + 32, 32), :] = next_ctx


def outer(*arrays):
    return pl.pallas_call(
        outer_kernel,
        in_specs=[pl.BlockSpec(memory_space=pltpu.VMEM)] * len(arrays),
        out_specs=[pl.BlockSpec(memory_space=pltpu.VMEM)] * 2,
        out_shape=[pltpu.VMEM((1024, 128), F32), pltpu.VMEM((512, 128), BF)],
        scratch_shapes=[pltpu.VMEM((3, 152, 128), F32), pltpu.VMEM((5, 96, 128), F32)],
        compiler_params=pltpu.CompilerParams(vmem_limit_bytes=16 << 20),
        cost_estimate=pl.CostEstimate(flops=200_000_000, bytes_accessed=3_000_000, transcendentals=0),
        name="outer",
    )(*arrays)


def edge_kernel(rows_ref, fine_ref, edge_emb_ref, edge_ctx_ref, out_ref, patch, final, sent):
    patch[...] = fine_ref[...]

    @pl.when(lax.axis_index("gx") == 4)
    def _():
        for z in range(2):
            wide = rows_ref[pl.ds(64 * 3 + 32 + 16 * z, 16), :].astype(F32)
            patch[pl.ds(512 * z, 16, stride=32), :] = wide
            patch[pl.ds(512 * z + 1, 16, stride=32), :] = pltpu.roll(wide, 64, 1)

    final[...] = patch[...][:, :64].astype(BF)
    copy = pltpu.make_async_copy(final, out_ref, sent)
    copy.start()
    rows = [rows_ref[pl.ds(64 * d + 16 * i, 16), :] for i in range(2) for d in range(8)]
    rows = jnp.concatenate(rows, axis=0).astype(F32)
    hits = jnp.where(rows[:, 97:98] == iota((256, 64), 1).astype(F32), 1.0, 0.0).astype(BF)
    sums = dot(rows.T.astype(BF), hits)
    scale = jnp.maximum(sums[96:97] + sums[98:99], 1.0)
    edge_ctx_ref[...] = sums[:64] / scale
    edge_emb_ref[...] = sums[64:96] / scale
    copy.wait()


def edges(rows, context):
    return pl.pallas_call(
        edge_kernel,
        in_specs=[pl.BlockSpec(memory_space=pltpu.VMEM)] * 2,
        out_specs=[pl.BlockSpec(memory_space=pltpu.VMEM)] * 2 + [pl.BlockSpec(memory_space=pl.ANY)],
        out_shape=[
            jax.ShapeDtypeStruct((32, 64), F32),
            jax.ShapeDtypeStruct((64, 64), F32),
            jax.ShapeDtypeStruct((1024, 64), BF),
        ],
        scratch_shapes=[pltpu.VMEM((1024, 128), F32), pltpu.VMEM((1024, 64), BF), pltpu.SemaphoreType.DMA],
        name="edges",
    )(keep(rows), keep(context))


def pairs(first, count):
    return [pair for i in range(first, count - 1, 2) for pair in ((i, i + 1), (i + 1, i))]


def per_device(embedding, face_slot, face_edge, conv1_w, conv1_b, conv2_w, conv2_b):
    emb = embedding.reshape(32, 256, 128)
    gy, gx = lax.axis_index("gy"), lax.axis_index("gx")
    slot = face_slot.reshape(256, 128)
    own, voxels = pool(emb)
    zb = lax.ppermute(own, "gz", pairs(1, 8))
    za = lax.ppermute(own, "gz", pairs(0, 8))
    cnt0, half, side0 = faces(0, voxels, slot, face_edge.reshape(1, 128))
    w1, w2 = jnp.swapaxes(conv1_w, 3, 4).reshape(27, 32, 64), conv2_w.reshape(27, 64, 64)
    zb, za, half = lax.optimization_barrier((zb, za, half))
    planes = [a.reshape(2, 16, 8, 128) for a in (za, own, zb)]
    y_even, x_even = (gy & 1) == 0, (gx & 1) == 0

    def y_edge(high):
        first = jnp.where(high, 14, 0)
        return jnp.concatenate([lax.dynamic_slice_in_dim(a, first, 2, axis=1) for a in planes], axis=0)

    to_a, to_b = lax.optimization_barrier((y_edge(y_even), y_edge(jnp.logical_not(y_even))))
    ya = lax.ppermute(to_a, "gy", pairs(0, 4))
    yb = lax.ppermute(to_b, "gy", pairs(1, 4))
    cnt1, face, side1 = faces(1, voxels, slot, half)
    ya, yb, face = lax.optimization_barrier((ya, yb, face))

    def x_edge(g):
        mid = jnp.concatenate([a[:, :, g] for a in planes], axis=0)
        return jnp.concatenate([mid, ya[:, :, g], yb[:, :, g]], axis=1).reshape(120, 128)

    low, high = x_edge(0), x_edge(7)
    to_b = jnp.concatenate([side0, side1, jnp.where(x_even, low, high)], axis=0)
    to_a = jnp.concatenate([side0, side1, jnp.where(x_even, high, low)], axis=0)
    to_b, to_a, w1 = lax.optimization_barrier((to_b, to_a, w1))
    w1a, w1b, w2a = bands(w1, w2)
    xa = lax.ppermute(to_a, "gx", pairs(0, 8))
    xb = lax.ppermute(to_b, "gx", [(1, 2), (2, 1), (5, 6), (6, 5), (4, 3)])
    twice = lambda b: jnp.concatenate([b, b]).reshape(1, 128)
    b1, b2 = twice(conv1_b), twice(conv2_b)
    w1a, w1b, w2a, cnt0, cnt1 = (keep(a) for a in (w1a, w1b, w2a, cnt0, cnt1))
    fine, sums, ends, near, rim = inner(
        own, za, zb, ya.reshape(96, 128), yb.reshape(96, 128), w1a, w1b, b1, w2a, b2, cnt0, cnt1
    )
    context, send = outer(
        xb, xa, keep(ends), keep(near), keep(fine), keep(sums), w1a, w1b, b1, w2a, b2, keep(rim), keep(face)
    )
    rows = lax.all_to_all(send, "gx", 0, 0, tiled=True)
    edge_emb, edge_ctx, context = edges(rows, context)
    context = jnp.transpose(context.reshape(2, 16, 32, 64), (3, 0, 1, 2))
    return (context, edge_emb, edge_ctx)


def solution(mesh):
    in_specs = (P(None, "gz", "gy", "gx"), P("gz", "gy", "gx"), P(("gz", "gy", "gx")), P(), P(), P(), P())
    out_specs = (P(None, "gz", "gy", "gx"), P(None, ("gz", "gy", "gx")), P(None, ("gz", "gy", "gx")))
    return jax.shard_map(per_device, mesh=mesh, in_specs=in_specs, out_specs=out_specs, check_vma=False)
```

```python
import functools

import jax
import jax.numpy as jnp
from jax import lax
from jax.experimental import pallas as pl
from jax.experimental.pallas import tpu as pltpu
from jax.sharding import PartitionSpec as P

BF = jnp.bfloat16
F32 = jnp.float32
NT = (((1,), (1,)), ((), ()))
NN = (((1,), (0,)), ((), ()))


def dot(a, b, dims=NN):
    return lax.dot_general(a, b, dims, preferred_element_type=F32)


def keep(array):
    return pltpu.with_memory_space_constraint(array, pltpu.VMEM)


def iota(shape, dim):
    return lax.broadcasted_iota(jnp.int32, shape, dim)


def split3(x):
    hi = x.astype(BF)
    rest = x - hi.astype(F32)
    mid = rest.astype(BF)
    low = (rest - mid.astype(F32)).astype(BF)
    return hi, mid, low


def pool_x_matrix():
    row, col = iota((32, 128), 0), iota((32, 128), 1)
    cell = 4 * (row & 7) + (row >> 3)
    return jnp.where((col >> 2) == cell, 1.0, 0.0).astype(BF)


def pool_kernel(emb_ref, out_ref, block, sums, arrived):
    chunks = arrived.shape[0]
    per = 32 // chunks
    copies = [
        pltpu.make_async_copy(emb_ref.at[pl.ds(per * i, per)], block.at[pl.ds(per * i, per)], arrived.at[i])
        for i in range(chunks)
    ]
    for copy in copies:
        copy.start()
    row, col = iota((32, 256), 0), iota((32, 256), 1)
    cell = ((col >> 7) << 4) + ((col & 63) >> 2)
    pool_zy = jnp.where(cell == row, 1.0, 0.0).astype(BF)
    pool_x = jnp.concatenate([pool_x_matrix()] * 3, axis=1)
    lane = iota((8, 128), 1)
    far, near = lane < 64, (lane & 32) == 0
    for i in range(chunks):
        copies[i].wait()
        for c in range(per * i, per * i + per):
            sums[pl.ds(32 * c, 32), :] = dot(pool_zy, block[c])
    for part in range(8):
        rows = jnp.concatenate([sums[pl.ds(4 * part + i, 32, stride=32), :] for i in range(4)], axis=0)
        cells = dot(pool_x, jnp.concatenate(split3(rows), axis=1), NT) * (1.0 / 32.0)
        v = [cells[8 * i : 8 * i + 8] for i in range(4)]
        a = [jnp.where(far, v[i], pltpu.roll(v[i + 2], 64, 1)) for i in range(2)]
        b = [jnp.where(far, pltpu.roll(v[i], 64, 1), v[i + 2]) for i in range(2)]
        done = []
        for lo, hi in (a, b):
            done.append(jnp.where(near, lo, pltpu.roll(hi, 32, 1)))
            done.append(jnp.where(near, pltpu.roll(lo, 96, 1), hi))
        out_ref[pl.ds(32 * part, 32), :] = jnp.concatenate(done, axis=0).astype(BF)


def pool(emb):
    chunks = 2
    return pl.pallas_call(
        pool_kernel,
        in_specs=[pl.BlockSpec(memory_space=pl.ANY)],
        out_specs=[pl.BlockSpec(memory_space=pltpu.VMEM)] * 2,
        out_shape=[pltpu.VMEM((256, 128), BF), pltpu.VMEM((32, 256, 128), BF)],
        scratch_shapes=[
            pltpu.VMEM((1024, 128), F32),
            pltpu.SemaphoreType.DMA((chunks,)),
        ],
        compiler_params=pltpu.CompilerParams(vmem_limit_bytes=32 << 20),
        cost_estimate=pl.CostEstimate(flops=80_000_000, bytes_accessed=2_200_000, transcendentals=0),
        name="pool",
    )(pltpu.with_memory_space_constraint(emb, pltpu.HBM))


def banded(tap, taps):
    zero = jnp.zeros_like(taps(tap, 0))
    w = [taps(tap, k) if 0 <= k < 3 else zero for k in range(-1, 4)]
    return [jnp.concatenate([w[k + 1], w[k]], axis=1) for k in range(4)]


def bands_kernel(w1_ref, w2_ref, w1a_ref, w1b_ref, w2a_ref):
    for tap in range(9):
        bands = banded(tap, lambda t, k: w1_ref[3 * t + k])
        w1a_ref[pl.ds(128 * tap, 128), :] = jnp.concatenate(bands, axis=0)
        w1b_ref[pl.ds(128 * tap, 128), :] = jnp.concatenate(bands[2:] + bands[:2], axis=0)
        bands = banded(tap, lambda t, k: w2_ref[3 * t + k].astype(F32).T.astype(BF))
        w2a_ref[pl.ds(256 * tap, 256), :] = jnp.concatenate(bands, axis=0)


def bands(w1, w2):
    return pl.pallas_call(
        bands_kernel,
        in_specs=[pl.BlockSpec(memory_space=pltpu.VMEM)] * 2,
        out_specs=[pl.BlockSpec(memory_space=pltpu.VMEM)] * 3,
        out_shape=[pltpu.VMEM((1152, 128), BF), pltpu.VMEM((1152, 128), BF), pltpu.VMEM((2304, 128), BF)],
        compiler_params=pltpu.CompilerParams(vmem_limit_bytes=16 << 20),
        cost_estimate=pl.CostEstimate(flops=1_000_000, bytes_accessed=10_000, transcendentals=0),
        name="bands",
    )(w1, w2)


def ordering(edge):
    i0, i1 = iota((128, 128), 0), iota((128, 128), 1)
    label = jnp.broadcast_to(edge, (128, 128))
    owner = ((label >> 6) & 7).astype(F32)
    local = (label & 63).astype(F32)
    ahead = jnp.where((owner == owner.T) & (i0 < i1), 1.0, 0.0)
    place = owner[0:1, :] * 16.0 + jnp.sum(ahead, axis=0, keepdims=True)
    chosen = place == i0.astype(F32)
    face = jnp.sum(jnp.where(chosen, i1.astype(F32), 0.0), axis=1, keepdims=True)
    edge = jnp.sum(jnp.where(chosen, local, 0.0), axis=1, keepdims=True)
    return jnp.broadcast_to(face, (128, 128)), jnp.broadcast_to(edge, (128, 128))


def face_kernel(half, emb_ref, slot_ref, given_ref, *refs):
    cnt_ref, after_ref, side_ref, wide, cells = refs
    wide[...] = emb_ref[:, pl.ds(128 * half, 128), :].astype(F32).reshape(4096, 128)
    if half == 0:
        face, edge = ordering(given_ref[...])
        after_ref[0:128] = face
        after_ref[128:256] = edge
    else:
        face, edge = given_ref[0:128], given_ref[128:256]
    faces = face.astype(jnp.int32)
    pool_x8 = jnp.concatenate([pool_x_matrix()] * 8, axis=1)
    sums = jnp.zeros((32, 128), F32)
    count = jnp.zeros((8, 128), F32)
    for yc in range(16):
        voxels, member = [], []
        for q in (64 * zi + 4 * yc + yy for zi in range(2) for yy in range(4)):
            voxels.append(wide[pl.ds(q, 32, stride=128), :].astype(BF))
            row = jnp.broadcast_to(slot_ref[128 * half + q : 128 * half + q + 1, :], (128, 128))
            member.append(jnp.where(row == faces, 1.0, 0.0).astype(BF))
        left = jnp.concatenate([jnp.concatenate(voxels, axis=1), pool_x8], axis=0)
        out = dot(left, jnp.concatenate(member, axis=1), NT)
        sums = sums + out[:32]
        for x4 in range(4):
            part = out[32 + 8 * x4 : 40 + 8 * x4]
            cells[x4, 8 * yc : 8 * yc + 8, :] = part
            count = count + part
    for x4 in range(4):
        cnt_ref[x4 // 2, 128 * (x4 % 2) : 128 * (x4 % 2) + 128, :] = cells[x4].T.astype(BF)
    for x2 in range(2):
        side_ref[pl.ds(16 * x2, 16), :] = cells[x2, pl.ds(0, 16, stride=8), :].astype(BF)
    if half == 0:
        after_ref[256:288] = sums
        after_ref[288:296] = count
    else:
        sums = sums + given_ref[256:288]
        number = jnp.sum(count + given_ref[288:296], axis=0, keepdims=True)
        stacked = jnp.concatenate([jnp.zeros((64, 128), F32), sums, jnp.broadcast_to(number, (32, 128))], axis=0)
        side_ref[pl.ds(32, 16), :] = edge.T[:16].astype(BF)
        lane = iota((128, 128), 1)
        rows = stacked.T
        high = jnp.floor(rows * (1.0 / 256.0)) * 256.0
        rows = jnp.where(lane == 96, high, jnp.where(lane == 98, rows - high, rows))
        after_ref[...] = jnp.where(lane == 97, edge, rows)


def faces(half, emb, slot, given):
    return pl.pallas_call(
        functools.partial(face_kernel, half),
        in_specs=[pl.BlockSpec(memory_space=pltpu.VMEM)] * 3,
        out_specs=[pl.BlockSpec(memory_space=pltpu.VMEM)] * 3,
        out_shape=[
            pltpu.VMEM((2, 256, 128), BF),
            pltpu.VMEM((128 if half else 296, 128), F32),
            pltpu.VMEM((48 if half else 32, 128), BF),
        ],
        scratch_shapes=[pltpu.VMEM((4096, 128), F32), pltpu.VMEM((4, 128, 128), F32)],
        compiler_params=pltpu.CompilerParams(vmem_limit_bytes=16 << 20),
        cost_estimate=pl.CostEstimate(flops=1_000_000, bytes_accessed=10_000, transcendentals=0),
        name="faces",
    )(keep(emb), slot, keep(given) if half else given)


ROWS1 = 6 * 20 * 8
ROWS2 = 4 * 18 * 8
HEAD = 8


def ordered(even, a, b):
    return jnp.where(even, b, a), jnp.where(even, a, b)


def taps_dot(lefts, weights, depth):
    total = None
    per = 256 // depth
    for t in range(0, 9, per):
        group = lefts[t : t + per]
        left = group[0] if len(group) == 1 else jnp.concatenate(group, axis=1)
        term = dot(left, weights[pl.ds(depth * t, depth * len(group)), :])
        total = term if total is None else total + term
    return total


def window(source, tap, z, plane, rows):
    return source[tap % 3 & 1, pl.ds((z + tap // 3) * plane + 16 * (tap % 3 >> 1), rows), :]


def inner_kernel(own_ref, za_ref, zb_ref, ya_ref, yb_ref, w1a_ref, w1b_ref, b1_ref, w2_ref, b2_ref, cnt0_ref,
                 cnt1_ref, fine_ref, sums_ref, ends_ref, near_ref, rim_ref, field, this, mixed, h0f, h1f, h0b, h0n, h1b):
    gz, gy = lax.axis_index("gz"), lax.axis_index("gy")
    z_even, y_even = (gz & 1) == 0, (gy & 1) == 0
    z_low, z_high = ordered(z_even, za_ref[...].astype(F32), zb_ref[...].astype(F32))
    zs = (z_low, own_ref[...].astype(F32), z_high)
    ya, yb = ya_ref[...].astype(F32), yb_ref[...].astype(F32)
    ys = []
    for whole in ordered(y_even, ya, yb):
        low, high = ordered(z_even, whole[0:32], whole[64:96])
        ys.append((low, whole[32:64], high))
    for plane in range(6):
        part, i = plane // 2, plane % 2
        base = HEAD + plane * 160
        field[pl.ds(base, 16), :] = ys[0][part][16 * i : 16 * i + 16]
        field[pl.ds(base + 16, 128), :] = zs[part][128 * i : 128 * i + 128]
        field[pl.ds(base + 144, 16), :] = ys[1][part][16 * i : 16 * i + 16]
        for k, g in enumerate((0, 7)):
            ends_ref[k, pl.ds(24 * plane, 20), :] = field[pl.ds(base + g, 20, stride=8), :]

    lane = iota((160, 128), 1)
    for z in range(6):
        for shift in range(2):
            now = field[pl.ds(HEAD + 160 * z + 8 * shift, 160), :]
            before = field[pl.ds(HEAD + 160 * z + 8 * shift - 1, 160), :]
            this[shift, pl.ds(160 * z, 160), :] = now.astype(BF)
            mixed[shift, pl.ds(160 * z, 160), :] = jnp.where(lane < 64, now, before).astype(BF)

    row = iota((144, 128), 0)
    stay = jnp.where((row < 8) & (gy == 0), 0.0, 1.0)
    stay = jnp.where((row >= 136) & (gy == 3), 0.0, stay)
    b1, b2 = b1_ref[...], b2_ref[...]

    def conv1(source, weights, z):
        lefts = [window(source, tap, z, 160, 144) for tap in range(9)]
        return jnp.maximum(taps_dot(lefts, weights, 128) + b1, 0.0)

    for z in range(4):
        inside = 1.0
        if z == 0:
            inside = jnp.where(gz == 0, 0.0, 1.0)
        if z == 3:
            inside = jnp.where(gz == 7, 0.0, 1.0)
        h0f[pl.ds(144 * z, 144), :] = conv1(mixed, w1b_ref, z) * (stay * inside)
        h1f[pl.ds(144 * z, 144), :] = conv1(this, w1a_ref, z) * (stay * inside)
    for z in range(4):
        for k, g in enumerate((0, 7)):
            near_ref[k, pl.ds(24 * z, 18), :] = h1f[pl.ds(144 * z + g, 18, stride=8), :]
        for shift in range(2):
            at = 144 * z + 8 * shift
            h0b[shift, pl.ds(144 * z, 144), :] = h0f[pl.ds(at, 144), :].astype(BF)
            h0n[shift, pl.ds(144 * z, 144), :] = h0f[pl.ds(at + 1, 144), :].astype(BF)
            h1b[shift, pl.ds(144 * z, 144), :] = h1f[pl.ds(at, 144), :].astype(BF)

    group = iota((128, 128), 0) & 7
    sums = None
    for z in range(2):
        lefts = []
        for tap in range(9):
            h = [window(source, tap, z, 144, 128) for source in (h0b, h1b, h0n)]
            lefts.append(jnp.concatenate([jnp.concatenate(h[p : p + 2], axis=1) for p in range(2)], axis=0))
        both = taps_dot(lefts, w2_ref, 256) + b2
        for p in range(2):
            ctx = jnp.where(group == 7 * p, 0.0, both[128 * p : 128 * p + 128]).astype(BF)
            wide = ctx.astype(F32)
            fine_ref[pl.ds(512 * z + 2 * p, 128, stride=4), :] = wide
            fine_ref[pl.ds(512 * z + 2 * p + 1, 128, stride=4), :] = pltpu.roll(wide, 64, 1)
            term = dot((cnt0_ref, cnt1_ref)[z][p], ctx)
            sums = term if sums is None else sums + term
    sums_ref[...] = sums
    row, col = iota((512, 128), 0), iota((512, 128), 1)
    cell = ((row >> 7) << 4) + ((row & 127) >> 3)
    pick = jnp.where((cell == col) & ((row & 7) == 7 * (row >> 8)), 1.0, 0.0).astype(BF)
    left = jnp.concatenate([cnt0_ref[0], cnt1_ref[0], cnt0_ref[1], cnt1_ref[1]], axis=1)
    rim_ref[...] = dot(left, pick).astype(BF)


def inner(*arrays):
    return pl.pallas_call(
        inner_kernel,
        in_specs=[pl.BlockSpec(memory_space=pltpu.VMEM)] * len(arrays),
        out_specs=[pl.BlockSpec(memory_space=pltpu.VMEM)] * 5,
        out_shape=[
            pltpu.VMEM((1024, 128), F32),
            pltpu.VMEM((256, 128), F32),
            pltpu.VMEM((2, 144, 128), F32),
            pltpu.VMEM((2, 96, 128), F32),
            pltpu.VMEM((256, 128), BF),
        ],
        scratch_shapes=[
            pltpu.VMEM((HEAD + ROWS1 + 8, 128), F32),
            pltpu.VMEM((2, ROWS1, 128), BF),
            pltpu.VMEM((2, ROWS1, 128), BF),
            pltpu.VMEM((ROWS2 + 16, 128), F32),
            pltpu.VMEM((ROWS2 + 16, 128), F32),
            pltpu.VMEM((2, ROWS2, 128), BF),
            pltpu.VMEM((2, ROWS2, 128), BF),
            pltpu.VMEM((2, ROWS2, 128), BF),
        ],
        compiler_params=pltpu.CompilerParams(vmem_limit_bytes=16 << 20),
        cost_estimate=pl.CostEstimate(flops=1_000_000, bytes_accessed=10_000, transcendentals=0),
        name="inner",
    )(*arrays)


def outer_kernel(xb_ref, xa_ref, ends_ref, near_ref, sums_ref, w1a_ref, w1b_ref, b1_ref, w2_ref, b2_ref, rim_ref,
                 face_ref, edge_ref, send_ref, column, hidden):
    gz, gy, gx = (lax.axis_index(a) for a in ("gz", "gy", "gx"))
    z_even, y_even, x_even = (gz & 1) == 0, (gy & 1) == 0, (gx & 1) == 0
    lane = iota((24, 128), 1)
    column[...] = jnp.zeros_like(column)
    got = xb_ref[...].astype(F32)
    for k, whole in enumerate(ordered(x_even, xa_ref[80:208].astype(F32), got[80:208])):
        planes = [whole[20 * i : 20 * i + 20] for i in range(6)]
        low0, high0 = ordered(z_even, planes[0], planes[4])
        low1, high1 = ordered(z_even, planes[1], planes[5])
        for plane, rows in enumerate((low0, low1, planes[2], planes[3], high0, high1)):
            first, last = ordered(y_even, rows[16:18], rows[18:20])
            halo = jnp.concatenate([first, rows[0:16], last, jnp.zeros((4, 128), F32)], axis=0)
            own = ends_ref[k, pl.ds(24 * plane, 24), :]
            left, right = (own, halo) if k == 0 else (halo, own)
            column[k, pl.ds(24 * plane, 24), :] = jnp.where(lane < 64, left, right)
            if k == 1:
                column[2, pl.ds(24 * plane, 24), :] = halo

    row, lane = iota((96, 128), 0), iota((96, 128), 1)
    z_of = jnp.where(row < 24, 0, jnp.where(row < 48, 1, jnp.where(row < 72, 2, 3)))
    y_of = row - 24 * z_of
    gone = ((z_of == 0) & (gz == 0)) | ((z_of == 3) & (gz == 7)) | ((y_of == 0) & (gy == 0)) | ((y_of == 17) & (gy == 3))
    out0 = gone | ((lane < 64) & (gx == 0))
    out1 = gone | ((lane >= 64) & (gx == 7))
    at = [24 * (tap // 3) + tap % 3 for tap in range(9)]
    lefts = [jnp.concatenate([column[k, pl.ds(r, 96), :] for k in range(2)], axis=0).astype(BF) for r in at]
    total = jnp.maximum(taps_dot(lefts, w1b_ref, 128) + b1_ref[...], 0.0)
    lefts = [column[2, pl.ds(r, 96), :].astype(BF) for r in at]
    beyond = jnp.maximum(taps_dot(lefts, w1a_ref, 128) + b1_ref[...], 0.0)
    hidden[0, 0:96] = jnp.where(out0, 0.0, total[0:96])
    hidden[1, 0:96] = near_ref[0]
    hidden[2, 0:96] = near_ref[1]
    hidden[3, 0:96] = jnp.where(out1, 0.0, total[96:192])
    hidden[4, 0:96] = jnp.where(gone, 0.0, beyond)

    lefts = []
    for r in at:
        h = [hidden[k, pl.ds(r, 40), :].astype(BF) for k in range(5)]
        lefts.append(jnp.concatenate([jnp.concatenate([h[k], h[k + 1]], axis=1) for k in (0, 2, 3)], axis=0))
    ctx = (taps_dot(lefts, w2_ref, 256) + b2_ref[...]).astype(BF).astype(F32)
    rows = []
    for k in range(2):
        for z in range(2):
            wide = ctx[40 * k + 24 * z : 40 * k + 24 * z + 16]
            edge_ref[pl.ds(32 * k + 16 * z, 16), :] = wide
            rows.append(jnp.where(gx == 4, 0.0, wide) if k == 0 else wide)
    sums = sums_ref[...] + dot(rim_ref[:, :64], jnp.concatenate(rows, axis=0).astype(BF))
    both = sums[:128] + pltpu.roll(sums[128:], 64, 1)
    lane = iota((128, 128), 1)
    mine = jnp.where(lane < 64, both, face_ref[...]).astype(BF)

    next_ctx = [ctx[80 + 24 * z : 96 + 24 * z] for z in range(2)]
    right = jnp.concatenate([v for c in next_ctx for v in (c, pltpu.roll(c, 64, 1))], axis=0).astype(BF)
    other = dot(got[0:64].T.astype(BF), right)
    edge = jnp.broadcast_to(got[64:65], (128, 128)).T
    other = jnp.where(lane < 64, other, jnp.where(lane == 97, edge, 0.0))
    other = jnp.where(gx == 3, other, 0.0).astype(BF)
    next_ctx = jnp.concatenate(next_ctx, axis=0).astype(BF)
    for d in range(8):
        send_ref[pl.ds(64 * d, 16), :] = mine[16 * d : 16 * d + 16]
        send_ref[pl.ds(64 * d + 16, 16), :] = other[16 * d : 16 * d + 16]
        send_ref[pl.ds(64 * d + 32, 32), :] = next_ctx


def outer(*arrays):
    return pl.pallas_call(
        outer_kernel,
        in_specs=[pl.BlockSpec(memory_space=pltpu.VMEM)] * len(arrays),
        out_specs=[pl.BlockSpec(memory_space=pltpu.VMEM)] * 2,
        out_shape=[pltpu.VMEM((64, 128), F32), pltpu.VMEM((512, 128), BF)],
        scratch_shapes=[pltpu.VMEM((3, 152, 128), F32), pltpu.VMEM((5, 96, 128), F32)],
        compiler_params=pltpu.CompilerParams(vmem_limit_bytes=16 << 20),
        cost_estimate=pl.CostEstimate(flops=200_000_000, bytes_accessed=3_000_000, transcendentals=0),
        name="outer",
    )(*arrays)


def edge_kernel(rows_ref, fine_ref, rim_ref, edge_emb_ref, edge_ctx_ref, out_ref, patch, final, sent):
    patch[...] = fine_ref[...]
    given = lax.axis_index("gx") == 4
    for k, x in enumerate((0, 30)):
        for z in range(2):
            wide = rim_ref[pl.ds(32 * k + 16 * z, 16), :]
            if k == 0:
                wide = jnp.where(given, rows_ref[pl.ds(64 * 3 + 32 + 16 * z, 16), :].astype(F32), wide)
            patch[pl.ds(512 * z + x, 16, stride=32), :] = wide
            patch[pl.ds(512 * z + x + 1, 16, stride=32), :] = pltpu.roll(wide, 64, 1)
    final[...] = patch[...][:, :64].astype(BF)
    copy = pltpu.make_async_copy(final, out_ref, sent)
    copy.start()
    rows = [rows_ref[pl.ds(64 * d + 16 * i, 16), :] for i in range(2) for d in range(8)]
    rows = jnp.concatenate(rows, axis=0).astype(F32)
    hits = jnp.where(rows[:, 97:98] == iota((256, 64), 1).astype(F32), 1.0, 0.0).astype(BF)
    sums = dot(rows.T.astype(BF), hits)
    scale = jnp.maximum(sums[96:97] + sums[98:99], 1.0)
    edge_ctx_ref[...] = sums[:64] / scale
    edge_emb_ref[...] = sums[64:96] / scale
    copy.wait()


def edges(rows, fine, rim):
    return pl.pallas_call(
        edge_kernel,
        in_specs=[pl.BlockSpec(memory_space=pltpu.VMEM)] * 3,
        out_specs=[pl.BlockSpec(memory_space=pltpu.VMEM)] * 2 + [pl.BlockSpec(memory_space=pl.ANY)],
        out_shape=[
            jax.ShapeDtypeStruct((32, 64), F32),
            jax.ShapeDtypeStruct((64, 64), F32),
            jax.ShapeDtypeStruct((1024, 64), BF),
        ],
        scratch_shapes=[pltpu.VMEM((1024, 128), F32), pltpu.VMEM((1024, 64), BF), pltpu.SemaphoreType.DMA],
        name="edges",
    )(keep(rows), keep(fine), keep(rim))


def pairs(first, count):
    return [pair for i in range(first, count - 1, 2) for pair in ((i, i + 1), (i + 1, i))]


def per_device(embedding, face_slot, face_edge, conv1_w, conv1_b, conv2_w, conv2_b):
    emb = embedding.reshape(32, 256, 128)
    gy, gx = lax.axis_index("gy"), lax.axis_index("gx")
    slot = face_slot.reshape(256, 128)
    own, voxels = pool(emb)
    zb = lax.ppermute(own, "gz", pairs(1, 8))
    za = lax.ppermute(own, "gz", pairs(0, 8))
    cnt0, half, side0 = faces(0, voxels, slot, face_edge.reshape(1, 128))
    w1, w2 = jnp.swapaxes(conv1_w, 3, 4).reshape(27, 32, 64), conv2_w.reshape(27, 64, 64)
    zb, za, half = lax.optimization_barrier((zb, za, half))
    planes = [a.reshape(2, 16, 8, 128) for a in (za, own, zb)]
    y_even, x_even = (gy & 1) == 0, (gx & 1) == 0

    def y_edge(high):
        first = jnp.where(high, 14, 0)
        return jnp.concatenate([lax.dynamic_slice_in_dim(a, first, 2, axis=1) for a in planes], axis=0)

    to_a, to_b = lax.optimization_barrier((y_edge(y_even), y_edge(jnp.logical_not(y_even))))
    ya = lax.ppermute(to_a, "gy", pairs(0, 4))
    yb = lax.ppermute(to_b, "gy", pairs(1, 4))
    cnt1, face, side1 = faces(1, voxels, slot, half)
    ya, yb, face = lax.optimization_barrier((ya, yb, face))

    def x_edge(g):
        mid = jnp.concatenate([a[:, :, g] for a in planes], axis=0)
        return jnp.concatenate([mid, ya[:, :, g], yb[:, :, g]], axis=1).reshape(120, 128)

    low, high = x_edge(0), x_edge(7)
    rest = jnp.zeros((8, 128), BF)
    to_b = jnp.concatenate([side0, side1, jnp.where(x_even, low, high), rest], axis=0)
    to_a = jnp.concatenate([side0, side1, jnp.where(x_even, high, low), rest], axis=0)
    to_b, to_a, w1 = lax.optimization_barrier((to_b, to_a, w1))
    w1a, w1b, w2a = bands(w1, w2)
    xa = lax.ppermute(to_a, "gx", pairs(0, 8))
    xb = lax.ppermute(to_b, "gx", [(1, 2), (2, 1), (5, 6), (6, 5), (4, 3)])
    twice = lambda b: jnp.concatenate([b, b]).reshape(1, 128)
    b1, b2 = twice(conv1_b), twice(conv2_b)
    w1a, w1b, w2a, cnt0, cnt1 = (keep(a) for a in (w1a, w1b, w2a, cnt0, cnt1))
    fine, sums, ends, near, rim = inner(
        own, za, zb, ya.reshape(96, 128), yb.reshape(96, 128), w1a, w1b, b1, w2a, b2, cnt0, cnt1
    )
    rim_ctx, send = outer(
        xb, xa, keep(ends), keep(near), keep(sums), w1a, w1b, b1, w2a, b2, keep(rim), keep(face)
    )
    rows = lax.all_to_all(send, "gx", 0, 0, tiled=True)
    edge_emb, edge_ctx, context = edges(rows, fine, rim_ctx)
    context = jnp.transpose(context.reshape(2, 16, 32, 64), (3, 0, 1, 2))
    return (context, edge_emb, edge_ctx)


def solution(mesh):
    in_specs = (P(None, "gz", "gy", "gx"), P("gz", "gy", "gx"), P(("gz", "gy", "gx")), P(), P(), P(), P())
    out_specs = (P(None, "gz", "gy", "gx"), P(None, ("gz", "gy", "gx")), P(None, ("gz", "gy", "gx")))
    return jax.shard_map(per_device, mesh=mesh, in_specs=in_specs, out_specs=out_specs, check_vma=False)
```

```python
import functools

import jax
import jax.numpy as jnp
from jax import lax
from jax.experimental import pallas as pl
from jax.experimental.pallas import tpu as pltpu
from jax.sharding import PartitionSpec as P

BF = jnp.bfloat16
F32 = jnp.float32
NT = (((1,), (1,)), ((), ()))
NN = (((1,), (0,)), ((), ()))


def dot(a, b, dims=NN):
    return lax.dot_general(a, b, dims, preferred_element_type=F32)


def keep(array):
    return pltpu.with_memory_space_constraint(array, pltpu.VMEM)


def iota(shape, dim):
    return lax.broadcasted_iota(jnp.int32, shape, dim)


def split3(x):
    hi = x.astype(BF)
    rest = x - hi.astype(F32)
    mid = rest.astype(BF)
    low = (rest - mid.astype(F32)).astype(BF)
    return hi, mid, low


def pool_x_matrix():
    row, col = iota((32, 128), 0), iota((32, 128), 1)
    cell = 4 * (row & 7) + (row >> 3)
    return jnp.where((col >> 2) == cell, 1.0, 0.0).astype(BF)


def pool_kernel(emb_ref, out_ref, block, sums, arrived):
    chunks = arrived.shape[0]
    per = 32 // chunks
    copies = [
        pltpu.make_async_copy(emb_ref.at[pl.ds(per * i, per)], block.at[pl.ds(per * i, per)], arrived.at[i])
        for i in range(chunks)
    ]
    for copy in copies:
        copy.start()
    row, col = iota((32, 256), 0), iota((32, 256), 1)
    cell = ((col >> 7) << 4) + ((col & 63) >> 2)
    pool_zy = jnp.where(cell == row, 1.0, 0.0).astype(BF)
    pool_x = jnp.concatenate([pool_x_matrix()] * 3, axis=1)
    lane = iota((8, 128), 1)
    far, near = lane < 64, (lane & 32) == 0
    for i in range(chunks):
        copies[i].wait()
        for c in range(per * i, per * i + per):
            sums[pl.ds(32 * c, 32), :] = dot(pool_zy, block[c])
    for part in range(8):
        rows = jnp.concatenate([sums[pl.ds(4 * part + i, 32, stride=32), :] for i in range(4)], axis=0)
        cells = dot(pool_x, jnp.concatenate(split3(rows), axis=1), NT) * (1.0 / 32.0)
        v = [cells[8 * i : 8 * i + 8] for i in range(4)]
        a = [jnp.where(far, v[i], pltpu.roll(v[i + 2], 64, 1)) for i in range(2)]
        b = [jnp.where(far, pltpu.roll(v[i], 64, 1), v[i + 2]) for i in range(2)]
        done = []
        for lo, hi in (a, b):
            done.append(jnp.where(near, lo, pltpu.roll(hi, 32, 1)))
            done.append(jnp.where(near, pltpu.roll(lo, 96, 1), hi))
        out_ref[pl.ds(32 * part, 32), :] = jnp.concatenate(done, axis=0).astype(BF)


def pool(emb):
    chunks = 2
    return pl.pallas_call(
        pool_kernel,
        in_specs=[pl.BlockSpec(memory_space=pl.ANY)],
        out_specs=[pl.BlockSpec(memory_space=pltpu.VMEM)] * 2,
        out_shape=[pltpu.VMEM((256, 128), BF), pltpu.VMEM((32, 256, 128), BF)],
        scratch_shapes=[
            pltpu.VMEM((1024, 128), F32),
            pltpu.SemaphoreType.DMA((chunks,)),
        ],
        compiler_params=pltpu.CompilerParams(vmem_limit_bytes=32 << 20),
        cost_estimate=pl.CostEstimate(flops=80_000_000, bytes_accessed=2_200_000, transcendentals=0),
        name="pool",
    )(pltpu.with_memory_space_constraint(emb, pltpu.HBM))


def banded(tap, taps):
    zero = jnp.zeros_like(taps(tap, 0))
    w = [taps(tap, k) if 0 <= k < 3 else zero for k in range(-1, 4)]
    return [jnp.concatenate([w[k + 1], w[k]], axis=1) for k in range(4)]


def bands_kernel(w1_ref, w2_ref, w1a_ref, w1b_ref, w2a_ref):
    for tap in range(9):
        bands = banded(tap, lambda t, k: w1_ref[3 * t + k])
        w1a_ref[pl.ds(128 * tap, 128), :] = jnp.concatenate(bands, axis=0)
        w1b_ref[pl.ds(128 * tap, 128), :] = jnp.concatenate(bands[2:] + bands[:2], axis=0)
        bands = banded(tap, lambda t, k: w2_ref[3 * t + k].astype(F32).T.astype(BF))
        w2a_ref[pl.ds(256 * tap, 256), :] = jnp.concatenate(bands, axis=0)


def bands(w1, w2):
    return pl.pallas_call(
        bands_kernel,
        in_specs=[pl.BlockSpec(memory_space=pltpu.VMEM)] * 2,
        out_specs=[pl.BlockSpec(memory_space=pltpu.VMEM)] * 3,
        out_shape=[pltpu.VMEM((1152, 128), BF), pltpu.VMEM((1152, 128), BF), pltpu.VMEM((2304, 128), BF)],
        compiler_params=pltpu.CompilerParams(vmem_limit_bytes=16 << 20),
        cost_estimate=pl.CostEstimate(flops=1_000_000, bytes_accessed=10_000, transcendentals=0),
        name="bands",
    )(w1, w2)


def ordering(edge):
    i0, i1 = iota((128, 128), 0), iota((128, 128), 1)
    label = jnp.broadcast_to(edge, (128, 128))
    owner = ((label >> 6) & 7).astype(F32)
    local = (label & 63).astype(F32)
    ahead = jnp.where((owner == owner.T) & (i0 < i1), 1.0, 0.0)
    place = owner[0:1, :] * 16.0 + jnp.sum(ahead, axis=0, keepdims=True)
    chosen = place == i0.astype(F32)
    face = jnp.sum(jnp.where(chosen, i1.astype(F32), 0.0), axis=1, keepdims=True)
    edge = jnp.sum(jnp.where(chosen, local, 0.0), axis=1, keepdims=True)
    return jnp.broadcast_to(face, (128, 128)), jnp.broadcast_to(edge, (128, 128))


def face_kernel(half, emb_ref, slot_ref, given_ref, *refs):
    cnt_ref, after_ref, side_ref, wide, cells = refs
    wide[...] = emb_ref[:, pl.ds(128 * half, 128), :].astype(F32).reshape(4096, 128)
    if half == 0:
        face, edge = ordering(given_ref[...])
        after_ref[0:128] = face
        after_ref[128:256] = edge
    else:
        face, edge = given_ref[0:128], given_ref[128:256]
    faces = face.astype(jnp.int32)
    pool_x8 = jnp.concatenate([pool_x_matrix()] * 8, axis=1)
    sums = jnp.zeros((32, 128), F32)
    count = jnp.zeros((8, 128), F32)
    for yc in range(16):
        voxels, member = [], []
        for q in (64 * zi + 4 * yc + yy for zi in range(2) for yy in range(4)):
            voxels.append(wide[pl.ds(q, 32, stride=128), :].astype(BF))
            row = jnp.broadcast_to(slot_ref[128 * half + q : 128 * half + q + 1, :], (128, 128))
            member.append(jnp.where(row == faces, 1.0, 0.0).astype(BF))
        left = jnp.concatenate([jnp.concatenate(voxels, axis=1), pool_x8], axis=0)
        out = dot(left, jnp.concatenate(member, axis=1), NT)
        sums = sums + out[:32]
        for x4 in range(4):
            part = out[32 + 8 * x4 : 40 + 8 * x4]
            cells[x4, 8 * yc : 8 * yc + 8, :] = part
            count = count + part
    for x4 in range(4):
        cnt_ref[x4 // 2, 128 * (x4 % 2) : 128 * (x4 % 2) + 128, :] = cells[x4].T.astype(BF)
    for x2 in range(2):
        side_ref[pl.ds(16 * x2, 16), :] = cells[x2, pl.ds(0, 16, stride=8), :].astype(BF)
    if half == 0:
        after_ref[256:288] = sums
        after_ref[288:296] = count
    else:
        sums = sums + given_ref[256:288]
        number = jnp.sum(count + given_ref[288:296], axis=0, keepdims=True)
        stacked = jnp.concatenate([jnp.zeros((64, 128), F32), sums, jnp.broadcast_to(number, (32, 128))], axis=0)
        side_ref[pl.ds(32, 16), :] = edge.T[:16].astype(BF)
        lane = iota((128, 128), 1)
        rows = stacked.T
        high = jnp.floor(rows * (1.0 / 256.0)) * 256.0
        rows = jnp.where(lane == 96, high, jnp.where(lane == 98, rows - high, rows))
        after_ref[...] = jnp.where(lane == 97, edge, rows)


def faces(half, emb, slot, given):
    return pl.pallas_call(
        functools.partial(face_kernel, half),
        in_specs=[pl.BlockSpec(memory_space=pltpu.VMEM)] * 3,
        out_specs=[pl.BlockSpec(memory_space=pltpu.VMEM)] * 3,
        out_shape=[
            pltpu.VMEM((2, 256, 128), BF),
            pltpu.VMEM((128 if half else 296, 128), F32),
            pltpu.VMEM((48 if half else 32, 128), BF),
        ],
        scratch_shapes=[pltpu.VMEM((4096, 128), F32), pltpu.VMEM((4, 128, 128), F32)],
        compiler_params=pltpu.CompilerParams(vmem_limit_bytes=16 << 20),
        cost_estimate=pl.CostEstimate(flops=1_000_000, bytes_accessed=10_000, transcendentals=0),
        name="faces",
    )(keep(emb), slot, keep(given) if half else given)


ROWS1 = 6 * 20 * 8
ROWS2 = 4 * 18 * 8
HEAD = 8


def ordered(even, a, b):
    return jnp.where(even, b, a), jnp.where(even, a, b)


def taps_dot(lefts, weights, depth):
    total = None
    per = 256 // depth
    for t in range(0, 9, per):
        group = lefts[t : t + per]
        left = group[0] if len(group) == 1 else jnp.concatenate(group, axis=1)
        term = dot(left, weights[pl.ds(depth * t, depth * len(group)), :])
        total = term if total is None else total + term
    return total


def window(source, tap, z, plane, rows):
    return source[tap % 3 & 1, pl.ds((z + tap // 3) * plane + 16 * (tap % 3 >> 1), rows), :]


def inner_kernel(own_ref, za_ref, zb_ref, ya_ref, yb_ref, w1a_ref, w1b_ref, b1_ref, w2_ref, b2_ref, cnt0_ref,
                 cnt1_ref, fine_ref, sums_ref, ends_ref, near_ref, rim_ref, field, this, mixed, h0f, h1f, h0b, h0n, h1b):
    gz, gy = lax.axis_index("gz"), lax.axis_index("gy")
    z_even, y_even = (gz & 1) == 0, (gy & 1) == 0
    z_low, z_high = ordered(z_even, za_ref[...].astype(F32), zb_ref[...].astype(F32))
    zs = (z_low, own_ref[...].astype(F32), z_high)
    ya, yb = ya_ref[...].astype(F32), yb_ref[...].astype(F32)
    ys = []
    for whole in ordered(y_even, ya, yb):
        low, high = ordered(z_even, whole[0:32], whole[64:96])
        ys.append((low, whole[32:64], high))
    for plane in range(6):
        part, i = plane // 2, plane % 2
        base = HEAD + plane * 160
        field[pl.ds(base, 16), :] = ys[0][part][16 * i : 16 * i + 16]
        field[pl.ds(base + 16, 128), :] = zs[part][128 * i : 128 * i + 128]
        field[pl.ds(base + 144, 16), :] = ys[1][part][16 * i : 16 * i + 16]
        for k, g in enumerate((0, 7)):
            ends_ref[k, pl.ds(24 * plane, 20), :] = field[pl.ds(base + g, 20, stride=8), :]

    lane = iota((160, 128), 1)
    for z in range(6):
        for shift in range(2):
            now = field[pl.ds(HEAD + 160 * z + 8 * shift, 160), :]
            before = field[pl.ds(HEAD + 160 * z + 8 * shift - 1, 160), :]
            this[shift, pl.ds(160 * z, 160), :] = now.astype(BF)
            mixed[shift, pl.ds(160 * z, 160), :] = jnp.where(lane < 64, now, before).astype(BF)

    row = iota((144, 128), 0)
    stay = jnp.where((row < 8) & (gy == 0), 0.0, 1.0)
    stay = jnp.where((row >= 136) & (gy == 3), 0.0, stay)
    b1, b2 = b1_ref[...], b2_ref[...]

    def conv1(source, weights, z):
        lefts = [window(source, tap, z, 160, 144) for tap in range(9)]
        return jnp.maximum(taps_dot(lefts, weights, 128) + b1, 0.0)

    for z in range(4):
        inside = 1.0
        if z == 0:
            inside = jnp.where(gz == 0, 0.0, 1.0)
        if z == 3:
            inside = jnp.where(gz == 7, 0.0, 1.0)
        h0f[pl.ds(144 * z, 144), :] = conv1(mixed, w1b_ref, z) * (stay * inside)
        h1f[pl.ds(144 * z, 144), :] = conv1(this, w1a_ref, z) * (stay * inside)
    for z in range(4):
        for k, g in enumerate((0, 7)):
            near_ref[k, pl.ds(24 * z, 18), :] = h1f[pl.ds(144 * z + g, 18, stride=8), :]
        for shift in range(2):
            at = 144 * z + 8 * shift
            h0b[shift, pl.ds(144 * z, 144), :] = h0f[pl.ds(at, 144), :].astype(BF)
            h0n[shift, pl.ds(144 * z, 144), :] = h0f[pl.ds(at + 1, 144), :].astype(BF)
            h1b[shift, pl.ds(144 * z, 144), :] = h1f[pl.ds(at, 144), :].astype(BF)

    group = iota((128, 128), 0) & 7
    sums = None
    for z in range(2):
        lefts = []
        for tap in range(9):
            h = [window(source, tap, z, 144, 128) for source in (h0b, h1b, h0n)]
            lefts.append(jnp.concatenate([jnp.concatenate(h[p : p + 2], axis=1) for p in range(2)], axis=0))
        both = taps_dot(lefts, w2_ref, 256) + b2
        for p in range(2):
            ctx = jnp.where(group == 7 * p, 0.0, both[128 * p : 128 * p + 128]).astype(BF)
            wide = ctx.astype(F32)
            fine_ref[pl.ds(512 * z + 2 * p, 128, stride=4), :] = wide
            fine_ref[pl.ds(512 * z + 2 * p + 1, 128, stride=4), :] = pltpu.roll(wide, 64, 1)
            term = dot((cnt0_ref, cnt1_ref)[z][p], ctx)
            sums = term if sums is None else sums + term
    sums_ref[...] = sums
    row, col = iota((512, 128), 0), iota((512, 128), 1)
    cell = ((row >> 7) << 4) + ((row & 127) >> 3)
    pick = jnp.where((cell == col) & ((row & 7) == 7 * (row >> 8)), 1.0, 0.0).astype(BF)
    left = jnp.concatenate([cnt0_ref[0], cnt1_ref[0], cnt0_ref[1], cnt1_ref[1]], axis=1)
    rim_ref[...] = dot(left, pick).astype(BF)


def inner(*arrays):
    return pl.pallas_call(
        inner_kernel,
        in_specs=[pl.BlockSpec(memory_space=pltpu.VMEM)] * len(arrays),
        out_specs=[pl.BlockSpec(memory_space=pltpu.VMEM)] * 5,
        out_shape=[
            pltpu.VMEM((1024, 128), F32),
            pltpu.VMEM((256, 128), F32),
            pltpu.VMEM((2, 144, 128), F32),
            pltpu.VMEM((2, 96, 128), F32),
            pltpu.VMEM((256, 128), BF),
        ],
        scratch_shapes=[
            pltpu.VMEM((HEAD + ROWS1 + 8, 128), F32),
            pltpu.VMEM((2, ROWS1, 128), BF),
            pltpu.VMEM((2, ROWS1, 128), BF),
            pltpu.VMEM((ROWS2 + 16, 128), F32),
            pltpu.VMEM((ROWS2 + 16, 128), F32),
            pltpu.VMEM((2, ROWS2, 128), BF),
            pltpu.VMEM((2, ROWS2, 128), BF),
            pltpu.VMEM((2, ROWS2, 128), BF),
        ],
        compiler_params=pltpu.CompilerParams(vmem_limit_bytes=16 << 20),
        cost_estimate=pl.CostEstimate(flops=1_000_000, bytes_accessed=10_000, transcendentals=0),
        name="inner",
    )(*arrays)


def outer_kernel(xb_ref, xa_ref, ends_ref, near_ref, sums_ref, w1a_ref, w1b_ref, b1_ref, w2_ref, b2_ref, rim_ref,
                 face_ref, edge_ref, send_ref, column, hidden):
    gz, gy, gx = (lax.axis_index(a) for a in ("gz", "gy", "gx"))
    z_even, y_even, x_even = (gz & 1) == 0, (gy & 1) == 0, (gx & 1) == 0
    lane = iota((24, 128), 1)
    column[...] = jnp.zeros_like(column)
    got = xb_ref[...].astype(F32)
    for k, whole in enumerate(ordered(x_even, xa_ref[80:208].astype(F32), got[80:208])):
        planes = [whole[20 * i : 20 * i + 20] for i in range(6)]
        low0, high0 = ordered(z_even, planes[0], planes[4])
        low1, high1 = ordered(z_even, planes[1], planes[5])
        for plane, rows in enumerate((low0, low1, planes[2], planes[3], high0, high1)):
            first, last = ordered(y_even, rows[16:18], rows[18:20])
            halo = jnp.concatenate([first, rows[0:16], last, jnp.zeros((4, 128), F32)], axis=0)
            own = ends_ref[k, pl.ds(24 * plane, 24), :]
            left, right = (own, halo) if k == 0 else (halo, own)
            column[k, pl.ds(24 * plane, 24), :] = jnp.where(lane < 64, left, right)
            if k == 1:
                column[2, pl.ds(24 * plane, 24), :] = halo

    row, lane = iota((96, 128), 0), iota((96, 128), 1)
    z_of = jnp.where(row < 24, 0, jnp.where(row < 48, 1, jnp.where(row < 72, 2, 3)))
    y_of = row - 24 * z_of
    gone = ((z_of == 0) & (gz == 0)) | ((z_of == 3) & (gz == 7)) | ((y_of == 0) & (gy == 0)) | ((y_of == 17) & (gy == 3))
    out0 = gone | ((lane < 64) & (gx == 0))
    out1 = gone | ((lane >= 64) & (gx == 7))
    at = [24 * (tap // 3) + tap % 3 for tap in range(9)]
    lefts = [jnp.concatenate([column[k, pl.ds(r, 96), :] for k in range(2)], axis=0).astype(BF) for r in at]
    total = jnp.maximum(taps_dot(lefts, w1b_ref, 128) + b1_ref[...], 0.0)
    lefts = [column[2, pl.ds(r, 96), :].astype(BF) for r in at]
    beyond = jnp.maximum(taps_dot(lefts, w1a_ref, 128) + b1_ref[...], 0.0)
    hidden[0, 0:96] = jnp.where(out0, 0.0, total[0:96])
    hidden[1, 0:96] = near_ref[0]
    hidden[2, 0:96] = near_ref[1]
    hidden[3, 0:96] = jnp.where(out1, 0.0, total[96:192])
    hidden[4, 0:96] = jnp.where(gone, 0.0, beyond)

    lefts = []
    for r in at:
        h = [hidden[k, pl.ds(r, 40), :].astype(BF) for k in range(5)]
        lefts.append(jnp.concatenate([jnp.concatenate([h[k], h[k + 1]], axis=1) for k in (0, 2, 3)], axis=0))
    ctx = (taps_dot(lefts, w2_ref, 256) + b2_ref[...]).astype(BF).astype(F32)
    rows = []
    for k in range(2):
        for z in range(2):
            wide = ctx[40 * k + 24 * z : 40 * k + 24 * z + 16]
            edge_ref[pl.ds(32 * k + 16 * z, 16), :] = wide
            rows.append(jnp.where(gx == 4, 0.0, wide) if k == 0 else wide)
    sums = sums_ref[...] + dot(rim_ref[:, :64], jnp.concatenate(rows, axis=0).astype(BF))
    both = sums[:128] + pltpu.roll(sums[128:], 64, 1)
    lane = iota((128, 128), 1)
    mine = jnp.where(lane < 64, both, face_ref[...]).astype(BF)

    next_ctx = [ctx[80 + 24 * z : 96 + 24 * z] for z in range(2)]
    right = jnp.concatenate([v for c in next_ctx for v in (c, pltpu.roll(c, 64, 1))], axis=0).astype(BF)
    other = dot(got[0:64].T.astype(BF), right)
    edge = jnp.broadcast_to(got[64:65], (128, 128)).T
    other = jnp.where(lane < 64, other, jnp.where(lane == 97, edge, 0.0))
    other = jnp.where(gx == 3, other, 0.0).astype(BF)
    next_ctx = jnp.concatenate(next_ctx, axis=0).astype(BF)
    for d in range(8):
        send_ref[pl.ds(64 * d, 16), :] = mine[16 * d : 16 * d + 16]
        send_ref[pl.ds(64 * d + 16, 16), :] = other[16 * d : 16 * d + 16]
        send_ref[pl.ds(64 * d + 32, 32), :] = next_ctx


def outer(*arrays):
    return pl.pallas_call(
        outer_kernel,
        in_specs=[pl.BlockSpec(memory_space=pltpu.VMEM)] * len(arrays),
        out_specs=[pl.BlockSpec(memory_space=pltpu.VMEM)] * 2,
        out_shape=[pltpu.VMEM((64, 128), F32), pltpu.VMEM((512, 128), BF)],
        scratch_shapes=[pltpu.VMEM((3, 152, 128), F32), pltpu.VMEM((5, 96, 128), F32)],
        compiler_params=pltpu.CompilerParams(vmem_limit_bytes=16 << 20),
        cost_estimate=pl.CostEstimate(flops=200_000_000, bytes_accessed=3_000_000, transcendentals=0),
        name="outer",
    )(*arrays)


def edge_kernel(rows_ref, fine_ref, rim_ref, edge_emb_ref, edge_ctx_ref, out_ref, field, final, sent):
    given = lax.axis_index("gx") == 4
    copies = []
    for z in range(2):
        half = pl.ds(512 * z, 512)
        field[half, :] = fine_ref[half, :]
        for k, x in enumerate((0, 30)):
            wide = rim_ref[pl.ds(32 * k + 16 * z, 16), :]
            if k == 0:
                wide = jnp.where(given, rows_ref[pl.ds(64 * 3 + 32 + 16 * z, 16), :].astype(F32), wide)
            field[pl.ds(512 * z + x, 16, stride=32), :] = wide
            field[pl.ds(512 * z + x + 1, 16, stride=32), :] = pltpu.roll(wide, 64, 1)
        final[half, :] = field[half, :][:, :64].astype(BF)
        copies.append(pltpu.make_async_copy(final.at[half], out_ref.at[half], sent.at[z]))
        copies[z].start()
    rows = [rows_ref[pl.ds(64 * d + 16 * i, 16), :] for i in range(2) for d in range(8)]
    rows = jnp.concatenate(rows, axis=0).astype(F32)
    hits = jnp.where(rows[:, 97:98] == iota((256, 64), 1).astype(F32), 1.0, 0.0).astype(BF)
    sums = dot(rows.T.astype(BF), hits)
    scale = jnp.maximum(sums[96:97] + sums[98:99], 1.0)
    edge_ctx_ref[...] = sums[:64] / scale
    edge_emb_ref[...] = sums[64:96] / scale
    for copy in copies:
        copy.wait()


def edges(rows, fine, rim):
    return pl.pallas_call(
        edge_kernel,
        in_specs=[pl.BlockSpec(memory_space=pltpu.VMEM)] * 3,
        out_specs=[pl.BlockSpec(memory_space=pltpu.VMEM)] * 2 + [pl.BlockSpec(memory_space=pl.ANY)],
        out_shape=[
            jax.ShapeDtypeStruct((32, 64), F32),
            jax.ShapeDtypeStruct((64, 64), F32),
            jax.ShapeDtypeStruct((1024, 64), BF),
        ],
        scratch_shapes=[pltpu.VMEM((1024, 128), F32), pltpu.VMEM((1024, 64), BF), pltpu.SemaphoreType.DMA((2,))],
        name="edges",
    )(keep(rows), keep(fine), keep(rim))


def pairs(first, count):
    return [pair for i in range(first, count - 1, 2) for pair in ((i, i + 1), (i + 1, i))]


def per_device(embedding, face_slot, face_edge, conv1_w, conv1_b, conv2_w, conv2_b):
    emb = embedding.reshape(32, 256, 128)
    gy, gx = lax.axis_index("gy"), lax.axis_index("gx")
    slot = face_slot.reshape(256, 128)
    own, voxels = pool(emb)
    zb = lax.ppermute(own, "gz", pairs(1, 8))
    za = lax.ppermute(own, "gz", pairs(0, 8))
    cnt0, half, side0 = faces(0, voxels, slot, face_edge.reshape(1, 128))
    w1, w2 = jnp.swapaxes(conv1_w, 3, 4).reshape(27, 32, 64), conv2_w.reshape(27, 64, 64)
    zb, za, half = lax.optimization_barrier((zb, za, half))
    planes = [a.reshape(2, 16, 8, 128) for a in (za, own, zb)]
    y_even, x_even = (gy & 1) == 0, (gx & 1) == 0

    def y_edge(high):
        first = jnp.where(high, 14, 0)
        return jnp.concatenate([lax.dynamic_slice_in_dim(a, first, 2, axis=1) for a in planes], axis=0)

    to_a, to_b = lax.optimization_barrier((y_edge(y_even), y_edge(jnp.logical_not(y_even))))
    ya = lax.ppermute(to_a, "gy", pairs(0, 4))
    yb = lax.ppermute(to_b, "gy", pairs(1, 4))
    cnt1, face, side1 = faces(1, voxels, slot, half)
    ya, yb, face = lax.optimization_barrier((ya, yb, face))

    def x_edge(g):
        mid = jnp.concatenate([a[:, :, g] for a in planes], axis=0)
        return jnp.concatenate([mid, ya[:, :, g], yb[:, :, g]], axis=1).reshape(120, 128)

    low, high = x_edge(0), x_edge(7)
    rest = jnp.zeros((8, 128), BF)
    to_b = jnp.concatenate([side0, side1, jnp.where(x_even, low, high), rest], axis=0)
    to_a = jnp.concatenate([side0, side1, jnp.where(x_even, high, low), rest], axis=0)
    to_b, w1 = lax.optimization_barrier((to_b, w1))
    w1a, w1b, w2a = bands(w1, w2)
    xa = lax.ppermute(to_a, "gx", pairs(0, 8))
    xb = lax.ppermute(to_b, "gx", [(1, 2), (2, 1), (5, 6), (6, 5), (4, 3)])
    twice = lambda b: jnp.concatenate([b, b]).reshape(1, 128)
    b1, b2 = twice(conv1_b), twice(conv2_b)
    w1a, w1b, w2a, cnt0, cnt1 = (keep(a) for a in (w1a, w1b, w2a, cnt0, cnt1))
    fine, sums, ends, near, rim = inner(
        own, za, zb, ya.reshape(96, 128), yb.reshape(96, 128), w1a, w1b, b1, w2a, b2, cnt0, cnt1
    )
    rim_ctx, send = outer(
        xb, xa, keep(ends), keep(near), keep(sums), w1a, w1b, b1, w2a, b2, keep(rim), keep(face)
    )
    rows = lax.all_to_all(send, "gx", 0, 0, tiled=True)
    edge_emb, edge_ctx, context = edges(rows, fine, rim_ctx)
    context = jnp.transpose(context.reshape(2, 16, 32, 64), (3, 0, 1, 2))
    return (context, edge_emb, edge_ctx)


def solution(mesh):
    in_specs = (P(None, "gz", "gy", "gx"), P("gz", "gy", "gx"), P(("gz", "gy", "gx")), P(), P(), P(), P())
    out_specs = (P(None, "gz", "gy", "gx"), P(None, ("gz", "gy", "gx")), P(None, ("gz", "gy", "gx")))
    return jax.shard_map(per_device, mesh=mesh, in_specs=in_specs, out_specs=out_specs, check_vma=False)
```

```python
import functools

import jax
import jax.numpy as jnp
from jax import lax
from jax.experimental import pallas as pl
from jax.experimental.pallas import tpu as pltpu
from jax.sharding import PartitionSpec as P

BF = jnp.bfloat16
F32 = jnp.float32
NT = (((1,), (1,)), ((), ()))
NN = (((1,), (0,)), ((), ()))


def dot(a, b, dims=NN):
    return lax.dot_general(a, b, dims, preferred_element_type=F32)


def keep(array):
    return pltpu.with_memory_space_constraint(array, pltpu.VMEM)


def iota(shape, dim):
    return lax.broadcasted_iota(jnp.int32, shape, dim)


def split3(x):
    hi = x.astype(BF)
    rest = x - hi.astype(F32)
    mid = rest.astype(BF)
    low = (rest - mid.astype(F32)).astype(BF)
    return hi, mid, low


def pool_x_matrix():
    row, col = iota((32, 128), 0), iota((32, 128), 1)
    cell = 4 * (row & 7) + (row >> 3)
    return jnp.where((col >> 2) == cell, 1.0, 0.0).astype(BF)


def pool_kernel(emb_ref, out_ref, block, sums, arrived):
    chunks = arrived.shape[0]
    per = 32 // chunks
    copies = [
        pltpu.make_async_copy(emb_ref.at[pl.ds(per * i, per)], block.at[pl.ds(per * i, per)], arrived.at[i])
        for i in range(chunks)
    ]
    for copy in copies:
        copy.start()
    row, col = iota((32, 256), 0), iota((32, 256), 1)
    cell = ((col >> 7) << 4) + ((col & 63) >> 2)
    pool_zy = jnp.where(cell == row, 1.0, 0.0).astype(BF)
    pool_x = jnp.concatenate([pool_x_matrix()] * 3, axis=1)
    lane = iota((8, 128), 1)
    far, near = lane < 64, (lane & 32) == 0
    for i in range(chunks):
        copies[i].wait()
        for c in range(per * i, per * i + per):
            sums[pl.ds(32 * c, 32), :] = dot(pool_zy, block[c])
    for part in range(8):
        rows = jnp.concatenate([sums[pl.ds(4 * part + i, 32, stride=32), :] for i in range(4)], axis=0)
        cells = dot(pool_x, jnp.concatenate(split3(rows), axis=1), NT) * (1.0 / 32.0)
        v = [cells[8 * i : 8 * i + 8] for i in range(4)]
        a = [jnp.where(far, v[i], pltpu.roll(v[i + 2], 64, 1)) for i in range(2)]
        b = [jnp.where(far, pltpu.roll(v[i], 64, 1), v[i + 2]) for i in range(2)]
        done = []
        for lo, hi in (a, b):
            done.append(jnp.where(near, lo, pltpu.roll(hi, 32, 1)))
            done.append(jnp.where(near, pltpu.roll(lo, 96, 1), hi))
        out_ref[pl.ds(32 * part, 32), :] = jnp.concatenate(done, axis=0).astype(BF)


def pool(emb):
    chunks = 2
    return pl.pallas_call(
        pool_kernel,
        in_specs=[pl.BlockSpec(memory_space=pl.ANY)],
        out_specs=[pl.BlockSpec(memory_space=pltpu.VMEM)] * 2,
        out_shape=[pltpu.VMEM((256, 128), BF), pltpu.VMEM((32, 256, 128), BF)],
        scratch_shapes=[
            pltpu.VMEM((1024, 128), F32),
            pltpu.SemaphoreType.DMA((chunks,)),
        ],
        compiler_params=pltpu.CompilerParams(vmem_limit_bytes=32 << 20),
        cost_estimate=pl.CostEstimate(flops=80_000_000, bytes_accessed=2_200_000, transcendentals=0),
        name="pool",
    )(pltpu.with_memory_space_constraint(emb, pltpu.HBM))


def banded(tap, taps):
    zero = jnp.zeros_like(taps(tap, 0))
    w = [taps(tap, k) if 0 <= k < 3 else zero for k in range(-1, 4)]
    return [jnp.concatenate([w[k + 1], w[k]], axis=1) for k in range(4)]


def bands_kernel(w1_ref, w2_ref, w1a_ref, w1b_ref, w2a_ref):
    for tap in range(9):
        bands = banded(tap, lambda t, k: w1_ref[3 * t + k])
        w1a_ref[pl.ds(128 * tap, 128), :] = jnp.concatenate(bands, axis=0)
        w1b_ref[pl.ds(128 * tap, 128), :] = jnp.concatenate(bands[2:] + bands[:2], axis=0)
        bands = banded(tap, lambda t, k: w2_ref[3 * t + k].astype(F32).T.astype(BF))
        w2a_ref[pl.ds(256 * tap, 256), :] = jnp.concatenate(bands, axis=0)


def bands(w1, w2):
    return pl.pallas_call(
        bands_kernel,
        in_specs=[pl.BlockSpec(memory_space=pltpu.VMEM)] * 2,
        out_specs=[pl.BlockSpec(memory_space=pltpu.VMEM)] * 3,
        out_shape=[pltpu.VMEM((1152, 128), BF), pltpu.VMEM((1152, 128), BF), pltpu.VMEM((2304, 128), BF)],
        compiler_params=pltpu.CompilerParams(vmem_limit_bytes=16 << 20),
        cost_estimate=pl.CostEstimate(flops=1_000_000, bytes_accessed=10_000, transcendentals=0),
        name="bands",
    )(w1, w2)


def ordering(edge):
    i0, i1 = iota((128, 128), 0), iota((128, 128), 1)
    label = jnp.broadcast_to(edge, (128, 128))
    owner = ((label >> 6) & 7).astype(F32)
    local = (label & 63).astype(F32)
    ahead = jnp.where((owner == owner.T) & (i0 < i1), 1.0, 0.0)
    place = owner[0:1, :] * 16.0 + jnp.sum(ahead, axis=0, keepdims=True)
    chosen = place == i0.astype(F32)
    face = jnp.sum(jnp.where(chosen, i1.astype(F32), 0.0), axis=1, keepdims=True)
    edge = jnp.sum(jnp.where(chosen, local, 0.0), axis=1, keepdims=True)
    return jnp.broadcast_to(face, (128, 128)), jnp.broadcast_to(edge, (128, 128))


def face_kernel(half, emb_ref, slot_ref, given_ref, *refs):
    cnt_ref, after_ref, side_ref, wide, cells = refs
    wide[...] = emb_ref[:, pl.ds(128 * half, 128), :].astype(F32).reshape(4096, 128)
    if half == 0:
        face, edge = ordering(given_ref[...])
        after_ref[0:128] = face
        after_ref[128:256] = edge
    else:
        face, edge = given_ref[0:128], given_ref[128:256]
    faces = face.astype(jnp.int32)
    pool_x8 = jnp.concatenate([pool_x_matrix()] * 8, axis=1)
    sums = jnp.zeros((32, 128), F32)
    count = jnp.zeros((8, 128), F32)
    for yc in range(16):
        voxels, member = [], []
        for q in (64 * zi + 4 * yc + yy for zi in range(2) for yy in range(4)):
            voxels.append(wide[pl.ds(q, 32, stride=128), :].astype(BF))
            row = jnp.broadcast_to(slot_ref[128 * half + q : 128 * half + q + 1, :], (128, 128))
            member.append(jnp.where(row == faces, 1.0, 0.0).astype(BF))
        left = jnp.concatenate([jnp.concatenate(voxels, axis=1), pool_x8], axis=0)
        out = dot(left, jnp.concatenate(member, axis=1), NT)
        sums = sums + out[:32]
        for x4 in range(4):
            part = out[32 + 8 * x4 : 40 + 8 * x4]
            cells[x4, 8 * yc : 8 * yc + 8, :] = part
            count = count + part
    for x4 in range(4):
        cnt_ref[x4 // 2, 128 * (x4 % 2) : 128 * (x4 % 2) + 128, :] = cells[x4].T.astype(BF)
    for x2 in range(2):
        side_ref[pl.ds(16 * x2, 16), :] = cells[x2, pl.ds(0, 16, stride=8), :].astype(BF)
    if half == 0:
        after_ref[256:288] = sums
        after_ref[288:296] = count
    else:
        sums = sums + given_ref[256:288]
        number = jnp.sum(count + given_ref[288:296], axis=0, keepdims=True)
        stacked = jnp.concatenate([jnp.zeros((64, 128), F32), sums, jnp.broadcast_to(number, (32, 128))], axis=0)
        side_ref[pl.ds(32, 16), :] = edge.T[:16].astype(BF)
        lane = iota((128, 128), 1)
        rows = stacked.T
        high = jnp.floor(rows * (1.0 / 256.0)) * 256.0
        rows = jnp.where(lane == 96, high, jnp.where(lane == 98, rows - high, rows))
        after_ref[...] = jnp.where(lane == 97, edge, rows)


def faces(half, emb, slot, given):
    return pl.pallas_call(
        functools.partial(face_kernel, half),
        in_specs=[pl.BlockSpec(memory_space=pltpu.VMEM)] * 3,
        out_specs=[pl.BlockSpec(memory_space=pltpu.VMEM)] * 3,
        out_shape=[
            pltpu.VMEM((2, 256, 128), BF),
            pltpu.VMEM((128 if half else 296, 128), F32),
            pltpu.VMEM((48 if half else 32, 128), BF),
        ],
        scratch_shapes=[pltpu.VMEM((4096, 128), F32), pltpu.VMEM((4, 128, 128), F32)],
        compiler_params=pltpu.CompilerParams(vmem_limit_bytes=16 << 20),
        cost_estimate=pl.CostEstimate(flops=1_000_000, bytes_accessed=10_000, transcendentals=0),
        name="faces",
    )(keep(emb), slot, keep(given) if half else given)


ROWS1 = 6 * 20 * 8
ROWS2 = 4 * 18 * 8
HEAD = 8


def ordered(even, a, b):
    return jnp.where(even, b, a), jnp.where(even, a, b)


def taps_dot(lefts, weights, depth):
    total = None
    per = 256 // depth
    for t in range(0, 9, per):
        group = lefts[t : t + per]
        left = group[0] if len(group) == 1 else jnp.concatenate(group, axis=1)
        term = dot(left, weights[pl.ds(depth * t, depth * len(group)), :])
        total = term if total is None else total + term
    return total


def window(source, tap, z, plane, rows):
    return source[tap % 3 & 1, pl.ds((z + tap // 3) * plane + 16 * (tap % 3 >> 1), rows), :]


def inner_kernel(own_ref, za_ref, zb_ref, ya_ref, yb_ref, w1a_ref, w1b_ref, b1_ref, w2_ref, b2_ref, cnt0_ref,
                 cnt1_ref, fine_ref, sums_ref, ends_ref, near_ref, rim_ref, field, this, mixed, h0f, h1f, h0b, h0n, h1b):
    gz, gy = lax.axis_index("gz"), lax.axis_index("gy")
    z_even, y_even = (gz & 1) == 0, (gy & 1) == 0
    z_low, z_high = ordered(z_even, za_ref[...].astype(F32), zb_ref[...].astype(F32))
    zs = (z_low, own_ref[...].astype(F32), z_high)
    ya, yb = ya_ref[...].astype(F32), yb_ref[...].astype(F32)
    ys = []
    for whole in ordered(y_even, ya, yb):
        low, high = ordered(z_even, whole[0:32], whole[64:96])
        ys.append((low, whole[32:64], high))
    for plane in range(6):
        part, i = plane // 2, plane % 2
        base = HEAD + plane * 160
        field[pl.ds(base, 16), :] = ys[0][part][16 * i : 16 * i + 16]
        field[pl.ds(base + 16, 128), :] = zs[part][128 * i : 128 * i + 128]
        field[pl.ds(base + 144, 16), :] = ys[1][part][16 * i : 16 * i + 16]
        for k, g in enumerate((0, 7)):
            ends_ref[k, pl.ds(24 * plane, 20), :] = field[pl.ds(base + g, 20, stride=8), :]

    lane = iota((160, 128), 1)
    for z in range(6):
        for shift in range(2):
            now = field[pl.ds(HEAD + 160 * z + 8 * shift, 160), :]
            before = field[pl.ds(HEAD + 160 * z + 8 * shift - 1, 160), :]
            this[shift, pl.ds(160 * z, 160), :] = now.astype(BF)
            mixed[shift, pl.ds(160 * z, 160), :] = jnp.where(lane < 64, now, before).astype(BF)

    row = iota((144, 128), 0)
    stay = jnp.where((row < 8) & (gy == 0), 0.0, 1.0)
    stay = jnp.where((row >= 136) & (gy == 3), 0.0, stay)
    b1, b2 = b1_ref[...], b2_ref[...]

    def conv1(source, weights, z):
        lefts = [window(source, tap, z, 160, 144) for tap in range(9)]
        return jnp.maximum(taps_dot(lefts, weights, 128) + b1, 0.0)

    for z in range(4):
        inside = 1.0
        if z == 0:
            inside = jnp.where(gz == 0, 0.0, 1.0)
        if z == 3:
            inside = jnp.where(gz == 7, 0.0, 1.0)
        h0f[pl.ds(144 * z, 144), :] = conv1(mixed, w1b_ref, z) * (stay * inside)
        h1f[pl.ds(144 * z, 144), :] = conv1(this, w1a_ref, z) * (stay * inside)
    for z in range(4):
        for k, g in enumerate((0, 7)):
            near_ref[k, pl.ds(24 * z, 18), :] = h1f[pl.ds(144 * z + g, 18, stride=8), :]
        for shift in range(2):
            at = 144 * z + 8 * shift
            h0b[shift, pl.ds(144 * z, 144), :] = h0f[pl.ds(at, 144), :].astype(BF)
            h0n[shift, pl.ds(144 * z, 144), :] = h0f[pl.ds(at + 1, 144), :].astype(BF)
            h1b[shift, pl.ds(144 * z, 144), :] = h1f[pl.ds(at, 144), :].astype(BF)

    group = iota((128, 128), 0) & 7
    sums = None
    for z in range(2):
        lefts = []
        for tap in range(9):
            h = [window(source, tap, z, 144, 128) for source in (h0b, h1b, h0n)]
            lefts.append(jnp.concatenate([jnp.concatenate(h[p : p + 2], axis=1) for p in range(2)], axis=0))
        both = taps_dot(lefts, w2_ref, 256) + b2
        for p in range(2):
            ctx = jnp.where(group == 7 * p, 0.0, both[128 * p : 128 * p + 128]).astype(BF)
            wide = ctx.astype(F32)
            fine_ref[pl.ds(512 * z + 2 * p, 128, stride=4), :] = wide
            fine_ref[pl.ds(512 * z + 2 * p + 1, 128, stride=4), :] = pltpu.roll(wide, 64, 1)
            term = dot((cnt0_ref, cnt1_ref)[z][p], ctx)
            sums = term if sums is None else sums + term
    sums_ref[...] = sums
    row, col = iota((512, 128), 0), iota((512, 128), 1)
    cell = ((row >> 7) << 4) + ((row & 127) >> 3)
    pick = jnp.where((cell == col) & ((row & 7) == 7 * (row >> 8)), 1.0, 0.0).astype(BF)
    left = jnp.concatenate([cnt0_ref[0], cnt1_ref[0], cnt0_ref[1], cnt1_ref[1]], axis=1)
    rim_ref[...] = dot(left, pick).astype(BF)


def inner(*arrays):
    return pl.pallas_call(
        inner_kernel,
        in_specs=[pl.BlockSpec(memory_space=pltpu.VMEM)] * len(arrays),
        out_specs=[pl.BlockSpec(memory_space=pltpu.VMEM)] * 5,
        out_shape=[
            pltpu.VMEM((1024, 128), F32),
            pltpu.VMEM((256, 128), F32),
            pltpu.VMEM((2, 144, 128), F32),
            pltpu.VMEM((2, 96, 128), F32),
            pltpu.VMEM((256, 128), BF),
        ],
        scratch_shapes=[
            pltpu.VMEM((HEAD + ROWS1 + 8, 128), F32),
            pltpu.VMEM((2, ROWS1, 128), BF),
            pltpu.VMEM((2, ROWS1, 128), BF),
            pltpu.VMEM((ROWS2 + 16, 128), F32),
            pltpu.VMEM((ROWS2 + 16, 128), F32),
            pltpu.VMEM((2, ROWS2, 128), BF),
            pltpu.VMEM((2, ROWS2, 128), BF),
            pltpu.VMEM((2, ROWS2, 128), BF),
        ],
        compiler_params=pltpu.CompilerParams(vmem_limit_bytes=16 << 20),
        cost_estimate=pl.CostEstimate(flops=1_000_000, bytes_accessed=10_000, transcendentals=0),
        name="inner",
    )(*arrays)


def outer_kernel(xb_ref, xa_ref, ends_ref, near_ref, sums_ref, w1a_ref, w1b_ref, b1_ref, w2_ref, b2_ref, rim_ref,
                 face_ref, edge_ref, send_ref, column, hidden):
    gz, gy, gx = (lax.axis_index(a) for a in ("gz", "gy", "gx"))
    z_even, y_even, x_even = (gz & 1) == 0, (gy & 1) == 0, (gx & 1) == 0
    lane = iota((24, 128), 1)
    column[...] = jnp.zeros_like(column)
    got = xb_ref[...].astype(F32)
    for k, whole in enumerate(ordered(x_even, xa_ref[80:208].astype(F32), got[80:208])):
        planes = [whole[20 * i : 20 * i + 20] for i in range(6)]
        low0, high0 = ordered(z_even, planes[0], planes[4])
        low1, high1 = ordered(z_even, planes[1], planes[5])
        for plane, rows in enumerate((low0, low1, planes[2], planes[3], high0, high1)):
            first, last = ordered(y_even, rows[16:18], rows[18:20])
            halo = jnp.concatenate([first, rows[0:16], last, jnp.zeros((4, 128), F32)], axis=0)
            own = ends_ref[k, pl.ds(24 * plane, 24), :]
            left, right = (own, halo) if k == 0 else (halo, own)
            column[k, pl.ds(24 * plane, 24), :] = jnp.where(lane < 64, left, right)
            if k == 1:
                column[2, pl.ds(24 * plane, 24), :] = halo

    row, lane = iota((96, 128), 0), iota((96, 128), 1)
    z_of = jnp.where(row < 24, 0, jnp.where(row < 48, 1, jnp.where(row < 72, 2, 3)))
    y_of = row - 24 * z_of
    gone = ((z_of == 0) & (gz == 0)) | ((z_of == 3) & (gz == 7)) | ((y_of == 0) & (gy == 0)) | ((y_of == 17) & (gy == 3))
    out0 = gone | ((lane < 64) & (gx == 0))
    out1 = gone | ((lane >= 64) & (gx == 7))
    at = [24 * (tap // 3) + tap % 3 for tap in range(9)]
    lefts = [jnp.concatenate([column[k, pl.ds(r, 96), :] for k in range(2)], axis=0).astype(BF) for r in at]
    total = jnp.maximum(taps_dot(lefts, w1b_ref, 128) + b1_ref[...], 0.0)
    lefts = [column[2, pl.ds(r, 96), :].astype(BF) for r in at]
    beyond = jnp.maximum(taps_dot(lefts, w1a_ref, 128) + b1_ref[...], 0.0)
    hidden[0, 0:96] = jnp.where(out0, 0.0, total[0:96])
    hidden[1, 0:96] = near_ref[0]
    hidden[2, 0:96] = near_ref[1]
    hidden[3, 0:96] = jnp.where(out1, 0.0, total[96:192])
    hidden[4, 0:96] = jnp.where(gone, 0.0, beyond)

    lefts = []
    for r in at:
        h = [hidden[k, pl.ds(r, 40), :].astype(BF) for k in range(5)]
        lefts.append(jnp.concatenate([jnp.concatenate([h[k], h[k + 1]], axis=1) for k in (0, 2, 3)], axis=0))
    ctx = (taps_dot(lefts, w2_ref, 256) + b2_ref[...]).astype(BF).astype(F32)
    rows = []
    for k in range(2):
        for z in range(2):
            wide = ctx[40 * k + 24 * z : 40 * k + 24 * z + 16]
            edge_ref[pl.ds(32 * k + 16 * z, 16), :] = wide
            rows.append(jnp.where(gx == 4, 0.0, wide) if k == 0 else wide)
    sums = sums_ref[...] + dot(rim_ref[:, :64], jnp.concatenate(rows, axis=0).astype(BF))
    both = sums[:128] + pltpu.roll(sums[128:], 64, 1)
    lane = iota((128, 128), 1)
    mine = jnp.where(lane < 64, both, face_ref[...]).astype(BF)

    next_ctx = [ctx[80 + 24 * z : 96 + 24 * z] for z in range(2)]
    right = jnp.concatenate([v for c in next_ctx for v in (c, pltpu.roll(c, 64, 1))], axis=0).astype(BF)
    other = dot(got[0:64].T.astype(BF), right)
    edge = jnp.broadcast_to(got[64:65], (128, 128)).T
    other = jnp.where(lane < 64, other, jnp.where(lane == 97, edge, 0.0))
    other = jnp.where(gx == 3, other, 0.0).astype(BF)
    next_ctx = jnp.concatenate(next_ctx, axis=0).astype(BF)
    for d in range(8):
        send_ref[pl.ds(64 * d, 16), :] = mine[16 * d : 16 * d + 16]
        send_ref[pl.ds(64 * d + 16, 16), :] = other[16 * d : 16 * d + 16]
        send_ref[pl.ds(64 * d + 32, 32), :] = next_ctx


def outer(*arrays):
    return pl.pallas_call(
        outer_kernel,
        in_specs=[pl.BlockSpec(memory_space=pltpu.VMEM)] * len(arrays),
        out_specs=[pl.BlockSpec(memory_space=pltpu.VMEM)] * 2,
        out_shape=[pltpu.VMEM((64, 128), F32), pltpu.VMEM((512, 128), BF)],
        scratch_shapes=[pltpu.VMEM((3, 152, 128), F32), pltpu.VMEM((5, 96, 128), F32)],
        compiler_params=pltpu.CompilerParams(vmem_limit_bytes=16 << 20),
        cost_estimate=pl.CostEstimate(flops=200_000_000, bytes_accessed=3_000_000, transcendentals=0),
        name="outer",
    )(*arrays)


def edge_kernel(rows_ref, fine_ref, rim_ref, edge_emb_ref, edge_ctx_ref, out_ref, patch, final, sent):
    patch[...] = fine_ref[...]
    given = lax.axis_index("gx") == 4
    for k, x in enumerate((0, 30)):
        for z in range(2):
            wide = rim_ref[pl.ds(32 * k + 16 * z, 16), :]
            if k == 0:
                wide = jnp.where(given, rows_ref[pl.ds(64 * 3 + 32 + 16 * z, 16), :].astype(F32), wide)
            patch[pl.ds(512 * z + x, 16, stride=32), :] = wide
            patch[pl.ds(512 * z + x + 1, 16, stride=32), :] = pltpu.roll(wide, 64, 1)
    final[...] = patch[...][:, :64].astype(BF)
    copy = pltpu.make_async_copy(final, out_ref, sent)
    copy.start()
    rows = [rows_ref[pl.ds(64 * d + 16 * i, 16), :] for i in range(2) for d in range(8)]
    rows = jnp.concatenate(rows, axis=0).astype(F32)
    hits = jnp.where(rows[:, 97:98] == iota((256, 64), 1).astype(F32), 1.0, 0.0).astype(BF)
    sums = dot(rows.T.astype(BF), hits)
    scale = jnp.maximum(sums[96:97] + sums[98:99], 1.0)
    edge_ctx_ref[...] = sums[:64] / scale
    edge_emb_ref[...] = sums[64:96] / scale
    copy.wait()


def edges(rows, fine, rim):
    return pl.pallas_call(
        edge_kernel,
        in_specs=[pl.BlockSpec(memory_space=pltpu.VMEM)] * 3,
        out_specs=[pl.BlockSpec(memory_space=pltpu.VMEM)] * 2 + [pl.BlockSpec(memory_space=pl.ANY)],
        out_shape=[
            jax.ShapeDtypeStruct((32, 64), F32),
            jax.ShapeDtypeStruct((64, 64), F32),
            jax.ShapeDtypeStruct((1024, 64), BF),
        ],
        scratch_shapes=[pltpu.VMEM((1024, 128), F32), pltpu.VMEM((1024, 64), BF), pltpu.SemaphoreType.DMA],
        name="edges",
    )(keep(rows), keep(fine), keep(rim))


def pairs(first, count):
    return [pair for i in range(first, count - 1, 2) for pair in ((i, i + 1), (i + 1, i))]


def per_device(embedding, face_slot, face_edge, conv1_w, conv1_b, conv2_w, conv2_b):
    emb = embedding.reshape(32, 256, 128)
    gy, gx = lax.axis_index("gy"), lax.axis_index("gx")
    slot = face_slot.reshape(256, 128)
    own, voxels = pool(emb)
    zb = lax.ppermute(own, "gz", pairs(1, 8))
    za = lax.ppermute(own, "gz", pairs(0, 8))
    cnt0, half, side0 = faces(0, voxels, slot, face_edge.reshape(1, 128))
    w1, w2 = jnp.swapaxes(conv1_w, 3, 4).reshape(27, 32, 64), conv2_w.reshape(27, 64, 64)
    zb, za, half, w1 = lax.optimization_barrier((zb, za, half, w1))
    planes = [a.reshape(2, 16, 8, 128) for a in (za, own, zb)]
    y_even, x_even = (gy & 1) == 0, (gx & 1) == 0

    def y_edge(high):
        first = jnp.where(high, 14, 0)
        return jnp.concatenate([lax.dynamic_slice_in_dim(a, first, 2, axis=1) for a in planes], axis=0)

    to_a, to_b = lax.optimization_barrier((y_edge(y_even), y_edge(jnp.logical_not(y_even))))
    ya = lax.ppermute(to_a, "gy", pairs(0, 4))
    yb = lax.ppermute(to_b, "gy", pairs(1, 4))
    cnt1, face, side1 = faces(1, voxels, slot, half)
    w1a, w1b, w2a = bands(w1, w2)
    ya, yb, face, w1a = lax.optimization_barrier((ya, yb, face, w1a))

    def x_edge(g):
        mid = jnp.concatenate([a[:, :, g] for a in planes], axis=0)
        return jnp.concatenate([mid, ya[:, :, g], yb[:, :, g]], axis=1).reshape(120, 128)

    low, high = x_edge(0), x_edge(7)
    rest = jnp.zeros((8, 128), BF)
    to_b = jnp.concatenate([side0, side1, jnp.where(x_even, low, high), rest], axis=0)
    to_a = jnp.concatenate([side0, side1, jnp.where(x_even, high, low), rest], axis=0)
    to_b, to_a = lax.optimization_barrier((to_b, to_a))
    xa = lax.ppermute(to_a, "gx", pairs(0, 8))
    xb = lax.ppermute(to_b, "gx", [(1, 2), (2, 1), (5, 6), (6, 5), (4, 3)])
    twice = lambda b: jnp.concatenate([b, b]).reshape(1, 128)
    b1, b2 = twice(conv1_b), twice(conv2_b)
    w1a, w1b, w2a, cnt0, cnt1 = (keep(a) for a in (w1a, w1b, w2a, cnt0, cnt1))
    fine, sums, ends, near, rim = inner(
        own, za, zb, ya.reshape(96, 128), yb.reshape(96, 128), w1a, w1b, b1, w2a, b2, cnt0, cnt1
    )
    rim_ctx, send = outer(
        xb, xa, keep(ends), keep(near), keep(sums), w1a, w1b, b1, w2a, b2, keep(rim), keep(face)
    )
    rows = lax.all_to_all(send, "gx", 0, 0, tiled=True)
    edge_emb, edge_ctx, context = edges(rows, fine, rim_ctx)
    context = jnp.transpose(context.reshape(2, 16, 32, 64), (3, 0, 1, 2))
    return (context, edge_emb, edge_ctx)


def solution(mesh):
    in_specs = (P(None, "gz", "gy", "gx"), P("gz", "gy", "gx"), P(("gz", "gy", "gx")), P(), P(), P(), P())
    out_specs = (P(None, "gz", "gy", "gx"), P(None, ("gz", "gy", "gx")), P(None, ("gz", "gy", "gx")))
    return jax.shard_map(per_device, mesh=mesh, in_specs=in_specs, out_specs=out_specs, check_vma=False)
```
